32 devices in a mesh: dp: 8 (over z, core), fsdp: 4 (over y, x).
Axes of the slice: x: 2, y: 2, z: 4, core: 2. Of those that a mesh axis runs over, the one named last changes fastest.
Arguments:
- patches: bfloat16 [8192, 384], P(('dp', 'fsdp')), may hold values from -6 to 6
- grad_embed: bfloat16 [8192, 3072], P(('dp', 'fsdp')), may hold values from -6 to 6
- weight: bfloat16 [384, 3072], P(None, 'fsdp'), may hold values from -0.3125 to 0.3125
- straggler: int32 [8], P('dp'), may hold values 0 or 1
- decode: int32 [8], P('dp'), may hold values from 1 to 3
- encode: int32 [8, 2], P('dp'), may hold values from 1 to 3
Outputs:
- embedded: bfloat16 [8192, 3072], P(('dp', 'fsdp'))
- weight_grad: float32 [384, 3072], P('dp', 'fsdp')
The draws below stay inside these ranges and needn't reach their ends.
All inputs are finite; a program needn't handle non-finite values. No bound on the sum of `straggler` on one device may be relied on, other than what follows from the above.
Results may differ from the reference program's by a relative error of at most 0.001.
Values may be sent and summed in bfloat16 or wider, within the bound.
No kernel may reach another device: no remote copies, remote signals or barrier semaphores. Data moves between devices by JAX's collectives and lax.ppermute only.
A program may use at most 64 MiB of HBM per device.

```python
import jax
import jax.numpy as jnp
from jax import lax

P_SIZE = 384
DW = 3072
REP_TOK = 1024
TOKENS = 8192
N_DP = 8


def place_ends(entries, key, least, top_value):
    longest = entries.shape.index(max(entries.shape))
    spots = []
    for shift in (0, 1):
        where = [jax.random.randint(jax.random.fold_in(key, axis), (), 0, length) for axis, length in enumerate(entries.shape)]
        where[longest] = (where[longest] + shift) % entries.shape[longest]
        spots.append(tuple(where))
    return entries.at[spots[0]].set(least).at[spots[1]].set(top_value)


def raised(array, key, source, target, shards_of, factor):
    def block_of(dim):
        return (jnp.arange(array.shape[dim]) // (array.shape[dim] // shards_of)).reshape((-1,) + (1,) * (array.ndim - 1 - dim))

    one_side = jax.random.permutation(key, shards_of)[block_of(target)]
    other_side = (block_of(target) + shards_of // 2) % shards_of
    return jnp.where((block_of(source) == one_side) | (block_of(source) == other_side), factor * array, array)


def block_scale(stream_key, dims, shards, smallest, top_value):
    loudness, own = 1.0, jax.random.fold_in(stream_key, 6)
    for axis_at, shards_of in shards:
        steps = jnp.exp(jax.random.uniform(jax.random.fold_in(own, axis_at), (shards_of,), jnp.float32, smallest / len(shards), top_value / len(shards)))
        loudness = loudness * jnp.repeat(steps, dims[axis_at] // shards_of).reshape([-1 if axis == axis_at else 1 for axis in range(len(dims))])
    return loudness


def scatter_about(key, extent, spread, bound, shards=(), dtype=jnp.bfloat16):
    level = block_scale(key, extent, shards, -0.22, 0.18) if shards else 1.0
    entries = jax.random.normal(key, extent, jnp.float32) * spread * level
    return jnp.minimum(jnp.maximum(entries, -bound), bound).astype(dtype)


def heavy_noise(key, dims, spread, limit, pieces, heavy, held_as=jnp.bfloat16):
    array = spread * jax.random.normal(key, dims, jnp.float32)
    if pieces:
        array = array * block_scale(key, dims, pieces, -0.22, 0.18)
    return jnp.clip(raised(array, jax.random.fold_in(key, 3), *heavy), -limit, limit).astype(held_as)


def setup_inputs(seed: int = 0) -> dict:
    key_of = jax.random.split(jax.random.key(seed), 7)
    patches = heavy_noise(key_of[0], (TOKENS, P_SIZE), 1.0, 6.0, ((0, 32),), (0, 1, 32, 2.75))
    grad_embed = scatter_about(key_of[1], (TOKENS, DW), 1.0, 6.0, ((0, 32),))
    weight = scatter_about(key_of[2], (P_SIZE, DW), P_SIZE ** -0.5, 0.3125, ((1, 4),))
    straggler = place_ends((jax.random.randint(key_of[3], (N_DP,), 0, 8) < 7).astype(jnp.int32), jax.random.fold_in(key_of[3], 1), 0, 1)
    decode = place_ends(jax.random.randint(key_of[4], (N_DP,), 1, 4), jax.random.fold_in(key_of[4], 1), 1, 3).astype(jnp.int32)
    encode = place_ends(jax.random.randint(key_of[5], (N_DP, 2), 1, 4), jax.random.fold_in(key_of[5], 1), 1, 3).astype(jnp.int32)
    return dict(patches=patches, grad_embed=grad_embed, weight=weight, straggler=straggler, decode=decode, encode=encode)


def reference(patches, grad_embed, weight, straggler, decode, encode):
    embedded = jnp.dot(patches, weight, preferred_element_type=jnp.float32).astype(jnp.bfloat16)
    served = straggler * decode
    factor = served * encode[:, 0] + jnp.roll(served * encode[:, 1], 1)
    scales = factor.astype(jnp.float32) / REP_TOK
    inputs = patches.reshape(N_DP, REP_TOK, P_SIZE)
    cotans = grad_embed.reshape(N_DP, REP_TOK, DW)

    def accumulate(total, items):
        inner, outer, scale = items
        term = lax.dot_general(inner, outer, (((0,), (0,)), ((), ())), preferred_element_type=jnp.float32)
        return total + scale * term, None

    start = jnp.zeros((P_SIZE, DW), jnp.float32)
    weight_grad, unused = lax.scan(accumulate, start, (inputs, cotans, scales))
    return embedded, weight_grad
```

```python
import functools
import math

import jax
import jax.numpy as jnp
from jax import lax
from jax.experimental import pallas as pl
from jax.experimental.pallas import tpu as pltpu
from jax.sharding import PartitionSpec as P

LANES = 128
TAIL = 16
STEP = math.log(2) / 16
TOP = 32760.0
F32, BF16, I16, I32 = jnp.float32, jnp.bfloat16, jnp.int16, jnp.int32
VMEM = pl.BlockSpec(memory_space=pltpu.VMEM)
SMEM = pl.BlockSpec(memory_space=pltpu.SMEM)


def exchange(block, axis, step):
    return lax.ppermute(block, axis, [(i, i ^ step) for i in range(lax.axis_size(axis))])


def shifted(block, axis, distance):
    count = lax.axis_size(axis)
    return lax.ppermute(block, axis, [((i - distance) % count, i) for i in range(count)])


def times(a, b, dims=((1,), (0,))):
    return lax.dot_general(a, b, (dims, ((), ())), preferred_element_type=F32)


def chunk_shape(rows, columns):
    return (columns // LANES * rows + TAIL, LANES)


def put_chunk(ref, value):
    rows, columns = value.shape
    largest = jnp.max(jnp.abs(value), axis=0, keepdims=True)
    power = jnp.ceil(jnp.log(jnp.maximum(largest, 2.0**-100)) * (1 / STEP))
    coded = jnp.round(value * (TOP * jnp.exp(power * -STEP))).astype(I32)
    power = power.astype(I32)
    tail = jnp.zeros((TAIL, LANES), I32)
    row = lax.broadcasted_iota(I32, (TAIL, LANES), 0)
    for j in range(columns // LANES):
        part = slice(j * LANES, (j + 1) * LANES)
        ref[pl.ds(j * rows, rows), :] = coded[:, part].astype(I16)
        tail = jnp.where(row == j, power[:, part], tail)
    ref[pl.ds(columns // LANES * rows, TAIL), :] = tail.astype(I16)


def chunk_sum(refs, rows, blocks):
    total = [0.0] * blocks
    for ref in refs:
        tail = jnp.exp(ref[pl.ds(blocks * rows, TAIL), :].astype(F32) * STEP) * (1 / TOP)
        for j in range(blocks):
            total[j] += ref[pl.ds(j * rows, rows), :].astype(F32) * tail[j : j + 1, :]
    return total


def partial_kernel(depth, place, scale, p_own, p_sib, g_own, g_sib, *outs):
    me, core = place[0], place[2]
    features = p_own.shape[1]
    rows = features // 2
    columns = g_own.shape[1] // len(outs)
    i = lax.broadcasted_iota(I32, (rows, features), 0)
    j = lax.broadcasted_iota(I32, (rows, features), 1)
    chosen = jnp.where(j == (i // depth * 2 + core) * depth + i % depth, 1.0, 0.0).astype(BF16)
    left = [times(chosen, p[...], ((1,), (1,))).astype(BF16) for p in (p_own, p_sib)]
    for k, out in enumerate(outs):
        here = pl.ds(pl.multiple_of((me ^ k) * columns, columns), columns)
        put_chunk(out, scale[0] * times(left[0], g_own[:, here]) + scale[1] * times(left[1], g_sib[:, here]))


def middle_kernel(depth, rows, place, *refs):
    *refs, held = refs
    blocks = held.shape[0]
    chunks = (refs[0].shape[0] - TAIL) // rows
    assert chunks == blocks
    peers = rows // depth
    ins, outs = refs[:-peers], refs[-peers:]
    for j, part in enumerate(chunk_sum(ins, rows, blocks)):
        held[j] = part
    for k, out in enumerate(outs):
        here = pl.ds(pl.multiple_of((place[1] ^ k) * depth, depth), depth)
        put_chunk(out, jnp.concatenate([held[j, here, :] for j in range(blocks)], axis=1))


def last_kernel(*refs):
    *ins, out = refs
    rows, columns = out.shape
    for j, part in enumerate(chunk_sum(ins, rows, columns // LANES)):
        out[:, j * LANES : (j + 1) * LANES] = part


def embed_kernel(place, patches, own, *refs):
    *others, out, halves = refs
    mine, theirs = others[: len(others) // 2], others[len(others) // 2 :]
    me, core = place[0], place[2]
    rows, columns = own.shape
    halves[0] = patches[:, : rows // 2]
    halves[1] = patches[:, rows // 2 :]

    def put(k, value):
        out[:, pl.ds(pl.multiple_of((me ^ k) * columns, columns), columns)] = value.astype(BF16)

    put(0, times(patches[...], own[...]))
    for k, (a, b) in enumerate(zip(mine, theirs), 1):
        put(k, times(halves[core], a[...]) + times(halves[1 - core], b[...]))


def call(kernel, outs, operands, scalars, scratch=(), flops=0):
    moved = sum(math.prod(a.shape) * a.dtype.itemsize for a in [*operands, *jax.tree.leaves(outs)])
    return pl.pallas_call(
        kernel,
        out_shape=outs,
        in_specs=[SMEM] * scalars + [VMEM] * (len(operands) - scalars),
        out_specs=jax.tree.map(lambda _: VMEM, outs),
        scratch_shapes=scratch,
        compiler_params=pltpu.CompilerParams(vmem_limit_bytes=40 * 2**20),
        cost_estimate=pl.CostEstimate(flops=flops, bytes_accessed=moved, transcendentals=0),
    )(*operands)


def tiled_body(patches, grad_embed, weight, straggler, decode, encode):
    count_dp, count_fsdp = lax.axis_size("dp"), lax.axis_size("fsdp")
    dp, me = lax.axis_index("dp"), lax.axis_index("fsdp")
    core = dp % 2
    place = jnp.stack([me, dp // 2, core])
    tokens, features = patches.shape
    columns = weight.shape[1]
    rows, depth, blocks = features // 2, features // count_dp, columns // LANES

    with jax.named_scope("swap_inputs"):
        g_sib = exchange(grad_embed, "dp", 1)
        p_sib = exchange(patches, "dp", 1)
        shares = (straggler * decode)[:, None] * encode
        s_sib = exchange(shares, "dp", 1)
        before = shifted(shares[:, 1], "dp", 1)
        before_sib = jnp.where(core == 0, shares[:, 1], shifted(shares[:, 1], "dp", 2))
    factors = jnp.concatenate([shares[:, 0] + before, s_sib[:, 0] + before_sib])
    scale = factors.astype(F32) / (tokens * count_fsdp)

    with jax.named_scope("gather_weight"):
        half = lax.dynamic_slice_in_dim(weight, core * rows, rows, 0)
        mine = [exchange(half, "fsdp", k) for k in range(1, count_fsdp)]
        theirs = [exchange(w, "dp", 1) for w in mine]

    with jax.named_scope("partial"):
        chunk = jax.ShapeDtypeStruct(chunk_shape(rows, columns), I16)
        parts = call(
            functools.partial(partial_kernel, depth),
            [chunk] * count_fsdp,
            [place, scale, patches, p_sib, grad_embed, g_sib],
            2,
            flops=4 * tokens * rows * columns * count_fsdp,
        )
        parts = [exchange(part, "fsdp", k) if k else part for k, part in enumerate(parts)]
    with jax.named_scope("middle"):
        chunk = jax.ShapeDtypeStruct(chunk_shape(depth, columns), I16)
        parts = call(
            functools.partial(middle_kernel, depth, rows),
            [chunk] * (count_dp // 2),
            [place, *parts],
            1,
            [pltpu.VMEM((blocks, rows, LANES), F32)],
        )
        parts = [exchange(part, "dp", 2 * k) if k else part for k, part in enumerate(parts)]
    with jax.named_scope("embed"):
        embedded = call(
            embed_kernel,
            jax.ShapeDtypeStruct((tokens, columns * count_fsdp), BF16),
            [place, patches, weight, *mine, *theirs],
            1,
            [pltpu.VMEM((2, tokens, rows), BF16)],
            flops=2 * tokens * features * columns * count_fsdp,
        )
    with jax.named_scope("last"):
        decoded = call(last_kernel, jax.ShapeDtypeStruct((depth, columns), F32), parts, 0)
    return embedded, decoded


def plain_body(patches, grad_embed, weight, straggler, decode, encode):
    shares = (straggler * decode)[:, None] * encode
    factor = (shares[:, 0] + shifted(shares[:, 1], "dp", 1))[0]
    scale = factor.astype(F32) / (patches.shape[0] * lax.axis_size("fsdp"))
    whole = lax.all_gather(weight, "fsdp", axis=1, tiled=True)
    embedded = times(patches, whole).astype(BF16)
    term = scale * times(grad_embed, patches, ((0,), (0,)))
    term = lax.psum_scatter(term, "fsdp", scatter_dimension=0, tiled=True)
    return embedded, lax.psum_scatter(term.T, "dp", scatter_dimension=0, tiled=True)


def body(patches, grad_embed, weight, straggler, decode, encode):
    fits = patches.shape[1] % (16 * lax.axis_size("dp")) == 0 and weight.shape[1] % LANES == 0
    run = tiled_body if fits else plain_body
    return run(patches, grad_embed, weight, straggler, decode, encode)


def solution(mesh):
    return jax.shard_map(
        body,
        mesh=mesh,
        in_specs=(
            P(("dp", "fsdp"), None),
            P(("dp", "fsdp"), None),
            P(None, "fsdp"),
            P("dp"),
            P("dp"),
            P("dp", None),
        ),
        out_specs=(P(("dp", "fsdp"), None), P("dp", "fsdp")),
        check_vma=False,
    )
```

```python
import functools
import math

import jax
import jax.numpy as jnp
from jax import lax
from jax.experimental import pallas as pl
from jax.experimental.pallas import tpu as pltpu
from jax.sharding import PartitionSpec as P

LANES = 128
TAIL = 16
STEP = math.log(2) / 16
TOP = 32760.0
F32, BF16, I16, I32 = jnp.float32, jnp.bfloat16, jnp.int16, jnp.int32
VMEM = pl.BlockSpec(memory_space=pltpu.VMEM)
SMEM = pl.BlockSpec(memory_space=pltpu.SMEM)
HBM = pl.BlockSpec(memory_space=pltpu.HBM)


def in_hbm(array):
    return pltpu.with_memory_space_constraint(array, pltpu.HBM)


def exchange(block, axis, step):
    return lax.ppermute(block, axis, [(i, i ^ step) for i in range(lax.axis_size(axis))])


def shifted(block, axis, distance):
    count = lax.axis_size(axis)
    return lax.ppermute(block, axis, [((i - distance) % count, i) for i in range(count)])


def times(a, b, dims=((1,), (0,))):
    return lax.dot_general(a, b, (dims, ((), ())), preferred_element_type=F32)


def chunk_shape(rows, columns):
    return (columns // LANES * rows + TAIL, LANES)


def put_chunk(ref, value):
    rows, columns = value.shape
    largest = jnp.max(jnp.abs(value), axis=0, keepdims=True)
    power = jnp.ceil(jnp.log(jnp.maximum(largest, 2.0**-100)) * (1 / STEP))
    coded = jnp.round(value * (TOP * jnp.exp(power * -STEP))).astype(I32)
    power = power.astype(I32)
    tail = jnp.zeros((TAIL, LANES), I32)
    row = lax.broadcasted_iota(I32, (TAIL, LANES), 0)
    for j in range(columns // LANES):
        part = slice(j * LANES, (j + 1) * LANES)
        ref[pl.ds(j * rows, rows), :] = coded[:, part].astype(I16)
        tail = jnp.where(row == j, power[:, part], tail)
    ref[pl.ds(columns // LANES * rows, TAIL), :] = tail.astype(I16)


def chunk_sum(refs, rows, blocks):
    total = [0.0] * blocks
    for ref in refs:
        tail = jnp.exp(ref[pl.ds(blocks * rows, TAIL), :].astype(F32) * STEP) * (1 / TOP)
        for j in range(blocks):
            total[j] += ref[pl.ds(j * rows, rows), :].astype(F32) * tail[j : j + 1, :]
    return total


def prepare_kernel(code, patches, sent, shares, arrived):
    tokens, features = patches.shape
    copy = pltpu.make_async_copy(patches, sent.at[pl.ds(0, tokens)], arrived)
    copy.start()
    served = code[0] * code[1]
    row = lax.broadcasted_iota(I32, (TAIL, features), 0)
    tail = jnp.where(row == 0, served * code[2], served * code[3])
    sent[tokens:, :] = tail.astype(F32).astype(BF16)
    shares[...] = tail[:8, :LANES]
    copy.wait()


def features_of(patches, core, depth):
    features = patches.shape[1]
    i = lax.broadcasted_iota(I32, (features // 2, features), 0)
    j = lax.broadcasted_iota(I32, (features // 2, features), 1)
    chosen = jnp.where(j == (i // depth * 2 + core) * depth + i % depth, 1.0, 0.0).astype(BF16)
    return times(chosen, patches, ((1,), (1,))).astype(BF16)


def partial_kernel(depth, place, grad_embed, patches, g_sib, p_sib, shares, before, before_sib, *refs):
    *outs, held, arrived = refs
    me, core = place[0], place[2]
    tokens = grad_embed.shape[0]
    columns = grad_embed.shape[1] // len(outs)
    here = [pl.ds(pl.multiple_of((me ^ k) * columns, columns), columns) for k in range(len(outs))]
    copies = [
        pltpu.make_async_copy(grad_embed.at[:, at], held.at[k], arrived.at[k]) for k, at in enumerate(here)
    ]
    for copy in copies:
        copy.start()
    left = features_of(patches[:tokens, :], core, depth)
    left_sib = features_of(p_sib[:tokens, :], core, depth)
    first_sib = p_sib[tokens:, :LANES].astype(F32)[0:1, 0:1]
    first, second = shares[0:1, 0:1].astype(F32), shares[1:2, 0:1].astype(F32)
    second_before = jnp.where(core == 0, second, before_sib[1:2, 0:1].astype(F32))
    scale = (first + before[1:2, 0:1].astype(F32)) / (tokens * len(outs))
    scale_sib = (first_sib + second_before) / (tokens * len(outs))
    for k, out in enumerate(outs):
        value = scale_sib * times(left_sib, g_sib[:, here[k]])
        copies[k].wait()
        put_chunk(out, value + scale * times(left, held[k]))


def middle_kernel(depth, rows, place, *refs):
    *refs, held = refs
    blocks = held.shape[0]
    chunks = (refs[0].shape[0] - TAIL) // rows
    assert chunks == blocks
    peers = rows // depth
    ins, outs = refs[:-peers], refs[-peers:]
    for j, part in enumerate(chunk_sum(ins, rows, blocks)):
        held[j] = part
    for k, out in enumerate(outs):
        here = pl.ds(pl.multiple_of((place[1] ^ k) * depth, depth), depth)
        put_chunk(out, jnp.concatenate([held[j, here, :] for j in range(blocks)], axis=1))


def last_kernel(*refs):
    *ins, out = refs
    rows, columns = out.shape
    for j, part in enumerate(chunk_sum(ins, rows, columns // LANES)):
        out[:, j * LANES : (j + 1) * LANES] = part


def embed_kernel(place, own, patches, first, second, far, far_sib, out, held, arrived):
    me, core = place[0], place[2]
    columns = own.shape[1]
    tokens = out.shape[0]
    copy = pltpu.make_async_copy(own, held, arrived)
    copy.start()

    def put(k, weight):
        here = pl.ds(pl.multiple_of((me ^ k) * columns, columns), columns)
        out[:, here] = times(patches[:tokens, :], weight[...]).astype(BF16)

    put(1 + core, first)
    put(2 - core, second)

    @pl.when(core == 0)
    def _():
        put(3, far)

    @pl.when(core == 1)
    def _():
        put(3, far_sib)

    copy.wait()
    put(0, held)


def call(kernel, outs, operands, specs=(), scratch=(), flops=0):
    moved = sum(math.prod(a.shape) * a.dtype.itemsize for a in [*operands, *jax.tree.leaves(outs)])
    return pl.pallas_call(
        kernel,
        out_shape=outs,
        in_specs=[*specs] + [VMEM] * (len(operands) - len(specs)),
        out_specs=jax.tree.map(lambda _: VMEM, outs),
        scratch_shapes=scratch,
        compiler_params=pltpu.CompilerParams(vmem_limit_bytes=40 * 2**20),
        cost_estimate=pl.CostEstimate(flops=flops, bytes_accessed=moved, transcendentals=0),
    )(*operands)


def tiled_body(patches, grad_embed, weight, straggler, decode, encode):
    count_dp, count_fsdp = lax.axis_size("dp"), lax.axis_size("fsdp")
    dp, me = lax.axis_index("dp"), lax.axis_index("fsdp")
    core = dp % 2
    place = jnp.stack([me, dp // 2, core])
    tokens, features = patches.shape
    columns = weight.shape[1]
    rows, depth, blocks = features // 2, features // count_dp, columns // LANES

    with jax.named_scope("swap_inputs"):
        g_sib = exchange(grad_embed, "dp", 1)
        sent, shares = call(
            prepare_kernel,
            [jax.ShapeDtypeStruct((tokens + TAIL, features), BF16), jax.ShapeDtypeStruct((8, LANES), I32)],
            [jnp.concatenate([straggler, decode, encode[0]]), in_hbm(patches)],
            [SMEM, HBM],
            [pltpu.SemaphoreType.DMA],
        )
        p_sib = exchange(sent, "dp", 1)
        before, before_sib = shifted(shares, "dp", 1), shifted(shares, "dp", 2)

    with jax.named_scope("gather_weight"):
        both = ("dp", "fsdp")
        near = [(d * 4 + f, d * 4 + (f ^ (1 + d % 2))) for d in range(count_dp) for f in range(4)]
        cross = [(d * 4 + f, d * 4 + (f ^ 3)) for d in range(0, count_dp, 2) for f in range(4)]
        first = lax.ppermute(weight, both, near)
        far = lax.ppermute(lax.optimization_barrier((weight, before))[0], both, cross)

    with jax.named_scope("partial"):
        chunk = jax.ShapeDtypeStruct(chunk_shape(rows, columns), I16)
        parts = call(
            functools.partial(partial_kernel, depth),
            [chunk] * count_fsdp,
            [place, in_hbm(grad_embed), sent, g_sib, p_sib, shares, before, before_sib],
            [SMEM, HBM],
            [pltpu.VMEM((count_fsdp, tokens, columns), BF16), pltpu.SemaphoreType.DMA((count_fsdp,))],
            flops=4 * tokens * rows * columns * count_fsdp,
        )
        parts = [exchange(part, "fsdp", k) if k else part for k, part in enumerate(parts)]
    with jax.named_scope("share_weight"):
        first, far, parts[0] = lax.optimization_barrier((first, far, parts[0]))
        second = exchange(first, "dp", 1)
        far_sib = lax.ppermute(far, "dp", [(d, d + 1) for d in range(0, count_dp, 2)])
    with jax.named_scope("middle"):
        chunk = jax.ShapeDtypeStruct(chunk_shape(depth, columns), I16)
        parts = call(
            functools.partial(middle_kernel, depth, rows),
            [chunk] * (count_dp // 2),
            [place, *parts],
            [SMEM],
            [pltpu.VMEM((blocks, rows, LANES), F32)],
        )
        parts = [exchange(part, "dp", 2 * k) if k else part for k, part in enumerate(parts)]
    with jax.named_scope("embed"):
        embedded = call(
            embed_kernel,
            jax.ShapeDtypeStruct((tokens, columns * count_fsdp), BF16),
            [place, in_hbm(weight), sent, first, second, far, far_sib],
            [SMEM, HBM],
            [pltpu.VMEM(weight.shape, BF16), pltpu.SemaphoreType.DMA],
            flops=2 * tokens * features * columns * count_fsdp,
        )
    with jax.named_scope("last"):
        embedded, *parts = lax.optimization_barrier((embedded, *parts))
        decoded = call(last_kernel, jax.ShapeDtypeStruct((depth, columns), F32), parts)
    return embedded, decoded


def plain_body(patches, grad_embed, weight, straggler, decode, encode):
    shares = (straggler * decode)[:, None] * encode
    factor = (shares[:, 0] + shifted(shares[:, 1], "dp", 1))[0]
    scale = factor.astype(F32) / (patches.shape[0] * lax.axis_size("fsdp"))
    whole = lax.all_gather(weight, "fsdp", axis=1, tiled=True)
    embedded = times(patches, whole).astype(BF16)
    term = scale * times(grad_embed, patches, ((0,), (0,)))
    term = lax.psum_scatter(term, "fsdp", scatter_dimension=0, tiled=True)
    return embedded, lax.psum_scatter(term.T, "dp", scatter_dimension=0, tiled=True)


def body(patches, grad_embed, weight, straggler, decode, encode):
    fits = patches.shape[1] % (16 * lax.axis_size("dp")) == 0 and weight.shape[1] % LANES == 0
    fits = fits and lax.axis_size("fsdp") == 4
    run = tiled_body if fits else plain_body
    return run(patches, grad_embed, weight, straggler, decode, encode)


def solution(mesh):
    return jax.shard_map(
        body,
        mesh=mesh,
        in_specs=(
            P(("dp", "fsdp"), None),
            P(("dp", "fsdp"), None),
            P(None, "fsdp"),
            P("dp"),
            P("dp"),
            P("dp", None),
        ),
        out_specs=(P(("dp", "fsdp"), None), P("dp", "fsdp")),
        check_vma=False,
    )
```

```python
import functools
import math

import jax
import jax.numpy as jnp
from jax import lax
from jax.experimental import pallas as pl
from jax.experimental.pallas import tpu as pltpu
from jax.sharding import PartitionSpec as P

LANES = 128
TAIL = 16
STEP = math.log(2) / 16
TOP = 32760.0
F32, BF16, I16, I32 = jnp.float32, jnp.bfloat16, jnp.int16, jnp.int32
VMEM = pl.BlockSpec(memory_space=pltpu.VMEM)
SMEM = pl.BlockSpec(memory_space=pltpu.SMEM)
HBM = pl.BlockSpec(memory_space=pltpu.HBM)


def in_hbm(array):
    return pltpu.with_memory_space_constraint(array, pltpu.HBM)


def exchange(block, axis, step):
    return lax.ppermute(block, axis, [(i, i ^ step) for i in range(lax.axis_size(axis))])


def shifted(block, axis, distance):
    count = lax.axis_size(axis)
    return lax.ppermute(block, axis, [((i - distance) % count, i) for i in range(count)])


def times(a, b, dims=((1,), (0,))):
    return lax.dot_general(a, b, (dims, ((), ())), preferred_element_type=F32)


def chunk_shape(rows, columns):
    return (columns // LANES * rows + TAIL, LANES)


def put_chunk(ref, value):
    rows, columns = value.shape
    largest = jnp.max(jnp.abs(value), axis=0, keepdims=True)
    power = jnp.ceil(jnp.log(jnp.maximum(largest, 2.0**-100)) * (1 / STEP))
    coded = jnp.round(value * (TOP * jnp.exp(power * -STEP))).astype(I32)
    power = power.astype(I32)
    tail = jnp.zeros((TAIL, LANES), I32)
    row = lax.broadcasted_iota(I32, (TAIL, LANES), 0)
    for j in range(columns // LANES):
        part = slice(j * LANES, (j + 1) * LANES)
        ref[pl.ds(j * rows, rows), :] = coded[:, part].astype(I16)
        tail = jnp.where(row == j, power[:, part], tail)
    ref[pl.ds(columns // LANES * rows, TAIL), :] = tail.astype(I16)


def chunk_sum(refs, rows, blocks):
    total = [0.0] * blocks
    for ref in refs:
        tail = jnp.exp(ref[pl.ds(blocks * rows, TAIL), :].astype(F32) * STEP) * (1 / TOP)
        for j in range(blocks):
            total[j] += ref[pl.ds(j * rows, rows), :].astype(F32) * tail[j : j + 1, :]
    return total


def features_of(patches, core, depth):
    features = patches.shape[1]
    i = lax.broadcasted_iota(I32, (features // 2, features), 0)
    j = lax.broadcasted_iota(I32, (features // 2, features), 1)
    chosen = jnp.where(j == (i // depth * 2 + core) * depth + i % depth, 1.0, 0.0).astype(BF16)
    return times(chosen, patches, ((1,), (1,))).astype(BF16)


def own_kernel(depth, place, patches, grad_embed, out, p_held, g_held, arrived):
    count, _, columns = out.shape
    here = [pl.ds(pl.multiple_of((place[0] ^ k) * columns, columns), columns) for k in range(count)]
    copies = [pltpu.make_async_copy(patches, p_held, arrived.at[count])]
    for k, at in enumerate(here):
        copies.append(pltpu.make_async_copy(grad_embed.at[:, at], g_held.at[k], arrived.at[k]))
    for copy in copies:
        copy.start()
    copies[0].wait()
    left = features_of(p_held[...], place[2], depth)
    for k in range(count):
        copies[1 + k].wait()
        out[k] = times(left, g_held[k])


def partial_kernel(depth, place, shares, own, patches, grad_embed, *outs):
    me, replica, core = place[0], place[1] * 2 + place[2], place[2]
    tokens, columns = patches.shape[0], own.shape[2]
    count = shares.shape[0]
    row, column = (lax.broadcasted_iota(I32, shares.shape, i) for i in (0, 1))

    def factor(r):
        held = jnp.where(row == (r + (count - 1) * column) % count, shares[...], 0).astype(F32)
        return jnp.sum(jnp.sum(held, axis=1, keepdims=True), axis=0, keepdims=True) / (tokens * len(outs))

    left = features_of(patches[...], core, depth)
    scale, scale_sib = factor(replica), factor(replica ^ 1)
    for k, out in enumerate(outs):
        here = pl.ds(pl.multiple_of((me ^ k) * columns, columns), columns)
        put_chunk(out, scale * own[k] + scale_sib * times(left, grad_embed[:, here]))


def middle_kernel(depth, rows, place, *refs):
    *refs, held = refs
    blocks = held.shape[0]
    chunks = (refs[0].shape[0] - TAIL) // rows
    assert chunks == blocks
    peers = rows // depth
    ins, outs = refs[:-peers], refs[-peers:]
    for j, part in enumerate(chunk_sum(ins, rows, blocks)):
        held[j] = part
    for k, out in enumerate(outs):
        here = pl.ds(pl.multiple_of((place[1] ^ k) * depth, depth), depth)
        put_chunk(out, jnp.concatenate([held[j, here, :] for j in range(blocks)], axis=1))


def last_kernel(*refs):
    *ins, out = refs
    rows, columns = out.shape
    for j, part in enumerate(chunk_sum(ins, rows, columns // LANES)):
        out[:, j * LANES : (j + 1) * LANES] = part


def near_kernel(patches, own, first, out, p_held, held, arrived):
    copies = [
        pltpu.make_async_copy(patches, p_held, arrived.at[0]),
        pltpu.make_async_copy(own, held, arrived.at[1]),
    ]
    for copy in copies:
        copy.start()
    copies[0].wait()
    out[1] = times(p_held[...], first[...]).astype(BF16)
    copies[1].wait()
    out[0] = times(p_held[...], held[...]).astype(BF16)


def embed_kernel(place, patches, near, second, far, far_sib, out, p_held, arrived):
    me, core = place[0], place[2]
    columns = near.shape[2]
    copy = pltpu.make_async_copy(patches, p_held, arrived)
    copy.start()

    def put(k, value):
        out[:, pl.ds(pl.multiple_of((me ^ k) * columns, columns), columns)] = value

    put(0, near[0])
    put(1 + core, near[1])
    copy.wait()
    put(2 - core, times(p_held[...], second[...]).astype(BF16))

    @pl.when(core == 0)
    def _():
        put(3, times(p_held[...], far[...]).astype(BF16))

    @pl.when(core == 1)
    def _():
        put(3, times(p_held[...], far_sib[...]).astype(BF16))


def call(kernel, outs, operands, specs=(), scratch=(), flops=0):
    moved = sum(math.prod(a.shape) * a.dtype.itemsize for a in [*operands, *jax.tree.leaves(outs)])
    return pl.pallas_call(
        kernel,
        out_shape=outs,
        in_specs=[*specs] + [VMEM] * (len(operands) - len(specs)),
        out_specs=jax.tree.map(lambda _: VMEM, outs),
        scratch_shapes=scratch,
        compiler_params=pltpu.CompilerParams(vmem_limit_bytes=40 * 2**20),
        cost_estimate=pl.CostEstimate(flops=flops, bytes_accessed=moved, transcendentals=0),
    )(*operands)


def tiled_body(patches, grad_embed, weight, straggler, decode, encode):
    count_dp, count_fsdp = lax.axis_size("dp"), lax.axis_size("fsdp")
    dp, me = lax.axis_index("dp"), lax.axis_index("fsdp")
    core = dp % 2
    place = jnp.stack([me, dp // 2, core])
    tokens, features = patches.shape
    columns = weight.shape[1]
    rows, depth, blocks = features // 2, features // count_dp, columns // LANES

    with jax.named_scope("swap_inputs"):
        g_sib = exchange(grad_embed, "dp", 1)
        p_sib = exchange(patches, "dp", 1)
        shares = jnp.broadcast_to((straggler * decode)[:, None] * encode, (count_dp, 2))
        shares = lax.all_to_all(shares, "dp", 0, 0, tiled=True)

    with jax.named_scope("gather_weight"):
        both = ("dp", "fsdp")
        near = [(d * 4 + f, d * 4 + (f ^ (1 + d % 2))) for d in range(count_dp) for f in range(4)]
        cross = [(d * 4 + f, d * 4 + (f ^ 3)) for d in range(0, count_dp, 2) for f in range(4)]
        first = lax.ppermute(weight, both, near)
        far = lax.ppermute(weight, both, cross)

    with jax.named_scope("own"):
        own = call(
            functools.partial(own_kernel, depth),
            jax.ShapeDtypeStruct((count_fsdp, rows, columns), F32),
            [place, in_hbm(patches), in_hbm(grad_embed)],
            [SMEM, HBM, HBM],
            [
                pltpu.VMEM(patches.shape, BF16),
                pltpu.VMEM((count_fsdp, tokens, columns), BF16),
                pltpu.SemaphoreType.DMA((count_fsdp + 1,)),
            ],
            flops=2 * tokens * rows * columns * count_fsdp,
        )
    with jax.named_scope("partial"):
        chunk = jax.ShapeDtypeStruct(chunk_shape(rows, columns), I16)
        parts = call(
            functools.partial(partial_kernel, depth),
            [chunk] * count_fsdp,
            [place, shares, own, p_sib, g_sib],
            [SMEM],
            flops=2 * tokens * rows * columns * count_fsdp,
        )
        parts = [exchange(part, "fsdp", k) if k else part for k, part in enumerate(parts)]
    with jax.named_scope("embed_near"):
        near = call(
            near_kernel,
            jax.ShapeDtypeStruct((2, tokens, columns), BF16),
            [in_hbm(patches), in_hbm(weight), first],
            [HBM, HBM],
            [pltpu.VMEM(patches.shape, BF16), pltpu.VMEM(weight.shape, BF16), pltpu.SemaphoreType.DMA((2,))],
            flops=4 * tokens * features * columns,
        )
        near, *parts = lax.optimization_barrier((near, *parts))
    with jax.named_scope("middle"):
        chunk = jax.ShapeDtypeStruct(chunk_shape(depth, columns), I16)
        parts = call(
            functools.partial(middle_kernel, depth, rows),
            [chunk] * (count_dp // 2),
            [place, *parts],
            [SMEM],
            [pltpu.VMEM((blocks, rows, LANES), F32)],
        )
        parts = [exchange(part, "dp", 2 * k) if k else part for k, part in enumerate(parts)]
    with jax.named_scope("share_weight"):
        sent, far, parts[0] = lax.optimization_barrier((first, far, parts[0]))
        second = exchange(sent, "dp", 1)
        far_sib = lax.ppermute(far, "dp", [(d, d + 1) for d in range(0, count_dp, 2)])
    with jax.named_scope("embed"):
        embedded = call(
            embed_kernel,
            jax.ShapeDtypeStruct((tokens, columns * count_fsdp), BF16),
            [place, in_hbm(patches), near, second, far, far_sib],
            [SMEM, HBM],
            [pltpu.VMEM(patches.shape, BF16), pltpu.SemaphoreType.DMA],
            flops=4 * tokens * features * columns,
        )
    with jax.named_scope("last"):
        embedded, *parts = lax.optimization_barrier((embedded, *parts))
        decoded = call(last_kernel, jax.ShapeDtypeStruct((depth, columns), F32), parts)
    return embedded, decoded


def plain_body(patches, grad_embed, weight, straggler, decode, encode):
    shares = (straggler * decode)[:, None] * encode
    factor = (shares[:, 0] + shifted(shares[:, 1], "dp", 1))[0]
    scale = factor.astype(F32) / (patches.shape[0] * lax.axis_size("fsdp"))
    whole = lax.all_gather(weight, "fsdp", axis=1, tiled=True)
    embedded = times(patches, whole).astype(BF16)
    term = scale * times(grad_embed, patches, ((0,), (0,)))
    term = lax.psum_scatter(term, "fsdp", scatter_dimension=0, tiled=True)
    return embedded, lax.psum_scatter(term.T, "dp", scatter_dimension=0, tiled=True)


def body(patches, grad_embed, weight, straggler, decode, encode):
    fits = patches.shape[1] % (16 * lax.axis_size("dp")) == 0 and weight.shape[1] % LANES == 0
    fits = fits and lax.axis_size("fsdp") == 4
    run = tiled_body if fits else plain_body
    return run(patches, grad_embed, weight, straggler, decode, encode)


def solution(mesh):
    return jax.shard_map(
        body,
        mesh=mesh,
        in_specs=(
            P(("dp", "fsdp"), None),
            P(("dp", "fsdp"), None),
            P(None, "fsdp"),
            P("dp"),
            P("dp"),
            P("dp", None),
        ),
        out_specs=(P(("dp", "fsdp"), None), P("dp", "fsdp")),
        check_vma=False,
    )
```

```python
import functools
import math

import jax
import jax.numpy as jnp
from jax import lax
from jax.experimental import pallas as pl
from jax.experimental.pallas import tpu as pltpu
from jax.sharding import PartitionSpec as P

LANES = 128
TAIL = 16
STEP = math.log(2) / 16
TOP = 32760.0
F32, BF16, I16, I32 = jnp.float32, jnp.bfloat16, jnp.int16, jnp.int32
VMEM = pl.BlockSpec(memory_space=pltpu.VMEM)
SMEM = pl.BlockSpec(memory_space=pltpu.SMEM)
HBM = pl.BlockSpec(memory_space=pltpu.HBM)


def in_hbm(array):
    return pltpu.with_memory_space_constraint(array, pltpu.HBM)


def exchange(block, axis, step):
    return lax.ppermute(block, axis, [(i, i ^ step) for i in range(lax.axis_size(axis))])


def shifted(block, axis, distance):
    count = lax.axis_size(axis)
    return lax.ppermute(block, axis, [((i - distance) % count, i) for i in range(count)])


def times(a, b, dims=((1,), (0,))):
    return lax.dot_general(a, b, (dims, ((), ())), preferred_element_type=F32)


def chunk_shape(rows, columns):
    return (columns // LANES * rows + TAIL, LANES)


def put_chunk(ref, blocks, extra=()):
    rows = blocks[0].shape[0]
    tail = jnp.zeros((TAIL, LANES), I32)
    row = lax.broadcasted_iota(I32, (TAIL, LANES), 0)
    for j, block in enumerate(blocks):
        largest = jnp.max(jnp.abs(block), axis=0, keepdims=True)
        power = jnp.ceil(jnp.log(jnp.maximum(largest, 2.0**-100)) * (1 / STEP))
        coded = jnp.round(block * (TOP * jnp.exp(power * -STEP)))
        ref[pl.ds(j * rows, rows), :] = coded.astype(I32).astype(I16)
        tail = jnp.where(row == j, power.astype(I32), tail)
    for j, number in enumerate(extra):
        tail = jnp.where(row == TAIL - len(extra) + j, number, tail)
    ref[pl.ds(len(blocks) * rows, TAIL), :] = tail.astype(I16)


def get_chunk(ref, rows):
    count = (ref.shape[0] - TAIL) // rows
    tail = ref[pl.ds(count * rows, TAIL), :].astype(F32)
    scale = jnp.exp(tail * STEP) * (1 / TOP)
    return [ref[pl.ds(j * rows, rows), :].astype(F32) * scale[j : j + 1, :] for j in range(count)], tail


def lanes(j):
    return slice(j * LANES, (j + 1) * LANES)


def own_kernel(depth, place, straggler, decode, encode, patches, grad_embed, *refs):
    kept, sent, shares, p_held, g_held, arrived = refs
    me, core = place[0], place[2]
    count, blocks, rows, _ = kept.shape
    columns, features = blocks * LANES, 2 * rows
    copies = [pltpu.make_async_copy(patches, p_held, arrived.at[count])]
    for k in range(count):
        here = pl.ds(pl.multiple_of((me ^ k) * columns, columns), columns)
        copies.append(pltpu.make_async_copy(grad_embed.at[:, here], g_held.at[k], arrived.at[k]))
    for copy in copies:
        copy.start()
    served = straggler[0] * decode[0]
    extra = served * encode[0, 0], served * encode[0, 1]
    row = lax.broadcasted_iota(I32, shares.shape, 0)
    shares[...] = jnp.where(row == 0, extra[0], extra[1])
    i = lax.broadcasted_iota(I32, (features, features), 0)
    j = lax.broadcasted_iota(I32, (features, features), 1)
    half, i = i // rows, i % rows
    chosen = jnp.where(j == (i // depth * 2 + (core ^ half)) * depth + i % depth, 1.0, 0.0).astype(BF16)
    copies[0].wait()
    left = times(chosen, p_held[...], ((1,), (1,))).astype(BF16)
    for k in range(count):
        copies[1 + k].wait()
        value = times(left, g_held[k])
        for j in range(blocks):
            kept[k, j] = value[:rows, lanes(j)]
        put_chunk(sent.at[k], [value[rows:, lanes(j)] for j in range(blocks)], extra)


def pair_kernel(place, tokens, kept, came, shares, before, before_sib, still, sent):
    core = place[2]
    _, blocks, rows, _ = kept.shape
    first, second = shares[0:1, 0:1].astype(F32), shares[1:2, 0:1].astype(F32)
    tail = get_chunk(came.at[0], rows)[1]
    first_sib, second_sib = tail[TAIL - 2 : TAIL - 1, 0:1], tail[TAIL - 1 :, 0:1]
    even = core == 0
    carried = jnp.where(even, before[1:2, 0:1], before_sib[1:2, 0:1]).astype(F32)
    scale = (first + jnp.where(even, carried, second_sib)) / tokens[0].astype(F32)
    scale_sib = (first_sib + jnp.where(even, second, carried)) / tokens[0].astype(F32)

    def value(k):
        parts, _ = get_chunk(came.at[k], rows)
        return [scale * kept[k, j] + scale_sib * part for j, part in enumerate(parts)]

    put_chunk(sent.at[0], value(1 + core))
    put_chunk(sent.at[1], value(3))
    for at, k in enumerate((0, 2 - core)):
        for j, part in enumerate(value(k)):
            still[at, j] = part


def step_kernel(kept, came, still, sent):
    _, blocks, rows, _ = kept.shape
    parts, _ = get_chunk(came.at[1], rows)
    put_chunk(sent, [kept[1, j] + part for j, part in enumerate(parts)])
    for j, part in enumerate(get_chunk(came.at[0], rows)[0]):
        still[j] = kept[0, j] + part


def middle_kernel(depth, place, kept, came, *refs):
    *outs, held = refs
    blocks, rows, _ = kept.shape
    for j, part in enumerate(get_chunk(came, rows)[0]):
        held[j] = kept[j] + part
    for k, out in enumerate(outs):
        here = pl.ds(pl.multiple_of((place[1] ^ k) * depth, depth), depth)
        put_chunk(out, [held[j, here, :] for j in range(blocks)])


def last_kernel(*refs):
    *ins, out = refs
    parts = [get_chunk(ref, out.shape[0])[0] for ref in ins]
    for j, terms in enumerate(zip(*parts)):
        out[:, lanes(j)] = sum(terms[1:], terms[0])


def near_kernel(patches, own, first, far, out, sent, p_held, held, arrived):
    copies = [
        pltpu.make_async_copy(patches, p_held, arrived.at[0]),
        pltpu.make_async_copy(own, held, arrived.at[1]),
    ]
    for copy in copies:
        copy.start()
    sent[0] = first[...]
    sent[1] = far[...]
    copies[0].wait()
    out[1] = times(p_held[...], first[...]).astype(BF16)
    copies[1].wait()
    out[0] = times(p_held[...], held[...]).astype(BF16)


def embed_kernel(place, patches, near, far, came, out, p_held, arrived):
    me, core = place[0], place[2]
    columns = near.shape[2]
    copy = pltpu.make_async_copy(patches, p_held, arrived)
    copy.start()

    def put(k, value):
        out[:, pl.ds(pl.multiple_of((me ^ k) * columns, columns), columns)] = value

    put(0, near[0])
    put(1 + core, near[1])
    copy.wait()
    put(2 - core, times(p_held[...], came[0]).astype(BF16))

    @pl.when(core == 0)
    def _():
        put(3, times(p_held[...], far[...]).astype(BF16))

    @pl.when(core == 1)
    def _():
        put(3, times(p_held[...], came[1]).astype(BF16))


def call(kernel, outs, operands, specs=(), scratch=(), flops=0):
    moved = sum(math.prod(a.shape) * a.dtype.itemsize for a in [*operands, *jax.tree.leaves(outs)]) if flops else 0
    return pl.pallas_call(
        kernel,
        out_shape=outs,
        in_specs=[*specs] + [VMEM] * (len(operands) - len(specs)),
        out_specs=jax.tree.map(lambda _: VMEM, outs),
        scratch_shapes=scratch,
        compiler_params=pltpu.CompilerParams(vmem_limit_bytes=40 * 2**20),
        cost_estimate=pl.CostEstimate(flops=flops, bytes_accessed=moved, transcendentals=0),
    )(*operands)


def tiled_body(patches, grad_embed, weight, straggler, decode, encode):
    count_dp, count_fsdp = lax.axis_size("dp"), lax.axis_size("fsdp")
    dp, me = lax.axis_index("dp"), lax.axis_index("fsdp")
    core = dp % 2
    place = jnp.stack([me, dp // 2, core])
    tokens, features = patches.shape
    columns = weight.shape[1]
    rows, depth, blocks = features // 2, features // count_dp, columns // LANES
    chunk = chunk_shape(rows, columns)
    even = range(0, count_dp, 2)

    def along_planes(block, step, replicas):
        pairs = [(d * 4 + f, d * 4 + (f ^ step(d % 2))) for d in replicas for f in range(4)]
        return lax.ppermute(block, ("dp", "fsdp"), pairs)

    with jax.named_scope("gather_weight"):
        first = along_planes(weight, lambda c: 1 + c, range(count_dp))
        far = along_planes(weight, lambda c: 3, even)

    with jax.named_scope("own"):
        kept, sent, shares = call(
            functools.partial(own_kernel, depth),
            [
                jax.ShapeDtypeStruct((count_fsdp, blocks, rows, LANES), F32),
                jax.ShapeDtypeStruct((count_fsdp, *chunk), I16),
                jax.ShapeDtypeStruct((8, LANES), I32),
            ],
            [place, straggler, decode, encode, in_hbm(patches), in_hbm(grad_embed)],
            [SMEM] * 4 + [HBM] * 2,
            [
                pltpu.VMEM(patches.shape, BF16),
                pltpu.VMEM((count_fsdp, tokens, columns), BF16),
                pltpu.SemaphoreType.DMA((count_fsdp + 1,)),
            ],
        )
    with jax.named_scope("pair"):
        came = exchange(sent, "dp", 1)
        before = lax.ppermute(shares, "dp", [((d - 1) % count_dp, d) for d in even])
        before_sib = lax.ppermute(shares, "dp", [((d - 1) % count_dp, d + 1) for d in even])
        kept, sent = call(
            pair_kernel,
            [
                jax.ShapeDtypeStruct((2, blocks, rows, LANES), F32),
                jax.ShapeDtypeStruct((2, *chunk), I16),
            ],
            [place, jnp.full((1,), tokens * count_fsdp, I32), kept, came, shares, before, before_sib],
            [SMEM] * 2,
        )
    with jax.named_scope("first_step"):
        came = along_planes(sent, lambda c: 1 + c, range(count_dp))
    with jax.named_scope("embed_near"):
        first, far, kept = lax.optimization_barrier((first, far, kept))
        near, pack = call(
            near_kernel,
            [jax.ShapeDtypeStruct((2, tokens, columns), BF16), jax.ShapeDtypeStruct((2, *weight.shape), BF16)],
            [in_hbm(patches), in_hbm(weight), first, far],
            [HBM, HBM],
            [pltpu.VMEM(patches.shape, BF16), pltpu.VMEM(weight.shape, BF16), pltpu.SemaphoreType.DMA((2,))],
            flops=4 * tokens * features * columns,
        )
    with jax.named_scope("first_step_sum"):
        near, pack, came = lax.optimization_barrier((near, pack, came))
        kept, sent = call(
            step_kernel,
            [jax.ShapeDtypeStruct((blocks, rows, LANES), F32), jax.ShapeDtypeStruct(chunk, I16)],
            [kept, came],
        )
    with jax.named_scope("second_step"):
        came = along_planes(sent, lambda c: 2 - c, range(count_dp))
    with jax.named_scope("share_weight"):
        pack = exchange(pack, "dp", 1)
    with jax.named_scope("middle"):
        parts = call(
            functools.partial(middle_kernel, depth),
            [jax.ShapeDtypeStruct(chunk_shape(depth, columns), I16)] * (count_dp // 2),
            [place, kept, came],
            [SMEM],
            [pltpu.VMEM((blocks, rows, LANES), F32)],
        )
        parts = [exchange(part, "dp", 2 * k) if k else part for k, part in enumerate(parts)]
    with jax.named_scope("embed"):
        embedded = call(
            embed_kernel,
            jax.ShapeDtypeStruct((tokens, columns * count_fsdp), BF16),
            [place, in_hbm(patches), near, far, pack],
            [SMEM, HBM],
            [pltpu.VMEM(patches.shape, BF16), pltpu.SemaphoreType.DMA],
            flops=4 * tokens * features * columns,
        )
    with jax.named_scope("last"):
        embedded, *parts = lax.optimization_barrier((embedded, *parts))
        decoded = call(last_kernel, jax.ShapeDtypeStruct((depth, columns), F32), parts)
    return embedded, decoded


def plain_body(patches, grad_embed, weight, straggler, decode, encode):
    shares = (straggler * decode)[:, None] * encode
    factor = (shares[:, 0] + shifted(shares[:, 1], "dp", 1))[0]
    scale = factor.astype(F32) / (patches.shape[0] * lax.axis_size("fsdp"))
    whole = lax.all_gather(weight, "fsdp", axis=1, tiled=True)
    embedded = times(patches, whole).astype(BF16)
    term = scale * times(grad_embed, patches, ((0,), (0,)))
    term = lax.psum_scatter(term, "fsdp", scatter_dimension=0, tiled=True)
    return embedded, lax.psum_scatter(term.T, "dp", scatter_dimension=0, tiled=True)


def body(patches, grad_embed, weight, straggler, decode, encode):
    fits = patches.shape[1] % (16 * lax.axis_size("dp")) == 0 and weight.shape[1] % LANES == 0
    fits = fits and lax.axis_size("fsdp") == 4
    run = tiled_body if fits else plain_body
    return run(patches, grad_embed, weight, straggler, decode, encode)


def solution(mesh):
    return jax.shard_map(
        body,
        mesh=mesh,
        in_specs=(
            P(("dp", "fsdp"), None),
            P(("dp", "fsdp"), None),
            P(None, "fsdp"),
            P("dp"),
            P("dp"),
            P("dp", None),
        ),
        out_specs=(P(("dp", "fsdp"), None), P("dp", "fsdp")),
        check_vma=False,
    )
```

```python
import functools
import math

import jax
import jax.numpy as jnp
from jax import lax
from jax.experimental import pallas as pl
from jax.experimental.pallas import tpu as pltpu
from jax.sharding import PartitionSpec as P

LANES = 128
TAIL = 16
STEP = math.log(2) / 16
TOP = 32760.0
F32, BF16, I16, I32 = jnp.float32, jnp.bfloat16, jnp.int16, jnp.int32
VMEM = pl.BlockSpec(memory_space=pltpu.VMEM)
SMEM = pl.BlockSpec(memory_space=pltpu.SMEM)
HBM = pl.BlockSpec(memory_space=pltpu.HBM)


def in_hbm(array):
    return pltpu.with_memory_space_constraint(array, pltpu.HBM)


def exchange(block, axis, step):
    return lax.ppermute(block, axis, [(i, i ^ step) for i in range(lax.axis_size(axis))])


def shifted(block, axis, distance):
    count = lax.axis_size(axis)
    return lax.ppermute(block, axis, [((i - distance) % count, i) for i in range(count)])


def times(a, b, dims=((1,), (0,))):
    return lax.dot_general(a, b, (dims, ((), ())), preferred_element_type=F32)


def chunk_shape(rows, columns):
    return (columns // LANES * rows + TAIL, LANES)


def put_chunk(ref, blocks, extra=()):
    rows = blocks[0].shape[0]
    tail = jnp.zeros((TAIL, LANES), I32)
    row = lax.broadcasted_iota(I32, (TAIL, LANES), 0)
    for j, block in enumerate(blocks):
        largest = jnp.max(jnp.abs(block), axis=0, keepdims=True)
        power = jnp.ceil(jnp.log(jnp.maximum(largest, 2.0**-100)) * (1 / STEP))
        coded = jnp.round(block * (TOP * jnp.exp(power * -STEP)))
        ref[pl.ds(j * rows, rows), :] = coded.astype(I32).astype(I16)
        tail = jnp.where(row == j, power.astype(I32), tail)
    for j, number in enumerate(extra):
        tail = jnp.where(row == TAIL - len(extra) + j, number, tail)
    ref[pl.ds(len(blocks) * rows, TAIL), :] = tail.astype(I16)


def get_chunk(ref, rows):
    count = (ref.shape[0] - TAIL) // rows
    tail = ref[pl.ds(count * rows, TAIL), :].astype(F32)
    scale = jnp.exp(tail * STEP) * (1 / TOP)
    return [ref[pl.ds(j * rows, rows), :].astype(F32) * scale[j : j + 1, :] for j in range(count)], tail


def lanes(j):
    return slice(j * LANES, (j + 1) * LANES)


def send_kernel(depth, place, patches, grad_embed, shares, before, sent, left, held, p_held, arrived):
    me, core = place[0], place[2]
    count, _, columns = held.shape
    blocks, features = columns // LANES, patches.shape[1]
    rows = features // 2
    copies = [pltpu.make_async_copy(patches, p_held, arrived.at[count])]
    for k in range(count):
        here = pl.ds(pl.multiple_of((me ^ k) * columns, columns), columns)
        copies.append(pltpu.make_async_copy(grad_embed.at[:, here], held.at[k], arrived.at[k]))
    for copy in copies:
        copy.start()
    extra = shares[:, 0:1], shares[:, 1:2], before[:, 1:2]
    i = lax.broadcasted_iota(I32, (features, features), 0)
    j = lax.broadcasted_iota(I32, (features, features), 1)
    half, i = i // rows, i % rows
    chosen = jnp.where(j == (i // depth * 2 + (core ^ half)) * depth + i % depth, 1.0, 0.0).astype(BF16)
    copies[0].wait()
    turned = times(chosen, p_held[...], ((1,), (1,))).astype(BF16)
    left[...] = turned[:rows]
    for k in range(count):
        copies[1 + k].wait()
        value = times(turned[rows:], held[k])
        put_chunk(sent.at[k], [value[:, lanes(j)] for j in range(blocks)], extra)


def own_kernel(left, held, kept):
    for k in range(kept.shape[0]):
        value = times(left[...], held[k])
        for j in range(kept.shape[1]):
            kept[k, j] = value[:, lanes(j)]


def pair_kernel(place, tokens, kept, came, shares, before, still, sent):
    core = place[2]
    _, blocks, rows, _ = kept.shape
    first, second, carried = (a.astype(F32) for a in (shares[:, 0:1], shares[:, 1:2], before[:, 1:2]))
    tail = get_chunk(came.at[0], rows)[1]
    first_sib, second_sib, carried_sib = (tail[TAIL - 3 + j : TAIL - 2 + j, 0:1] for j in range(3))
    even = core == 0
    scale = (first + jnp.where(even, carried, second_sib)) / tokens[0].astype(F32)
    scale_sib = (first_sib + jnp.where(even, second, carried_sib)) / tokens[0].astype(F32)

    def value(k):
        parts, _ = get_chunk(came.at[k], rows)
        return [scale * kept[k, j] + scale_sib * part for j, part in enumerate(parts)]

    put_chunk(sent.at[0], value(1 + core))
    put_chunk(sent.at[1], value(3))
    for at, k in enumerate((0, 2 - core)):
        for j, part in enumerate(value(k)):
            still[at, j] = part


def step_kernel(kept, came, still, sent):
    _, blocks, rows, _ = kept.shape
    parts, _ = get_chunk(came.at[1], rows)
    put_chunk(sent, [kept[1, j] + part for j, part in enumerate(parts)])
    for j, part in enumerate(get_chunk(came.at[0], rows)[0]):
        still[j] = kept[0, j] + part


def middle_kernel(depth, place, kept, came, *refs):
    *outs, held = refs
    blocks, rows, _ = kept.shape
    for j, part in enumerate(get_chunk(came, rows)[0]):
        held[j] = kept[j] + part
    for k, out in enumerate(outs):
        here = pl.ds(pl.multiple_of((place[1] ^ k) * depth, depth), depth)
        put_chunk(out, [held[j, here, :] for j in range(blocks)])


def last_kernel(*refs):
    *ins, out = refs
    parts = [get_chunk(ref, out.shape[0])[0] for ref in ins]
    for j, terms in enumerate(zip(*parts)):
        out[:, lanes(j)] = sum(terms[1:], terms[0])


def near_kernel(patches, own, first, out, p_held, held, arrived):
    copies = [
        pltpu.make_async_copy(patches, p_held, arrived.at[0]),
        pltpu.make_async_copy(own, held, arrived.at[1]),
    ]
    for copy in copies:
        copy.start()
    copies[0].wait()
    out[1] = times(p_held[...], first[...]).astype(BF16)
    copies[1].wait()
    out[0] = times(p_held[...], held[...]).astype(BF16)


def embed_kernel(place, patches, near, second, far, out, p_held, arrived):
    me, core = place[0], place[2]
    columns = near.shape[2]
    copy = pltpu.make_async_copy(patches, p_held, arrived)
    copy.start()

    def put(k, value):
        out[:, pl.ds(pl.multiple_of((me ^ k) * columns, columns), columns)] = value

    put(0, near[0])
    put(1 + core, near[1])
    copy.wait()
    put(2 - core, times(p_held[...], second[...]).astype(BF16))
    put(3, times(p_held[...], far[...]).astype(BF16))


def call(kernel, outs, operands, specs=(), scratch=(), flops=0):
    moved = sum(math.prod(a.shape) * a.dtype.itemsize for a in [*operands, *jax.tree.leaves(outs)]) if flops else 0
    return pl.pallas_call(
        kernel,
        out_shape=outs,
        in_specs=[*specs] + [VMEM] * (len(operands) - len(specs)),
        out_specs=jax.tree.map(lambda _: VMEM, outs),
        scratch_shapes=scratch,
        compiler_params=pltpu.CompilerParams(vmem_limit_bytes=40 * 2**20),
        cost_estimate=pl.CostEstimate(flops=flops, bytes_accessed=moved, transcendentals=0),
    )(*operands)


def tiled_body(patches, grad_embed, weight, straggler, decode, encode):
    count_dp, count_fsdp = lax.axis_size("dp"), lax.axis_size("fsdp")
    dp, me = lax.axis_index("dp"), lax.axis_index("fsdp")
    core = dp % 2
    place = jnp.stack([me, dp // 2, core])
    tokens, features = patches.shape
    columns = weight.shape[1]
    rows, depth, blocks = features // 2, features // count_dp, columns // LANES
    chunk = chunk_shape(rows, columns)
    even = range(0, count_dp, 2)

    def along_planes(block, step, replicas):
        pairs = [(d * 4 + f, d * 4 + (f ^ step(d % 2))) for d in replicas for f in range(4)]
        return lax.ppermute(block, ("dp", "fsdp"), pairs)

    with jax.named_scope("gather_weight"):
        first = along_planes(weight, lambda c: 1 + c, range(count_dp))

    with jax.named_scope("shares"):
        shares = encode * straggler[:, None] * decode[:, None]
        before = lax.ppermute(shares, "dp", [((d - 1) % count_dp, d) for d in even])
    with jax.named_scope("send"):
        sent, left, held = call(
            functools.partial(send_kernel, depth),
            [
                jax.ShapeDtypeStruct((count_fsdp, *chunk), I16),
                jax.ShapeDtypeStruct((rows, tokens), BF16),
                jax.ShapeDtypeStruct((count_fsdp, tokens, columns), BF16),
            ],
            [place, in_hbm(patches), in_hbm(grad_embed), shares, before],
            [SMEM, HBM, HBM],
            [pltpu.VMEM(patches.shape, BF16), pltpu.SemaphoreType.DMA((count_fsdp + 1,))],
        )
    with jax.named_scope("own"):
        kept = call(
            own_kernel,
            jax.ShapeDtypeStruct((count_fsdp, blocks, rows, LANES), F32),
            [left, held],
            flops=2 * tokens * rows * columns * count_fsdp,
        )
    with jax.named_scope("pair"):
        came = exchange(sent, "dp", 1)
        first, came = lax.optimization_barrier((first, came))
        kept, sent = call(
            pair_kernel,
            [
                jax.ShapeDtypeStruct((2, blocks, rows, LANES), F32),
                jax.ShapeDtypeStruct((2, *chunk), I16),
            ],
            [place, jnp.full((1,), tokens * count_fsdp, I32), kept, came, shares, before],
            [SMEM] * 2,
        )
    with jax.named_scope("first_step"):
        came = along_planes(sent, lambda c: 1 + c, range(count_dp))
    with jax.named_scope("embed_near"):
        near = call(
            near_kernel,
            jax.ShapeDtypeStruct((2, tokens, columns), BF16),
            [in_hbm(patches), in_hbm(weight), first],
            [HBM, HBM],
            [pltpu.VMEM(patches.shape, BF16), pltpu.VMEM(weight.shape, BF16), pltpu.SemaphoreType.DMA((2,))],
            flops=4 * tokens * features * columns,
        )
    with jax.named_scope("first_step_sum"):
        near, came = lax.optimization_barrier((near, came))
        kept, sent = call(
            step_kernel,
            [jax.ShapeDtypeStruct((blocks, rows, LANES), F32), jax.ShapeDtypeStruct(chunk, I16)],
            [kept, came],
        )
    with jax.named_scope("second_step"):
        came = along_planes(sent, lambda c: 2 - c, range(count_dp))
    with jax.named_scope("share_weight"):
        shared, kept = lax.optimization_barrier((first, kept))
        second = exchange(shared, "dp", 1)
    with jax.named_scope("middle"):
        parts = call(
            functools.partial(middle_kernel, depth),
            [jax.ShapeDtypeStruct(chunk_shape(depth, columns), I16)] * (count_dp // 2),
            [place, kept, came],
            [SMEM],
            [pltpu.VMEM((blocks, rows, LANES), F32)],
        )
        parts = [exchange(part, "dp", 2 * k) if k else part for k, part in enumerate(parts)]
    with jax.named_scope("relay_weight"):
        far, parts[0] = lax.optimization_barrier((first, parts[0]))
        far = along_planes(far, lambda c: 2 - c, range(count_dp))
    with jax.named_scope("embed"):
        embedded = call(
            embed_kernel,
            jax.ShapeDtypeStruct((tokens, columns * count_fsdp), BF16),
            [place, in_hbm(patches), near, second, far],
            [SMEM, HBM],
            [pltpu.VMEM(patches.shape, BF16), pltpu.SemaphoreType.DMA],
            flops=4 * tokens * features * columns,
        )
    with jax.named_scope("last"):
        embedded, *parts = lax.optimization_barrier((embedded, *parts))
        decoded = call(last_kernel, jax.ShapeDtypeStruct((depth, columns), F32), parts)
    return embedded, decoded


def plain_body(patches, grad_embed, weight, straggler, decode, encode):
    shares = (straggler * decode)[:, None] * encode
    factor = (shares[:, 0] + shifted(shares[:, 1], "dp", 1))[0]
    scale = factor.astype(F32) / (patches.shape[0] * lax.axis_size("fsdp"))
    whole = lax.all_gather(weight, "fsdp", axis=1, tiled=True)
    embedded = times(patches, whole).astype(BF16)
    term = scale * times(grad_embed, patches, ((0,), (0,)))
    term = lax.psum_scatter(term, "fsdp", scatter_dimension=0, tiled=True)
    return embedded, lax.psum_scatter(term.T, "dp", scatter_dimension=0, tiled=True)


def body(patches, grad_embed, weight, straggler, decode, encode):
    fits = patches.shape[1] % (16 * lax.axis_size("dp")) == 0 and weight.shape[1] % LANES == 0
    fits = fits and lax.axis_size("fsdp") == 4
    run = tiled_body if fits else plain_body
    return run(patches, grad_embed, weight, straggler, decode, encode)


def solution(mesh):
    return jax.shard_map(
        body,
        mesh=mesh,
        in_specs=(
            P(("dp", "fsdp"), None),
            P(("dp", "fsdp"), None),
            P(None, "fsdp"),
            P("dp"),
            P("dp"),
            P("dp", None),
        ),
        out_specs=(P(("dp", "fsdp"), None), P("dp", "fsdp")),
        check_vma=False,
    )
```

```python
import functools
import math

import jax
import jax.numpy as jnp
from jax import lax
from jax.experimental import pallas as pl
from jax.experimental.pallas import tpu as pltpu
from jax.sharding import PartitionSpec as P

LANES = 128
TAIL = 16
STEP = math.log(2) / 16
TOP = 32760.0
F32, BF16, I16, I32 = jnp.float32, jnp.bfloat16, jnp.int16, jnp.int32
VMEM = pl.BlockSpec(memory_space=pltpu.VMEM)
SMEM = pl.BlockSpec(memory_space=pltpu.SMEM)
HBM = pl.BlockSpec(memory_space=pltpu.HBM)


def in_hbm(array):
    return pltpu.with_memory_space_constraint(array, pltpu.HBM)


def exchange(block, axis, step):
    return lax.ppermute(block, axis, [(i, i ^ step) for i in range(lax.axis_size(axis))])


def shifted(block, axis, distance):
    count = lax.axis_size(axis)
    return lax.ppermute(block, axis, [((i - distance) % count, i) for i in range(count)])


def times(a, b, dims=((1,), (0,))):
    return lax.dot_general(a, b, (dims, ((), ())), preferred_element_type=F32)


def chunk_shape(rows, columns):
    return (columns // LANES * rows + TAIL, LANES)


def put_chunk(ref, blocks, extra=()):
    rows = blocks[0].shape[0]
    tail = jnp.zeros((TAIL, LANES), I32)
    row = lax.broadcasted_iota(I32, (TAIL, LANES), 0)
    for j, block in enumerate(blocks):
        largest = jnp.max(jnp.abs(block), axis=0, keepdims=True)
        power = jnp.ceil(jnp.log(jnp.maximum(largest, 2.0**-100)) * (1 / STEP))
        coded = jnp.round(block * (TOP * jnp.exp(power * -STEP)))
        ref[pl.ds(j * rows, rows), :] = coded.astype(I32).astype(I16)
        tail = jnp.where(row == j, power.astype(I32), tail)
    for j, number in enumerate(extra):
        tail = jnp.where(row == TAIL - len(extra) + j, number, tail)
    ref[pl.ds(len(blocks) * rows, TAIL), :] = tail.astype(I16)


def get_chunk(ref, rows):
    count = (ref.shape[0] - TAIL) // rows
    tail = ref[pl.ds(count * rows, TAIL), :].astype(F32)
    scale = jnp.exp(tail * STEP) * (1 / TOP)
    return [ref[pl.ds(j * rows, rows), :].astype(F32) * scale[j : j + 1, :] for j in range(count)], tail


def lanes(j):
    return slice(j * LANES, (j + 1) * LANES)


def send_kernel(depth, place, patches, grad_embed, shares, sent, left, held, p_held, arrived):
    me, core = place[0], place[2]
    count, _, columns = held.shape
    blocks, features = columns // LANES, patches.shape[1]
    rows = features // 2
    copies = [pltpu.make_async_copy(patches, p_held, arrived.at[count])]
    for k in range(count):
        here = pl.ds(pl.multiple_of((me ^ k) * columns, columns), columns)
        copies.append(pltpu.make_async_copy(grad_embed.at[:, here], held.at[k], arrived.at[k]))
    for copy in copies:
        copy.start()
    extra = shares[:, 0:1], shares[:, 1:2]
    i = lax.broadcasted_iota(I32, (features, features), 0)
    j = lax.broadcasted_iota(I32, (features, features), 1)
    half, i = i // rows, i % rows
    chosen = jnp.where(j == (i // depth * 2 + (core ^ half)) * depth + i % depth, 1.0, 0.0).astype(BF16)
    copies[0].wait()
    turned = times(chosen, p_held[...], ((1,), (1,))).astype(BF16)
    left[...] = turned[:rows]
    for k in range(count):
        copies[1 + k].wait()
        value = times(turned[rows:], held[k])
        put_chunk(sent.at[k], [value[:, lanes(j)] for j in range(blocks)], extra)


def own_kernel(left, held, kept):
    for k in range(kept.shape[0]):
        value = times(left[...], held[k])
        for j in range(kept.shape[1]):
            kept[k, j] = value[:, lanes(j)]


def pair_kernel(place, tokens, kept, came, shares, before, before_sib, still, sent):
    core = place[2]
    _, blocks, rows, _ = kept.shape
    first, second = shares[:, 0:1].astype(F32), shares[:, 1:2].astype(F32)
    tail = get_chunk(came.at[0], rows)[1]
    first_sib, second_sib = (tail[TAIL - 2 + j : TAIL - 1 + j, 0:1] for j in range(2))
    even = core == 0
    carried = jnp.where(even, before[:, 1:2], before_sib[:, 1:2]).astype(F32)
    scale = (first + jnp.where(even, carried, second_sib)) / tokens[0].astype(F32)
    scale_sib = (first_sib + jnp.where(even, second, carried)) / tokens[0].astype(F32)

    def value(k):
        parts, _ = get_chunk(came.at[k], rows)
        return [scale * kept[k, j] + scale_sib * part for j, part in enumerate(parts)]

    put_chunk(sent.at[0], value(1 + core))
    put_chunk(sent.at[1], value(3))
    for at, k in enumerate((0, 2 - core)):
        for j, part in enumerate(value(k)):
            still[at, j] = part


def step_kernel(kept, came, still, sent):
    _, blocks, rows, _ = kept.shape
    parts, _ = get_chunk(came.at[1], rows)
    put_chunk(sent, [kept[1, j] + part for j, part in enumerate(parts)])
    for j, part in enumerate(get_chunk(came.at[0], rows)[0]):
        still[j] = kept[0, j] + part


def middle_kernel(depth, place, kept, came, *refs):
    *outs, held = refs
    blocks, rows, _ = kept.shape
    for j, part in enumerate(get_chunk(came, rows)[0]):
        held[j] = kept[j] + part
    for k, out in enumerate(outs):
        here = pl.ds(pl.multiple_of((place[1] ^ k) * depth, depth), depth)
        put_chunk(out, [held[j, here, :] for j in range(blocks)])


def last_kernel(*refs):
    *ins, out = refs
    parts = [get_chunk(ref, out.shape[0])[0] for ref in ins]
    for j, terms in enumerate(zip(*parts)):
        out[:, lanes(j)] = sum(terms[1:], terms[0])


def near_kernel(place, patches, own, first, second, out, p_held, held, arrived):
    core = place[2]
    copies = [
        pltpu.make_async_copy(patches, p_held, arrived.at[0]),
        pltpu.make_async_copy(own, held, arrived.at[1]),
    ]
    for copy in copies:
        copy.start()
    copies[0].wait()
    out[1 + core] = times(p_held[...], first[...]).astype(BF16)
    out[2 - core] = times(p_held[...], second[...]).astype(BF16)
    copies[1].wait()
    out[0] = times(p_held[...], held[...]).astype(BF16)


def embed_kernel(place, patches, near, far, out, p_held, arrived):
    me, columns = place[0], near.shape[2]
    copy = pltpu.make_async_copy(patches, p_held, arrived)
    copy.start()

    def put(k, value):
        out[:, pl.ds(pl.multiple_of((me ^ k) * columns, columns), columns)] = value

    for k in range(3):
        put(k, near[k])
    copy.wait()
    put(3, times(p_held[...], far[...]).astype(BF16))


def call(kernel, outs, operands, specs=(), scratch=(), flops=0):
    moved = sum(math.prod(a.shape) * a.dtype.itemsize for a in [*operands, *jax.tree.leaves(outs)]) if flops else 0
    return pl.pallas_call(
        kernel,
        out_shape=outs,
        in_specs=[*specs] + [VMEM] * (len(operands) - len(specs)),
        out_specs=jax.tree.map(lambda _: VMEM, outs),
        scratch_shapes=scratch,
        compiler_params=pltpu.CompilerParams(vmem_limit_bytes=40 * 2**20),
        cost_estimate=pl.CostEstimate(flops=flops, bytes_accessed=moved, transcendentals=0),
    )(*operands)


def tiled_body(patches, grad_embed, weight, straggler, decode, encode):
    count_dp, count_fsdp = lax.axis_size("dp"), lax.axis_size("fsdp")
    dp, me = lax.axis_index("dp"), lax.axis_index("fsdp")
    core = dp % 2
    place = jnp.stack([me, dp // 2, core])
    tokens, features = patches.shape
    columns = weight.shape[1]
    rows, depth, blocks = features // 2, features // count_dp, columns // LANES
    chunk = chunk_shape(rows, columns)
    even = range(0, count_dp, 2)

    def along_planes(block, step, replicas):
        pairs = [(d * 4 + f, d * 4 + (f ^ step(d % 2))) for d in replicas for f in range(4)]
        return lax.ppermute(block, ("dp", "fsdp"), pairs)

    with jax.named_scope("gather_weight"):
        first = along_planes(weight, lambda c: 1 + c, range(count_dp))

    with jax.named_scope("shares"):
        shares = encode * straggler[:, None] * decode[:, None]
        before = lax.ppermute(shares, "dp", [((d - 1) % count_dp, d) for d in even])
    with jax.named_scope("send"):
        sent, left, held = call(
            functools.partial(send_kernel, depth),
            [
                jax.ShapeDtypeStruct((count_fsdp, *chunk), I16),
                jax.ShapeDtypeStruct((rows, tokens), BF16),
                jax.ShapeDtypeStruct((count_fsdp, tokens, columns), BF16),
            ],
            [place, in_hbm(patches), in_hbm(grad_embed), shares],
            [SMEM, HBM, HBM],
            [pltpu.VMEM(patches.shape, BF16), pltpu.SemaphoreType.DMA((count_fsdp + 1,))],
        )
    with jax.named_scope("own"):
        first, left = lax.optimization_barrier((first, left))
        kept = call(
            own_kernel,
            jax.ShapeDtypeStruct((count_fsdp, blocks, rows, LANES), F32),
            [left, held],
            flops=10**11,
        )
    with jax.named_scope("relay_weight"):
        far = along_planes(first, lambda c: 2 - c, range(count_dp))
        second = exchange(first, "dp", 1)
    with jax.named_scope("pair"):
        came = exchange(sent, "dp", 1)
        before_sib = lax.ppermute(before, "dp", [(d, d + 1) for d in even])
        kept, sent = call(
            pair_kernel,
            [
                jax.ShapeDtypeStruct((2, blocks, rows, LANES), F32),
                jax.ShapeDtypeStruct((2, *chunk), I16),
            ],
            [place, jnp.full((1,), tokens * count_fsdp, I32), kept, came, shares, before, before_sib],
            [SMEM] * 2,
            flops=10**11,
        )
    with jax.named_scope("first_step"):
        came = along_planes(sent, lambda c: 1 + c, range(count_dp))
    with jax.named_scope("embed_near"):
        near = call(
            near_kernel,
            jax.ShapeDtypeStruct((3, tokens, columns), BF16),
            [place, in_hbm(patches), in_hbm(weight), first, second],
            [SMEM, HBM, HBM],
            [pltpu.VMEM(patches.shape, BF16), pltpu.VMEM(weight.shape, BF16), pltpu.SemaphoreType.DMA((2,))],
            flops=6 * tokens * features * columns,
        )
    with jax.named_scope("embed"):
        embedded = call(
            embed_kernel,
            jax.ShapeDtypeStruct((tokens, columns * count_fsdp), BF16),
            [place, in_hbm(patches), near, far],
            [SMEM, HBM],
            [pltpu.VMEM(patches.shape, BF16), pltpu.SemaphoreType.DMA],
            flops=2 * tokens * features * columns,
        )
    with jax.named_scope("first_step_sum"):
        embedded, came = lax.optimization_barrier((embedded, came))
        kept, sent = call(
            step_kernel,
            [jax.ShapeDtypeStruct((blocks, rows, LANES), F32), jax.ShapeDtypeStruct(chunk, I16)],
            [kept, came],
        )
    with jax.named_scope("second_step"):
        came = along_planes(sent, lambda c: 2 - c, range(count_dp))
    with jax.named_scope("middle"):
        parts = call(
            functools.partial(middle_kernel, depth),
            [jax.ShapeDtypeStruct(chunk_shape(depth, columns), I16)] * (count_dp // 2),
            [place, kept, came],
            [SMEM],
            [pltpu.VMEM((blocks, rows, LANES), F32)],
        )
        parts = [exchange(part, "dp", 2 * k) if k else part for k, part in enumerate(parts)]
    with jax.named_scope("last"):
        decoded = call(last_kernel, jax.ShapeDtypeStruct((depth, columns), F32), parts)
    return embedded, decoded


def plain_body(patches, grad_embed, weight, straggler, decode, encode):
    shares = (straggler * decode)[:, None] * encode
    factor = (shares[:, 0] + shifted(shares[:, 1], "dp", 1))[0]
    scale = factor.astype(F32) / (patches.shape[0] * lax.axis_size("fsdp"))
    whole = lax.all_gather(weight, "fsdp", axis=1, tiled=True)
    embedded = times(patches, whole).astype(BF16)
    term = scale * times(grad_embed, patches, ((0,), (0,)))
    term = lax.psum_scatter(term, "fsdp", scatter_dimension=0, tiled=True)
    return embedded, lax.psum_scatter(term.T, "dp", scatter_dimension=0, tiled=True)


def body(patches, grad_embed, weight, straggler, decode, encode):
    fits = patches.shape[1] % (16 * lax.axis_size("dp")) == 0 and weight.shape[1] % LANES == 0
    fits = fits and lax.axis_size("fsdp") == 4
    run = tiled_body if fits else plain_body
    return run(patches, grad_embed, weight, straggler, decode, encode)


def solution(mesh):
    return jax.shard_map(
        body,
        mesh=mesh,
        in_specs=(
            P(("dp", "fsdp"), None),
            P(("dp", "fsdp"), None),
            P(None, "fsdp"),
            P("dp"),
            P("dp"),
            P("dp", None),
        ),
        out_specs=(P(("dp", "fsdp"), None), P("dp", "fsdp")),
        check_vma=False,
    )
```

```python
import functools
import math

import jax
import jax.numpy as jnp
from jax import lax
from jax.experimental import pallas as pl
from jax.experimental.pallas import tpu as pltpu
from jax.sharding import PartitionSpec as P

LANES = 128
TAIL = 16
STEP = math.log(2) / 16
TOP = 32760.0
F32, BF16, I16, I32 = jnp.float32, jnp.bfloat16, jnp.int16, jnp.int32
VMEM = pl.BlockSpec(memory_space=pltpu.VMEM)
SMEM = pl.BlockSpec(memory_space=pltpu.SMEM)
HBM = pl.BlockSpec(memory_space=pltpu.HBM)


def in_hbm(array):
    return pltpu.with_memory_space_constraint(array, pltpu.HBM)


def exchange(block, axis, step):
    return lax.ppermute(block, axis, [(i, i ^ step) for i in range(lax.axis_size(axis))])


def shifted(block, axis, distance):
    count = lax.axis_size(axis)
    return lax.ppermute(block, axis, [((i - distance) % count, i) for i in range(count)])


def times(a, b, dims=((1,), (0,))):
    return lax.dot_general(a, b, (dims, ((), ())), preferred_element_type=F32)


def chunk_shape(rows, columns):
    return (columns // LANES * rows + TAIL, LANES)


def put_chunk(ref, blocks, extra=()):
    rows = blocks[0].shape[0]
    tail = jnp.zeros((TAIL, LANES), I32)
    row = lax.broadcasted_iota(I32, (TAIL, LANES), 0)
    for j, block in enumerate(blocks):
        largest = jnp.max(jnp.abs(block), axis=0, keepdims=True)
        power = jnp.ceil(jnp.log(jnp.maximum(largest, 2.0**-100)) * (1 / STEP))
        coded = jnp.round(block * (TOP * jnp.exp(power * -STEP)))
        ref[pl.ds(j * rows, rows), :] = coded.astype(I32).astype(I16)
        tail = jnp.where(row == j, power.astype(I32), tail)
    for j, number in enumerate(extra):
        tail = jnp.where(row == TAIL - len(extra) + j, number, tail)
    ref[pl.ds(len(blocks) * rows, TAIL), :] = tail.astype(I16)


def get_chunk(ref, rows):
    count = (ref.shape[0] - TAIL) // rows
    tail = ref[pl.ds(count * rows, TAIL), :].astype(F32)
    scale = jnp.exp(tail * STEP) * (1 / TOP)
    return [ref[pl.ds(j * rows, rows), :].astype(F32) * scale[j : j + 1, :] for j in range(count)], tail


def lanes(j):
    return slice(j * LANES, (j + 1) * LANES)


def send_kernel(depth, place, patches, grad_embed, shares, sent, left, held, p_held, arrived):
    me, core = place[0], place[2]
    count, _, columns = held.shape
    blocks, features = columns // LANES, patches.shape[1]
    rows = features // 2
    copies = [pltpu.make_async_copy(patches, p_held, arrived.at[count])]
    for k in range(count):
        here = pl.ds(pl.multiple_of((me ^ k) * columns, columns), columns)
        copies.append(pltpu.make_async_copy(grad_embed.at[:, here], held.at[k], arrived.at[k]))
    for copy in copies:
        copy.start()
    extra = shares[:, 0:1], shares[:, 1:2]
    i = lax.broadcasted_iota(I32, (features, features), 0)
    j = lax.broadcasted_iota(I32, (features, features), 1)
    half, i = i // rows, i % rows
    chosen = jnp.where(j == (i // depth * 2 + (core ^ half)) * depth + i % depth, 1.0, 0.0).astype(BF16)
    copies[0].wait()
    turned = times(chosen, p_held[...], ((1,), (1,))).astype(BF16)
    left[...] = turned[:rows]
    for k in range(count):
        copies[1 + k].wait()
        value = times(turned[rows:], held[k])
        put_chunk(sent.at[k], [value[:, lanes(j)] for j in range(blocks)], extra)


def own_kernel(left, held, kept):
    for k in range(kept.shape[0]):
        value = times(left[...], held[k])
        for j in range(kept.shape[1]):
            kept[k, j] = value[:, lanes(j)]


def pair_kernel(place, tokens, kept, came, shares, before, before_sib, still, sent):
    core = place[2]
    _, blocks, rows, _ = kept.shape
    first, second = shares[:, 0:1].astype(F32), shares[:, 1:2].astype(F32)
    tail = get_chunk(came.at[0], rows)[1]
    first_sib, second_sib = (tail[TAIL - 2 + j : TAIL - 1 + j, 0:1] for j in range(2))
    even = core == 0
    carried = jnp.where(even, before[:, 1:2], before_sib[:, 1:2]).astype(F32)
    scale = (first + jnp.where(even, carried, second_sib)) / tokens[0].astype(F32)
    scale_sib = (first_sib + jnp.where(even, second, carried)) / tokens[0].astype(F32)

    def value(k):
        parts, _ = get_chunk(came.at[k], rows)
        return [scale * kept[k, j] + scale_sib * part for j, part in enumerate(parts)]

    put_chunk(sent.at[0], value(1 + core))
    put_chunk(sent.at[1], value(3))
    for at, k in enumerate((0, 2 - core)):
        for j, part in enumerate(value(k)):
            still[at, j] = part


def step_kernel(kept, came, still, sent):
    _, blocks, rows, _ = kept.shape
    parts, _ = get_chunk(came.at[1], rows)
    put_chunk(sent, [kept[1, j] + part for j, part in enumerate(parts)])
    for j, part in enumerate(get_chunk(came.at[0], rows)[0]):
        still[j] = kept[0, j] + part


def middle_kernel(depth, place, kept, came, *refs):
    *outs, held = refs
    blocks, rows, _ = kept.shape
    for j, part in enumerate(get_chunk(came, rows)[0]):
        held[j] = kept[j] + part
    for k, out in enumerate(outs):
        here = pl.ds(pl.multiple_of((place[1] ^ k) * depth, depth), depth)
        put_chunk(out, [held[j, here, :] for j in range(blocks)])


def last_kernel(*refs):
    *ins, out = refs
    parts = [get_chunk(ref, out.shape[0])[0] for ref in ins]
    for j, terms in enumerate(zip(*parts)):
        out[:, lanes(j)] = sum(terms[1:], terms[0])


def near_kernel(place, patches, own, first, second, out, p_held, held, arrived):
    core = place[2]
    copies = [
        pltpu.make_async_copy(patches, p_held, arrived.at[0]),
        pltpu.make_async_copy(own, held, arrived.at[1]),
    ]
    for copy in copies:
        copy.start()
    copies[0].wait()
    out[1 + core] = times(p_held[...], first[...]).astype(BF16)
    out[2 - core] = times(p_held[...], second[...]).astype(BF16)
    copies[1].wait()
    out[0] = times(p_held[...], held[...]).astype(BF16)


def embed_kernel(place, patches, near, far, far_sib, out, p_held, halves, arrived):
    me, core, columns = place[0], place[2], near.shape[2]
    rows = far.shape[0]
    copy = pltpu.make_async_copy(patches, p_held, arrived)
    copy.start()

    def put(k, value):
        out[:, pl.ds(pl.multiple_of((me ^ k) * columns, columns), columns)] = value

    for k in range(3):
        put(k, near[k])
    copy.wait()
    halves[0] = p_held[:, :rows]
    halves[1] = p_held[:, rows:]
    put(3, (times(halves[core], far[...]) + times(halves[1 - core], far_sib[...])).astype(BF16))


def call(kernel, outs, operands, specs=(), scratch=(), flops=0):
    moved = sum(math.prod(a.shape) * a.dtype.itemsize for a in [*operands, *jax.tree.leaves(outs)]) if flops else 0
    return pl.pallas_call(
        kernel,
        out_shape=outs,
        in_specs=[*specs] + [VMEM] * (len(operands) - len(specs)),
        out_specs=jax.tree.map(lambda _: VMEM, outs),
        scratch_shapes=scratch,
        compiler_params=pltpu.CompilerParams(vmem_limit_bytes=40 * 2**20),
        cost_estimate=pl.CostEstimate(flops=flops, bytes_accessed=moved, transcendentals=0),
    )(*operands)


def tiled_body(patches, grad_embed, weight, straggler, decode, encode):
    count_dp, count_fsdp = lax.axis_size("dp"), lax.axis_size("fsdp")
    dp, me = lax.axis_index("dp"), lax.axis_index("fsdp")
    core = dp % 2
    place = jnp.stack([me, dp // 2, core])
    tokens, features = patches.shape
    columns = weight.shape[1]
    rows, depth, blocks = features // 2, features // count_dp, columns // LANES
    chunk = chunk_shape(rows, columns)
    even = range(0, count_dp, 2)

    def along_planes(block, step, replicas):
        pairs = [(d * 4 + f, d * 4 + (f ^ step(d % 2))) for d in replicas for f in range(4)]
        return lax.ppermute(block, ("dp", "fsdp"), pairs)

    with jax.named_scope("gather_weight"):
        first = along_planes(weight, lambda c: 1 + c, range(count_dp))

    with jax.named_scope("shares"):
        shares = encode * straggler[:, None] * decode[:, None]
        before = lax.ppermute(shares, "dp", [((d - 1) % count_dp, d) for d in even])
    with jax.named_scope("send"):
        sent, left, held = call(
            functools.partial(send_kernel, depth),
            [
                jax.ShapeDtypeStruct((count_fsdp, *chunk), I16),
                jax.ShapeDtypeStruct((rows, tokens), BF16),
                jax.ShapeDtypeStruct((count_fsdp, tokens, columns), BF16),
            ],
            [place, in_hbm(patches), in_hbm(grad_embed), shares],
            [SMEM, HBM, HBM],
            [pltpu.VMEM(patches.shape, BF16), pltpu.SemaphoreType.DMA((count_fsdp + 1,))],
        )
    with jax.named_scope("own"):
        first, left = lax.optimization_barrier((first, left))
        kept = call(
            own_kernel,
            jax.ShapeDtypeStruct((count_fsdp, blocks, rows, LANES), F32),
            [left, held],
            flops=10**11,
        )
    with jax.named_scope("relay_weight"):
        second = exchange(first, "dp", 1)
        half = lax.dynamic_slice_in_dim(first, core * rows, rows, 0)
        far = along_planes(half, lambda c: 2 - c, range(count_dp))
    with jax.named_scope("pair"):
        came = exchange(sent, "dp", 1)
        before_sib = lax.ppermute(before, "dp", [(d, d + 1) for d in even])
        kept, sent = call(
            pair_kernel,
            [
                jax.ShapeDtypeStruct((2, blocks, rows, LANES), F32),
                jax.ShapeDtypeStruct((2, *chunk), I16),
            ],
            [place, jnp.full((1,), tokens * count_fsdp, I32), kept, came, shares, before, before_sib],
            [SMEM] * 2,
            flops=10**11,
        )
    with jax.named_scope("first_step"):
        came = along_planes(sent, lambda c: 1 + c, range(count_dp))
    with jax.named_scope("embed_near"):
        far, second = lax.optimization_barrier((far, second))
        near = call(
            near_kernel,
            jax.ShapeDtypeStruct((3, tokens, columns), BF16),
            [place, in_hbm(patches), in_hbm(weight), first, second],
            [SMEM, HBM, HBM],
            [pltpu.VMEM(patches.shape, BF16), pltpu.VMEM(weight.shape, BF16), pltpu.SemaphoreType.DMA((2,))],
            flops=6 * 10**9,
        )
    with jax.named_scope("first_step_sum"):
        near, far, came = lax.optimization_barrier((near, far, came))
        kept, sent = call(
            step_kernel,
            [jax.ShapeDtypeStruct((blocks, rows, LANES), F32), jax.ShapeDtypeStruct(chunk, I16)],
            [kept, came],
        )
    with jax.named_scope("second_step"):
        came = along_planes(sent, lambda c: 2 - c, range(count_dp))
    with jax.named_scope("relay_weight"):
        far, kept = lax.optimization_barrier((far, kept))
        far_sib = exchange(far, "dp", 1)
    with jax.named_scope("embed"):
        embedded = call(
            embed_kernel,
            jax.ShapeDtypeStruct((tokens, columns * count_fsdp), BF16),
            [place, in_hbm(patches), near, far, far_sib],
            [SMEM, HBM],
            [pltpu.VMEM(patches.shape, BF16), pltpu.VMEM((2, tokens, rows), BF16), pltpu.SemaphoreType.DMA],
            flops=2 * tokens * features * columns,
        )
    with jax.named_scope("middle"):
        embedded, came = lax.optimization_barrier((embedded, came))
        parts = call(
            functools.partial(middle_kernel, depth),
            [jax.ShapeDtypeStruct(chunk_shape(depth, columns), I16)] * (count_dp // 2),
            [place, kept, came],
            [SMEM],
            [pltpu.VMEM((blocks, rows, LANES), F32)],
        )
        parts = [exchange(part, "dp", 2 * k) if k else part for k, part in enumerate(parts)]
    with jax.named_scope("last"):
        decoded = call(last_kernel, jax.ShapeDtypeStruct((depth, columns), F32), parts)
    return embedded, decoded


def plain_body(patches, grad_embed, weight, straggler, decode, encode):
    shares = (straggler * decode)[:, None] * encode
    factor = (shares[:, 0] + shifted(shares[:, 1], "dp", 1))[0]
    scale = factor.astype(F32) / (patches.shape[0] * lax.axis_size("fsdp"))
    whole = lax.all_gather(weight, "fsdp", axis=1, tiled=True)
    embedded = times(patches, whole).astype(BF16)
    term = scale * times(grad_embed, patches, ((0,), (0,)))
    term = lax.psum_scatter(term, "fsdp", scatter_dimension=0, tiled=True)
    return embedded, lax.psum_scatter(term.T, "dp", scatter_dimension=0, tiled=True)


def body(patches, grad_embed, weight, straggler, decode, encode):
    fits = patches.shape[1] % (16 * lax.axis_size("dp")) == 0 and weight.shape[1] % LANES == 0
    fits = fits and lax.axis_size("fsdp") == 4
    run = tiled_body if fits else plain_body
    return run(patches, grad_embed, weight, straggler, decode, encode)


def solution(mesh):
    return jax.shard_map(
        body,
        mesh=mesh,
        in_specs=(
            P(("dp", "fsdp"), None),
            P(("dp", "fsdp"), None),
            P(None, "fsdp"),
            P("dp"),
            P("dp"),
            P("dp", None),
        ),
        out_specs=(P(("dp", "fsdp"), None), P("dp", "fsdp")),
        check_vma=False,
    )
```

```python
import functools
import math

import jax
import jax.numpy as jnp
from jax import lax
from jax.experimental import pallas as pl
from jax.experimental.pallas import tpu as pltpu
from jax.sharding import PartitionSpec as P

LANES = 128
TAIL = 16
STEP = math.log(2) / 16
TOP = 32760.0
F32, BF16, I16, I32 = jnp.float32, jnp.bfloat16, jnp.int16, jnp.int32
VMEM = pl.BlockSpec(memory_space=pltpu.VMEM)
SMEM = pl.BlockSpec(memory_space=pltpu.SMEM)
HBM = pl.BlockSpec(memory_space=pltpu.HBM)


def in_hbm(array):
    return pltpu.with_memory_space_constraint(array, pltpu.HBM)


def exchange(block, axis, step):
    return lax.ppermute(block, axis, [(i, i ^ step) for i in range(lax.axis_size(axis))])


def shifted(block, axis, distance):
    count = lax.axis_size(axis)
    return lax.ppermute(block, axis, [((i - distance) % count, i) for i in range(count)])


def times(a, b, dims=((1,), (0,))):
    return lax.dot_general(a, b, (dims, ((), ())), preferred_element_type=F32)


def chunk_shape(rows, columns):
    return (columns // LANES * rows + TAIL, LANES)


def put_chunk(ref, blocks, extra=()):
    rows = blocks[0].shape[0]
    tail = jnp.zeros((TAIL, LANES), I32)
    row = lax.broadcasted_iota(I32, (TAIL, LANES), 0)
    for j, block in enumerate(blocks):
        largest = jnp.max(jnp.abs(block), axis=0, keepdims=True)
        power = jnp.ceil(jnp.log(jnp.maximum(largest, 2.0**-100)) * (1 / STEP))
        coded = block * (TOP * jnp.exp(power * -STEP))
        ref[pl.ds(j * rows, rows), :] = coded.astype(I32).astype(I16)
        tail = jnp.where(row == j, power.astype(I32), tail)
    for j, number in enumerate(extra):
        tail = jnp.where(row == TAIL - len(extra) + j, number, tail)
    ref[pl.ds(len(blocks) * rows, TAIL), :] = tail.astype(I16)


def get_chunk(ref, rows):
    count = (ref.shape[0] - TAIL) // rows
    tail = ref[pl.ds(count * rows, TAIL), :].astype(F32)
    scale = jnp.exp(tail * STEP) * (1 / TOP)
    return [ref[pl.ds(j * rows, rows), :].astype(F32) * scale[j : j + 1, :] for j in range(count)], tail


def lanes(j):
    return slice(j * LANES, (j + 1) * LANES)


def send_kernel(depth, place, patches, grad_embed, shares, sent, left, held, p_held, arrived):
    me, core = place[0], place[2]
    count, _, columns = held.shape
    blocks, features = columns // LANES, patches.shape[1]
    rows = features // 2
    copies = [pltpu.make_async_copy(patches, p_held, arrived.at[count])]
    for k in range(count):
        here = pl.ds(pl.multiple_of((me ^ k) * columns, columns), columns)
        copies.append(pltpu.make_async_copy(grad_embed.at[:, here], held.at[k], arrived.at[k]))
    for copy in copies:
        copy.start()
    extra = shares[:, 0:1], shares[:, 1:2]
    i = lax.broadcasted_iota(I32, (features, features), 0)
    j = lax.broadcasted_iota(I32, (features, features), 1)
    half, i = i // rows, i % rows
    chosen = jnp.where(j == (i // depth * 2 + (core ^ half)) * depth + i % depth, 1.0, 0.0).astype(BF16)
    copies[0].wait()
    turned = times(chosen, p_held[...], ((1,), (1,))).astype(BF16)
    left[...] = turned[:rows]
    for k in range(count):
        copies[1 + k].wait()
        value = times(turned[rows:], held[k])
        put_chunk(sent.at[k], [value[:, lanes(j)] for j in range(blocks)], extra)


def own_kernel(left, held, kept):
    for k in range(kept.shape[0]):
        value = times(left[...], held[k])
        for j in range(kept.shape[1]):
            kept[k, j] = value[:, lanes(j)]


def pair_kernel(place, tokens, kept, came, shares, before, before_sib, still, sent):
    core = place[2]
    _, blocks, rows, _ = kept.shape
    first, second = shares[:, 0:1].astype(F32), shares[:, 1:2].astype(F32)
    tail = get_chunk(came.at[0], rows)[1]
    first_sib, second_sib = (tail[TAIL - 2 + j : TAIL - 1 + j, 0:1] for j in range(2))
    even = core == 0
    carried = jnp.where(even, before[:, 1:2], before_sib[:, 1:2]).astype(F32)
    scale = (first + jnp.where(even, carried, second_sib)) / tokens[0].astype(F32)
    scale_sib = (first_sib + jnp.where(even, second, carried)) / tokens[0].astype(F32)

    def value(k):
        parts, _ = get_chunk(came.at[k], rows)
        return [scale * kept[k, j] + scale_sib * part for j, part in enumerate(parts)]

    put_chunk(sent.at[0], value(1 + core))
    put_chunk(sent.at[1], value(3))
    for at, k in enumerate((0, 2 - core)):
        for j, part in enumerate(value(k)):
            still[at, j] = part


def step_kernel(kept, came, still, sent):
    _, blocks, rows, _ = kept.shape
    parts, _ = get_chunk(came.at[1], rows)
    put_chunk(sent, [kept[1, j] + part for j, part in enumerate(parts)])
    for j, part in enumerate(get_chunk(came.at[0], rows)[0]):
        still[j] = kept[0, j] + part


def middle_kernel(depth, place, kept, came, *refs):
    *outs, held = refs
    blocks, rows, _ = kept.shape
    for j, part in enumerate(get_chunk(came, rows)[0]):
        held[j] = kept[j] + part
    for k, out in enumerate(outs):
        here = pl.ds(pl.multiple_of((place[1] ^ k) * depth, depth), depth)
        put_chunk(out, [held[j, here, :] for j in range(blocks)])


def last_kernel(*refs):
    *ins, out = refs
    parts = [get_chunk(ref, out.shape[0])[0] for ref in ins]
    for j, terms in enumerate(zip(*parts)):
        out[:, lanes(j)] = sum(terms[1:], terms[0])


def half_kernel(place, first, half, arrived):
    rows = half.shape[0]
    copy = pltpu.make_async_copy(first.at[pl.ds(pl.multiple_of(place[2] * rows, rows), rows)], half, arrived)
    copy.start()
    copy.wait()


def near_kernel(place, patches, own, first, second, out, p_held, held, arrived):
    core = place[2]
    copies = [
        pltpu.make_async_copy(patches, p_held, arrived.at[0]),
        pltpu.make_async_copy(own, held, arrived.at[1]),
    ]
    for copy in copies:
        copy.start()
    copies[0].wait()
    out[1 + core] = times(p_held[...], first[...]).astype(BF16)
    out[2 - core] = times(p_held[...], second[...]).astype(BF16)
    copies[1].wait()
    out[0] = times(p_held[...], held[...]).astype(BF16)


def embed_kernel(place, patches, near, far, far_sib, out, p_held, halves, arrived):
    me, core, columns = place[0], place[2], near.shape[2]
    rows = far.shape[0]
    copy = pltpu.make_async_copy(patches, p_held, arrived)
    copy.start()

    def put(k, value):
        out[:, pl.ds(pl.multiple_of((me ^ k) * columns, columns), columns)] = value

    for k in range(3):
        put(k, near[k])
    copy.wait()
    halves[0] = p_held[:, :rows]
    halves[1] = p_held[:, rows:]
    put(3, (times(halves[core], far[...]) + times(halves[1 - core], far_sib[...])).astype(BF16))


def call(kernel, outs, operands, specs=(), scratch=(), flops=0):
    moved = sum(math.prod(a.shape) * a.dtype.itemsize for a in [*operands, *jax.tree.leaves(outs)]) if flops else 0
    return pl.pallas_call(
        kernel,
        out_shape=outs,
        in_specs=[*specs] + [VMEM] * (len(operands) - len(specs)),
        out_specs=jax.tree.map(lambda _: VMEM, outs),
        scratch_shapes=scratch,
        compiler_params=pltpu.CompilerParams(vmem_limit_bytes=24 * 2**20),
        cost_estimate=pl.CostEstimate(flops=flops, bytes_accessed=moved, transcendentals=0),
    )(*operands)


def tiled_body(patches, grad_embed, weight, straggler, decode, encode):
    count_dp, count_fsdp = lax.axis_size("dp"), lax.axis_size("fsdp")
    dp, me = lax.axis_index("dp"), lax.axis_index("fsdp")
    core = dp % 2
    place = jnp.stack([me, dp // 2, core])
    tokens, features = patches.shape
    columns = weight.shape[1]
    rows, depth, blocks = features // 2, features // count_dp, columns // LANES
    chunk = chunk_shape(rows, columns)

    def along_planes(block, step, replicas):
        pairs = [(d * 4 + f, d * 4 + (f ^ step(d % 2))) for d in replicas for f in range(4)]
        return lax.ppermute(block, ("dp", "fsdp"), pairs)

    with jax.named_scope("gather_weight"):
        first = along_planes(weight, lambda c: 1 + c, range(count_dp))

    with jax.named_scope("shares"):
        shares = encode * straggler[:, None] * decode[:, None]
        before = shifted(shares, "dp", 1)
    with jax.named_scope("send"):
        sent, left, held = call(
            functools.partial(send_kernel, depth),
            [
                jax.ShapeDtypeStruct((count_fsdp, *chunk), I16),
                jax.ShapeDtypeStruct((rows, tokens), BF16),
                jax.ShapeDtypeStruct((count_fsdp, tokens, columns), BF16),
            ],
            [place, in_hbm(patches), in_hbm(grad_embed), shares],
            [SMEM, HBM, HBM],
            [pltpu.VMEM(patches.shape, BF16), pltpu.SemaphoreType.DMA((count_fsdp + 1,))],
        )
    with jax.named_scope("own"):
        first, left = lax.optimization_barrier((first, left))
        kept = call(
            own_kernel,
            jax.ShapeDtypeStruct((count_fsdp, blocks, rows, LANES), F32),
            [left, held],
            flops=10**11,
        )
    with jax.named_scope("relay_weight"):
        second = exchange(first, "dp", 1)
        half = call(
            half_kernel,
            jax.ShapeDtypeStruct((rows, columns), BF16),
            [place, first],
            [SMEM, pl.BlockSpec(memory_space=pl.ANY)],
            [pltpu.SemaphoreType.DMA],
        )
        far = along_planes(half, lambda c: 2 - c, range(count_dp))
    with jax.named_scope("pair"):
        came = exchange(sent, "dp", 1)
        before_sib = exchange(before, "dp", 1)
        kept, sent = call(
            pair_kernel,
            [
                jax.ShapeDtypeStruct((2, blocks, rows, LANES), F32),
                jax.ShapeDtypeStruct((2, *chunk), I16),
            ],
            [place, jnp.full((1,), tokens * count_fsdp, I32), kept, came, shares, before, before_sib],
            [SMEM] * 2,
            flops=10**11,
        )
    with jax.named_scope("first_step"):
        came = along_planes(sent, lambda c: 1 + c, range(count_dp))
    with jax.named_scope("embed_near"):
        far, second = lax.optimization_barrier((far, second))
        near = call(
            near_kernel,
            jax.ShapeDtypeStruct((3, tokens, columns), BF16),
            [place, in_hbm(patches), in_hbm(weight), first, second],
            [SMEM, HBM, HBM],
            [pltpu.VMEM(patches.shape, BF16), pltpu.VMEM(weight.shape, BF16), pltpu.SemaphoreType.DMA((2,))],
            flops=6 * 10**9,
        )
    with jax.named_scope("first_step_sum"):
        near, far, came = lax.optimization_barrier((near, far, came))
        kept, sent = call(
            step_kernel,
            [jax.ShapeDtypeStruct((blocks, rows, LANES), F32), jax.ShapeDtypeStruct(chunk, I16)],
            [kept, came],
        )
    with jax.named_scope("second_step"):
        came = along_planes(sent, lambda c: 2 - c, range(count_dp))
    with jax.named_scope("relay_weight"):
        far, kept = lax.optimization_barrier((far, kept))
        far_sib = exchange(far, "dp", 1)
    with jax.named_scope("embed"):
        embedded = call(
            embed_kernel,
            jax.ShapeDtypeStruct((tokens, columns * count_fsdp), BF16),
            [place, in_hbm(patches), near, far, far_sib],
            [SMEM, HBM],
            [pltpu.VMEM(patches.shape, BF16), pltpu.VMEM((2, tokens, rows), BF16), pltpu.SemaphoreType.DMA],
            flops=2 * tokens * features * columns,
        )
    with jax.named_scope("middle"):
        embedded, came = lax.optimization_barrier((embedded, came))
        parts = call(
            functools.partial(middle_kernel, depth),
            [jax.ShapeDtypeStruct(chunk_shape(depth, columns), I16)] * (count_dp // 2),
            [place, kept, came],
            [SMEM],
            [pltpu.VMEM((blocks, rows, LANES), F32)],
        )
        parts = [exchange(part, "dp", 2 * k) if k else part for k, part in enumerate(parts)]
    with jax.named_scope("last"):
        decoded = call(last_kernel, jax.ShapeDtypeStruct((depth, columns), F32), parts)
    return embedded, decoded


def plain_body(patches, grad_embed, weight, straggler, decode, encode):
    shares = (straggler * decode)[:, None] * encode
    factor = (shares[:, 0] + shifted(shares[:, 1], "dp", 1))[0]
    scale = factor.astype(F32) / (patches.shape[0] * lax.axis_size("fsdp"))
    whole = lax.all_gather(weight, "fsdp", axis=1, tiled=True)
    embedded = times(patches, whole).astype(BF16)
    term = scale * times(grad_embed, patches, ((0,), (0,)))
    term = lax.psum_scatter(term, "fsdp", scatter_dimension=0, tiled=True)
    return embedded, lax.psum_scatter(term.T, "dp", scatter_dimension=0, tiled=True)


def body(patches, grad_embed, weight, straggler, decode, encode):
    fits = patches.shape[1] % (16 * lax.axis_size("dp")) == 0 and weight.shape[1] % LANES == 0
    fits = fits and lax.axis_size("fsdp") == 4
    run = tiled_body if fits else plain_body
    return run(patches, grad_embed, weight, straggler, decode, encode)


def solution(mesh):
    return jax.shard_map(
        body,
        mesh=mesh,
        in_specs=(
            P(("dp", "fsdp"), None),
            P(("dp", "fsdp"), None),
            P(None, "fsdp"),
            P("dp"),
            P("dp"),
            P("dp", None),
        ),
        out_specs=(P(("dp", "fsdp"), None), P("dp", "fsdp")),
        check_vma=False,
    )
```

```python
import functools
import math

import jax
import jax.numpy as jnp
from jax import lax
from jax.experimental import pallas as pl
from jax.experimental.pallas import tpu as pltpu
from jax.sharding import PartitionSpec as P

LANES = 128
TAIL = 16
STEP = math.log(2) / 16
TOP = 32760.0
F32, BF16, I16, I32 = jnp.float32, jnp.bfloat16, jnp.int16, jnp.int32
VMEM = pl.BlockSpec(memory_space=pltpu.VMEM)
SMEM = pl.BlockSpec(memory_space=pltpu.SMEM)
HBM = pl.BlockSpec(memory_space=pltpu.HBM)


def in_hbm(array):
    return pltpu.with_memory_space_constraint(array, pltpu.HBM)


def exchange(block, axis, step):
    return lax.ppermute(block, axis, [(i, i ^ step) for i in range(lax.axis_size(axis))])


def shifted(block, axis, distance):
    count = lax.axis_size(axis)
    return lax.ppermute(block, axis, [((i - distance) % count, i) for i in range(count)])


def times(a, b, dims=((1,), (0,))):
    return lax.dot_general(a, b, (dims, ((), ())), preferred_element_type=F32)


def chunk_shape(rows, columns):
    return (columns // LANES * rows + TAIL, LANES)


def put_chunk(ref, blocks, extra=()):
    rows = blocks[0].shape[0]
    tail = jnp.zeros((TAIL, LANES), I32)
    row = lax.broadcasted_iota(I32, (TAIL, LANES), 0)
    for j, block in enumerate(blocks):
        largest = jnp.max(jnp.abs(block), axis=0, keepdims=True)
        power = jnp.ceil(jnp.log(jnp.maximum(largest, 2.0**-100)) * (1 / STEP))
        coded = block * (TOP * jnp.exp(power * -STEP))
        ref[pl.ds(j * rows, rows), :] = coded.astype(I32).astype(I16)
        tail = jnp.where(row == j, power.astype(I32), tail)
    for j, number in enumerate(extra):
        tail = jnp.where(row == TAIL - len(extra) + j, number, tail)
    ref[pl.ds(len(blocks) * rows, TAIL), :] = tail.astype(I16)


def get_chunk(ref, rows):
    count = (ref.shape[0] - TAIL) // rows
    tail = ref[pl.ds(count * rows, TAIL), :].astype(F32)
    scale = jnp.exp(tail * STEP) * (1 / TOP)
    return [ref[pl.ds(j * rows, rows), :].astype(F32) * scale[j : j + 1, :] for j in range(count)], tail


def lanes(j):
    return slice(j * LANES, (j + 1) * LANES)


def send_kernel(depth, place, patches, grad_embed, shares, sent, left, held, p_held, arrived):
    me, core = place[0], place[2]
    count, _, columns = held.shape
    blocks, features = columns // LANES, patches.shape[1]
    rows = features // 2
    copies = [pltpu.make_async_copy(patches, p_held, arrived.at[count])]
    for k in range(count):
        here = pl.ds(pl.multiple_of((me ^ k) * columns, columns), columns)
        copies.append(pltpu.make_async_copy(grad_embed.at[:, here], held.at[k], arrived.at[k]))
    for copy in copies:
        copy.start()
    extra = shares[:, 0:1], shares[:, 1:2]
    i = lax.broadcasted_iota(I32, (features, features), 0)
    j = lax.broadcasted_iota(I32, (features, features), 1)
    half, i = i // rows, i % rows
    chosen = jnp.where(j == (i // depth * 2 + (core ^ half)) * depth + i % depth, 1.0, 0.0).astype(BF16)
    copies[0].wait()
    turned = times(chosen, p_held[...], ((1,), (1,))).astype(BF16)
    left[...] = turned[:rows]
    for k in range(count):
        copies[1 + k].wait()
        value = times(turned[rows:], held[k])
        put_chunk(sent.at[k], [value[:, lanes(j)] for j in range(blocks)], extra)


def own_kernel(left, held, kept):
    for k in range(kept.shape[0]):
        value = times(left[...], held[k])
        for j in range(kept.shape[1]):
            kept[k, j] = value[:, lanes(j)]


def pair_kernel(bounds, place, tokens, kept, came, shares, before, before_sib, *outs):
    core = place[2]
    rows = kept.shape[2]
    first, second = shares[:, 0:1].astype(F32), shares[:, 1:2].astype(F32)
    tail = get_chunk(came.at[0], rows)[1]
    first_sib, second_sib = (tail[TAIL - 2 + j : TAIL - 1 + j, 0:1] for j in range(2))
    even = core == 0
    carried = jnp.where(even, before[:, 1:2], before_sib[:, 1:2]).astype(F32)
    scale = (first + jnp.where(even, carried, second_sib)) / tokens[0].astype(F32)
    scale_sib = (first_sib + jnp.where(even, second, carried)) / tokens[0].astype(F32)
    for (lo, hi), still, sent in zip(bounds, outs[::2], outs[1::2]):

        def value(k):
            parts, _ = get_chunk(came.at[k], rows)
            return [scale * kept[k, j] + scale_sib * parts[j] for j in range(lo, hi)]

        put_chunk(sent.at[0], value(1 + core))
        put_chunk(sent.at[1], value(3))
        for at, k in enumerate((0, 2 - core)):
            for j, part in enumerate(value(k)):
                still[at, j] = part


def step_kernel(kept, came, still, sent):
    _, blocks, rows, _ = kept.shape
    parts, _ = get_chunk(came.at[1], rows)
    put_chunk(sent, [kept[1, j] + part for j, part in enumerate(parts)])
    for j, part in enumerate(get_chunk(came.at[0], rows)[0]):
        still[j] = kept[0, j] + part


def middle_kernel(depth, place, kept, came, *refs):
    *outs, held = refs
    blocks, rows, _ = kept.shape
    for j, part in enumerate(get_chunk(came, rows)[0]):
        held[j] = kept[j] + part
    for k, out in enumerate(outs):
        here = pl.ds(pl.multiple_of((place[1] ^ k) * depth, depth), depth)
        put_chunk(out, [held[j, here, :] for j in range(blocks)])


def last_kernel(bounds, *refs):
    *ins, out = refs
    count = len(ins) // len(bounds)
    for i, (lo, _) in enumerate(bounds):
        parts = [get_chunk(ref, out.shape[0])[0] for ref in ins[i * count : (i + 1) * count]]
        for j, terms in enumerate(zip(*parts)):
            out[:, lanes(lo + j)] = sum(terms[1:], terms[0])


def half_kernel(place, first, half):
    rows = half.shape[0]
    half[...] = first[pl.ds(pl.multiple_of(place[2] * rows, rows), rows), :]


def near_kernel(place, patches, own, first, second, out, p_held, held, made, arrived, left):
    me, core, columns = place[0], place[2], own.shape[1]
    copies = [
        pltpu.make_async_copy(patches, p_held, arrived.at[0]),
        pltpu.make_async_copy(own, held, arrived.at[1]),
    ]
    for copy in copies:
        copy.start()
    copies[0].wait()
    sends = []
    for k, (step, weight) in enumerate(((1 + core, first), (2 - core, second), (0, held))):
        if k == 2:
            copies[1].wait()
        made[k] = times(p_held[...], weight[...]).astype(BF16)
        here = pl.ds(pl.multiple_of((me ^ step) * columns, columns), columns)
        sends.append(pltpu.make_async_copy(made.at[k], out.at[:, here], left.at[k]))
        sends[-1].start()
    for send in sends:
        send.wait()


def diagonal_kernel(place, patches, far, far_sib, begun, out, p_held, halves, made, arrived, left):
    me, core, rows, columns = place[0], place[2], far.shape[0], far.shape[1]
    copy = pltpu.make_async_copy(patches, p_held, arrived)
    copy.start()
    copy.wait()
    halves[0] = p_held[:, :rows]
    halves[1] = p_held[:, rows:]
    made[...] = (times(halves[core], far[...]) + times(halves[1 - core], far_sib[...])).astype(BF16)
    here = pl.ds(pl.multiple_of((me ^ 3) * columns, columns), columns)
    send = pltpu.make_async_copy(made, out.at[:, here], left)
    send.start()
    send.wait()


def call(kernel, outs, operands, specs=(), scratch=(), flops=0, out_spec=VMEM, aliases={}):
    moved = sum(math.prod(a.shape) * a.dtype.itemsize for a in [*operands, *jax.tree.leaves(outs)]) if flops else 0
    return pl.pallas_call(
        kernel,
        out_shape=outs,
        in_specs=[*specs] + [VMEM] * (len(operands) - len(specs)),
        out_specs=jax.tree.map(lambda _: out_spec, outs),
        scratch_shapes=scratch,
        input_output_aliases=aliases,
        compiler_params=pltpu.CompilerParams(vmem_limit_bytes=24 * 2**20),
        cost_estimate=pl.CostEstimate(flops=flops, bytes_accessed=moved, transcendentals=0),
    )(*operands)


def tiled_body(patches, grad_embed, weight, straggler, decode, encode):
    count_dp, count_fsdp = lax.axis_size("dp"), lax.axis_size("fsdp")
    dp, me = lax.axis_index("dp"), lax.axis_index("fsdp")
    core = dp % 2
    place = jnp.stack([me, dp // 2, core])
    tokens, features = patches.shape
    columns = weight.shape[1]
    rows, depth, blocks = features // 2, features // count_dp, columns // LANES
    chunk = chunk_shape(rows, columns)
    bounds = [(0, blocks // 2), (blocks // 2, blocks)]

    def along_planes(block, step, replicas):
        pairs = [(d * 4 + f, d * 4 + (f ^ step(d % 2))) for d in replicas for f in range(4)]
        return lax.ppermute(block, ("dp", "fsdp"), pairs)

    with jax.named_scope("gather_weight"):
        first = along_planes(weight, lambda c: 1 + c, range(count_dp))

    with jax.named_scope("shares"):
        shares = encode * straggler[:, None] * decode[:, None]
        before = shifted(shares, "dp", 1)
    with jax.named_scope("send"):
        sent, left, held = call(
            functools.partial(send_kernel, depth),
            [
                jax.ShapeDtypeStruct((count_fsdp, *chunk), I16),
                jax.ShapeDtypeStruct((rows, tokens), BF16),
                jax.ShapeDtypeStruct((count_fsdp, tokens, columns), BF16),
            ],
            [place, in_hbm(patches), in_hbm(grad_embed), shares],
            [SMEM, HBM, HBM],
            [pltpu.VMEM(patches.shape, BF16), pltpu.SemaphoreType.DMA((count_fsdp + 1,))],
        )
    with jax.named_scope("own"):
        first, left = lax.optimization_barrier((first, left))
        kept = call(
            own_kernel,
            jax.ShapeDtypeStruct((count_fsdp, blocks, rows, LANES), F32),
            [left, held],
            flops=10**11,
        )
    with jax.named_scope("relay_weight"):
        second = exchange(first, "dp", 1)
        half = call(
            half_kernel,
            jax.ShapeDtypeStruct((rows, columns), BF16),
            [place, first],
            [SMEM],
        )
        far = along_planes(half, lambda c: 2 - c, range(count_dp))
    with jax.named_scope("pair"):
        came = exchange(sent, "dp", 1)
        before_sib = exchange(before, "dp", 1)
        outs = call(
            functools.partial(pair_kernel, bounds),
            [
                shape
                for lo, hi in bounds
                for shape in (
                    jax.ShapeDtypeStruct((2, hi - lo, rows, LANES), F32),
                    jax.ShapeDtypeStruct((2, *chunk_shape(rows, (hi - lo) * LANES)), I16),
                )
            ],
            [place, jnp.full((1,), tokens * count_fsdp, I32), kept, came, shares, before, before_sib],
            [SMEM] * 2,
            flops=10**11,
        )
        kept_parts = list(outs[::2])
        came_parts = [along_planes(sent, lambda c: 1 + c, range(count_dp)) for sent in outs[1::2]]
    with jax.named_scope("embed_near"):
        far, second = lax.optimization_barrier((far, second))
        near = call(
            near_kernel,
            jax.ShapeDtypeStruct((tokens, columns * count_fsdp), BF16),
            [place, in_hbm(patches), in_hbm(weight), first, second],
            [SMEM, HBM, HBM],
            [
                pltpu.VMEM(patches.shape, BF16),
                pltpu.VMEM(weight.shape, BF16),
                pltpu.VMEM((3, tokens, columns), BF16),
                pltpu.SemaphoreType.DMA((2,)),
                pltpu.SemaphoreType.DMA((3,)),
            ],
            flops=2 * 10**9,
            out_spec=HBM,
        )
        near, came_parts[0] = lax.optimization_barrier((near, came_parts[0]))
    with jax.named_scope("steps"):
        for i, (lo, hi) in enumerate(bounds):
            kept_parts[i], sent = call(
                step_kernel,
                [
                    jax.ShapeDtypeStruct((hi - lo, rows, LANES), F32),
                    jax.ShapeDtypeStruct(chunk_shape(rows, (hi - lo) * LANES), I16),
                ],
                [kept_parts[i], came_parts[i]],
                flops=(0, 10**10)[i],
            )
            came_parts[i] = along_planes(sent, lambda c: 2 - c, range(count_dp))
    with jax.named_scope("embed_diagonal"):
        far, kept_parts[1] = lax.optimization_barrier((far, kept_parts[1]))
        far_sib = exchange(far, "dp", 1)
        embedded = call(
            diagonal_kernel,
            jax.ShapeDtypeStruct((tokens, columns * count_fsdp), BF16),
            [place, in_hbm(patches), far, far_sib, near],
            [SMEM, HBM, VMEM, VMEM, HBM],
            [
                pltpu.VMEM(patches.shape, BF16),
                pltpu.VMEM((2, tokens, rows), BF16),
                pltpu.VMEM((tokens, columns), BF16),
                pltpu.SemaphoreType.DMA,
                pltpu.SemaphoreType.DMA,
            ],
            flops=2 * tokens * features * columns,
            out_spec=HBM,
            aliases={4: 0},
        )
        embedded, came_parts[1] = lax.optimization_barrier((embedded, came_parts[1]))
    with jax.named_scope("middle"):
        sums = []
        for i, (lo, hi) in enumerate(bounds):
            if i:
                came_parts[i], sums[1] = lax.optimization_barrier((came_parts[i], sums[1]))
            parts = call(
                functools.partial(middle_kernel, depth),
                [jax.ShapeDtypeStruct(chunk_shape(depth, (hi - lo) * LANES), I16)] * (count_dp // 2),
                [place, kept_parts[i], came_parts[i]],
                [SMEM],
                [pltpu.VMEM((hi - lo, rows, LANES), F32)],
                flops=10**10,
            )
            sums += [exchange(part, "dp", 2 * k) if k else part for k, part in enumerate(parts)]
    with jax.named_scope("last"):
        decoded = call(
            functools.partial(last_kernel, bounds), jax.ShapeDtypeStruct((depth, columns), F32), sums
        )
    return embedded, decoded


def plain_body(patches, grad_embed, weight, straggler, decode, encode):
    shares = (straggler * decode)[:, None] * encode
    factor = (shares[:, 0] + shifted(shares[:, 1], "dp", 1))[0]
    scale = factor.astype(F32) / (patches.shape[0] * lax.axis_size("fsdp"))
    whole = lax.all_gather(weight, "fsdp", axis=1, tiled=True)
    embedded = times(patches, whole).astype(BF16)
    term = scale * times(grad_embed, patches, ((0,), (0,)))
    term = lax.psum_scatter(term, "fsdp", scatter_dimension=0, tiled=True)
    return embedded, lax.psum_scatter(term.T, "dp", scatter_dimension=0, tiled=True)


def body(patches, grad_embed, weight, straggler, decode, encode):
    fits = patches.shape[1] % (16 * lax.axis_size("dp")) == 0 and weight.shape[1] % LANES == 0
    fits = fits and lax.axis_size("fsdp") == 4
    run = tiled_body if fits else plain_body
    return run(patches, grad_embed, weight, straggler, decode, encode)


def solution(mesh):
    return jax.shard_map(
        body,
        mesh=mesh,
        in_specs=(
            P(("dp", "fsdp"), None),
            P(("dp", "fsdp"), None),
            P(None, "fsdp"),
            P("dp"),
            P("dp"),
            P("dp", None),
        ),
        out_specs=(P(("dp", "fsdp"), None), P("dp", "fsdp")),
        check_vma=False,
    )
```

```python
import functools
import math

import jax
import jax.numpy as jnp
from jax import lax
from jax.experimental import pallas as pl
from jax.experimental.pallas import tpu as pltpu
from jax.sharding import PartitionSpec as P

LANES = 128
TAIL = 16
STEP = math.log(2) / 16
TOP = 32760.0
F32, BF16, I16, I32 = jnp.float32, jnp.bfloat16, jnp.int16, jnp.int32
VMEM = pl.BlockSpec(memory_space=pltpu.VMEM)
SMEM = pl.BlockSpec(memory_space=pltpu.SMEM)
HBM = pl.BlockSpec(memory_space=pltpu.HBM)


def in_hbm(array):
    return pltpu.with_memory_space_constraint(array, pltpu.HBM)


def exchange(block, axis, step):
    return lax.ppermute(block, axis, [(i, i ^ step) for i in range(lax.axis_size(axis))])


def shifted(block, axis, distance):
    count = lax.axis_size(axis)
    return lax.ppermute(block, axis, [((i - distance) % count, i) for i in range(count)])


def times(a, b, dims=((1,), (0,))):
    return lax.dot_general(a, b, (dims, ((), ())), preferred_element_type=F32)


def chunk_shape(rows, columns):
    return (columns // LANES * rows + TAIL, LANES)


def put_chunk(ref, blocks, extra=()):
    rows = blocks[0].shape[0]
    tail = jnp.zeros((TAIL, LANES), I32)
    row = lax.broadcasted_iota(I32, (TAIL, LANES), 0)
    for j, block in enumerate(blocks):
        largest = jnp.max(jnp.abs(block), axis=0, keepdims=True)
        power = jnp.ceil(jnp.log(jnp.maximum(largest, 2.0**-100)) * (1 / STEP))
        coded = block * (TOP * jnp.exp(power * -STEP))
        ref[pl.ds(j * rows, rows), :] = coded.astype(I32).astype(I16)
        tail = jnp.where(row == j, power.astype(I32), tail)
    for j, number in enumerate(extra):
        tail = jnp.where(row == TAIL - len(extra) + j, number, tail)
    ref[pl.ds(len(blocks) * rows, TAIL), :] = tail.astype(I16)


def get_chunk(ref, rows):
    count = (ref.shape[0] - TAIL) // rows
    tail = ref[pl.ds(count * rows, TAIL), :].astype(F32)
    scale = jnp.exp(tail * STEP) * (1 / TOP)
    return [ref[pl.ds(j * rows, rows), :].astype(F32) * scale[j : j + 1, :] for j in range(count)], tail


def lanes(j):
    return slice(j * LANES, (j + 1) * LANES)


def send_kernel(depth, place, patches, grad_embed, shares, sent, left, held, p_held, arrived):
    me, core = place[0], place[2]
    count, _, columns = held.shape
    blocks, features = columns // LANES, patches.shape[1]
    rows = features // 2
    copies = [pltpu.make_async_copy(patches, p_held, arrived.at[count])]
    for k in range(count):
        here = pl.ds(pl.multiple_of((me ^ k) * columns, columns), columns)
        copies.append(pltpu.make_async_copy(grad_embed.at[:, here], held.at[k], arrived.at[k]))
    for copy in copies:
        copy.start()
    extra = shares[:, 0:1], shares[:, 1:2]
    i = lax.broadcasted_iota(I32, (features, features), 0)
    j = lax.broadcasted_iota(I32, (features, features), 1)
    half, i = i // rows, i % rows
    chosen = jnp.where(j == (i // depth * 2 + (core ^ half)) * depth + i % depth, 1.0, 0.0).astype(BF16)
    copies[0].wait()
    turned = times(chosen, p_held[...], ((1,), (1,))).astype(BF16)
    left[...] = turned[:rows]
    for k in range(count):
        copies[1 + k].wait()
        value = times(turned[rows:], held[k])
        put_chunk(sent.at[k], [value[:, lanes(j)] for j in range(blocks)], extra)


def own_kernel(left, held, kept):
    for k in range(kept.shape[0]):
        value = times(left[...], held[k])
        for j in range(kept.shape[1]):
            kept[k, j] = value[:, lanes(j)]


def pair_kernel(place, tokens, kept, came, shares, before, before_sib, still, sent):
    core = place[2]
    _, blocks, rows, _ = kept.shape
    first, second = shares[:, 0:1].astype(F32), shares[:, 1:2].astype(F32)
    tail = get_chunk(came.at[0], rows)[1]
    first_sib, second_sib = (tail[TAIL - 2 + j : TAIL - 1 + j, 0:1] for j in range(2))
    even = core == 0
    carried = jnp.where(even, before[:, 1:2], before_sib[:, 1:2]).astype(F32)
    scale = (first + jnp.where(even, carried, second_sib)) / tokens[0].astype(F32)
    scale_sib = (first_sib + jnp.where(even, second, carried)) / tokens[0].astype(F32)

    def value(k):
        parts, _ = get_chunk(came.at[k], rows)
        return [scale * kept[k, j] + scale_sib * part for j, part in enumerate(parts)]

    put_chunk(sent.at[0], value(1 + core))
    put_chunk(sent.at[1], value(3))
    for at, k in enumerate((0, 2 - core)):
        for j, part in enumerate(value(k)):
            still[at, j] = part


def step_kernel(kept, came, still, sent):
    _, blocks, rows, _ = kept.shape
    parts, _ = get_chunk(came.at[1], rows)
    put_chunk(sent, [kept[1, j] + part for j, part in enumerate(parts)])
    for j, part in enumerate(get_chunk(came.at[0], rows)[0]):
        still[j] = kept[0, j] + part


def middle_kernel(depth, place, kept, came, *refs):
    *outs, held = refs
    blocks, rows, _ = kept.shape
    for j, part in enumerate(get_chunk(came, rows)[0]):
        held[j] = kept[j] + part
    for k, out in enumerate(outs):
        here = pl.ds(pl.multiple_of((place[1] ^ k) * depth, depth), depth)
        put_chunk(out, [held[j, here, :] for j in range(blocks)])


def last_kernel(*refs):
    *ins, out = refs
    parts = [get_chunk(ref, out.shape[0])[0] for ref in ins]
    for j, terms in enumerate(zip(*parts)):
        out[:, lanes(j)] = sum(terms[1:], terms[0])


def half_kernel(place, first, half):
    rows = half.shape[0]
    half[...] = first[pl.ds(pl.multiple_of(place[2] * rows, rows), rows), :]


def near_kernel(place, patches, own, first, second, out, p_held, held, arrived):
    core = place[2]
    copies = [
        pltpu.make_async_copy(patches, p_held, arrived.at[0]),
        pltpu.make_async_copy(own, held, arrived.at[1]),
    ]
    for copy in copies:
        copy.start()
    copies[0].wait()
    out[1 + core] = times(p_held[...], first[...]).astype(BF16)
    out[2 - core] = times(p_held[...], second[...]).astype(BF16)
    copies[1].wait()
    out[0] = times(p_held[...], held[...]).astype(BF16)


def embed_kernel(place, patches, near, far, far_sib, out, p_held, halves, arrived):
    me, core, columns = place[0], place[2], near.shape[2]
    rows = far.shape[0]
    copy = pltpu.make_async_copy(patches, p_held, arrived)
    copy.start()

    def put(k, value):
        out[:, pl.ds(pl.multiple_of((me ^ k) * columns, columns), columns)] = value

    for k in range(3):
        put(k, near[k])
    copy.wait()
    halves[0] = p_held[:, :rows]
    halves[1] = p_held[:, rows:]
    put(3, (times(halves[core], far[...]) + times(halves[1 - core], far_sib[...])).astype(BF16))


def call(kernel, outs, operands, specs=(), scratch=(), flops=0):
    moved = sum(math.prod(a.shape) * a.dtype.itemsize for a in [*operands, *jax.tree.leaves(outs)]) if flops else 0
    return pl.pallas_call(
        kernel,
        out_shape=outs,
        in_specs=[*specs] + [VMEM] * (len(operands) - len(specs)),
        out_specs=jax.tree.map(lambda _: VMEM, outs),
        scratch_shapes=scratch,
        compiler_params=pltpu.CompilerParams(vmem_limit_bytes=24 * 2**20),
        cost_estimate=pl.CostEstimate(flops=flops, bytes_accessed=moved, transcendentals=0),
    )(*operands)


def tiled_body(patches, grad_embed, weight, straggler, decode, encode):
    count_dp, count_fsdp = lax.axis_size("dp"), lax.axis_size("fsdp")
    dp, me = lax.axis_index("dp"), lax.axis_index("fsdp")
    core = dp % 2
    place = jnp.stack([me, dp // 2, core])
    tokens, features = patches.shape
    columns = weight.shape[1]
    rows, depth, blocks = features // 2, features // count_dp, columns // LANES
    chunk = chunk_shape(rows, columns)

    def along_planes(block, step, replicas):
        pairs = [(d * 4 + f, d * 4 + (f ^ step(d % 2))) for d in replicas for f in range(4)]
        return lax.ppermute(block, ("dp", "fsdp"), pairs)

    with jax.named_scope("gather_weight"):
        first = along_planes(weight, lambda c: 1 + c, range(count_dp))

    with jax.named_scope("shares"):
        shares = encode * straggler[:, None] * decode[:, None]
        before = shifted(shares, "dp", 1)
    with jax.named_scope("send"):
        sent, left, held = call(
            functools.partial(send_kernel, depth),
            [
                jax.ShapeDtypeStruct((count_fsdp, *chunk), I16),
                jax.ShapeDtypeStruct((rows, tokens), BF16),
                jax.ShapeDtypeStruct((count_fsdp, tokens, columns), BF16),
            ],
            [place, in_hbm(patches), in_hbm(grad_embed), shares],
            [SMEM, HBM, HBM],
            [pltpu.VMEM(patches.shape, BF16), pltpu.SemaphoreType.DMA((count_fsdp + 1,))],
        )
    with jax.named_scope("own"):
        kept = call(
            own_kernel,
            jax.ShapeDtypeStruct((count_fsdp, blocks, rows, LANES), F32),
            [left, held],
            flops=10**11,
        )
        first, kept = lax.optimization_barrier((first, kept))
    with jax.named_scope("relay_weight"):
        second = exchange(first, "dp", 1)
        half = call(
            half_kernel,
            jax.ShapeDtypeStruct((rows, columns), BF16),
            [place, first],
            [SMEM],
        )
        far = along_planes(half, lambda c: 2 - c, range(count_dp))
    with jax.named_scope("pair"):
        came = exchange(sent, "dp", 1)
        before_sib = exchange(before, "dp", 1)
        kept, sent = call(
            pair_kernel,
            [
                jax.ShapeDtypeStruct((2, blocks, rows, LANES), F32),
                jax.ShapeDtypeStruct((2, *chunk), I16),
            ],
            [place, jnp.full((1,), tokens * count_fsdp, I32), kept, came, shares, before, before_sib],
            [SMEM] * 2,
            flops=10**11,
        )
    with jax.named_scope("first_step"):
        came = along_planes(sent, lambda c: 1 + c, range(count_dp))
    with jax.named_scope("embed_near"):
        far, second = lax.optimization_barrier((far, second))
        near = call(
            near_kernel,
            jax.ShapeDtypeStruct((3, tokens, columns), BF16),
            [place, in_hbm(patches), in_hbm(weight), first, second],
            [SMEM, HBM, HBM],
            [pltpu.VMEM(patches.shape, BF16), pltpu.VMEM(weight.shape, BF16), pltpu.SemaphoreType.DMA((2,))],
            flops=6 * 10**9,
        )
    with jax.named_scope("first_step_sum"):
        near, far, came = lax.optimization_barrier((near, far, came))
        kept, sent = call(
            step_kernel,
            [jax.ShapeDtypeStruct((blocks, rows, LANES), F32), jax.ShapeDtypeStruct(chunk, I16)],
            [kept, came],
        )
    with jax.named_scope("second_step"):
        came = along_planes(sent, lambda c: 2 - c, range(count_dp))
    with jax.named_scope("relay_weight"):
        far, kept = lax.optimization_barrier((far, kept))
        far_sib = exchange(far, "dp", 1)
    with jax.named_scope("embed"):
        embedded = call(
            embed_kernel,
            jax.ShapeDtypeStruct((tokens, columns * count_fsdp), BF16),
            [place, in_hbm(patches), near, far, far_sib],
            [SMEM, HBM],
            [pltpu.VMEM(patches.shape, BF16), pltpu.VMEM((2, tokens, rows), BF16), pltpu.SemaphoreType.DMA],
            flops=2 * tokens * features * columns,
        )
    with jax.named_scope("middle"):
        embedded, came = lax.optimization_barrier((embedded, came))
        parts = call(
            functools.partial(middle_kernel, depth),
            [jax.ShapeDtypeStruct(chunk_shape(depth, columns), I16)] * (count_dp // 2),
            [place, kept, came],
            [SMEM],
            [pltpu.VMEM((blocks, rows, LANES), F32)],
        )
        parts = [exchange(part, "dp", 2 * k) if k else part for k, part in enumerate(parts)]
    with jax.named_scope("last"):
        decoded = call(last_kernel, jax.ShapeDtypeStruct((depth, columns), F32), parts)
    return embedded, decoded


def plain_body(patches, grad_embed, weight, straggler, decode, encode):
    shares = (straggler * decode)[:, None] * encode
    factor = (shares[:, 0] + shifted(shares[:, 1], "dp", 1))[0]
    scale = factor.astype(F32) / (patches.shape[0] * lax.axis_size("fsdp"))
    whole = lax.all_gather(weight, "fsdp", axis=1, tiled=True)
    embedded = times(patches, whole).astype(BF16)
    term = scale * times(grad_embed, patches, ((0,), (0,)))
    term = lax.psum_scatter(term, "fsdp", scatter_dimension=0, tiled=True)
    return embedded, lax.psum_scatter(term.T, "dp", scatter_dimension=0, tiled=True)


def body(patches, grad_embed, weight, straggler, decode, encode):
    fits = patches.shape[1] % (16 * lax.axis_size("dp")) == 0 and weight.shape[1] % LANES == 0
    fits = fits and lax.axis_size("fsdp") == 4
    run = tiled_body if fits else plain_body
    return run(patches, grad_embed, weight, straggler, decode, encode)


def solution(mesh):
    return jax.shard_map(
        body,
        mesh=mesh,
        in_specs=(
            P(("dp", "fsdp"), None),
            P(("dp", "fsdp"), None),
            P(None, "fsdp"),
            P("dp"),
            P("dp"),
            P("dp", None),
        ),
        out_specs=(P(("dp", "fsdp"), None), P("dp", "fsdp")),
        check_vma=False,
    )
```

```python
import functools
import math

import jax
import jax.numpy as jnp
from jax import lax
from jax.experimental import pallas as pl
from jax.experimental.pallas import tpu as pltpu
from jax.sharding import PartitionSpec as P

LANES = 128
TAIL = 16
STEP = math.log(2) / 16
TOP = 32760.0
F32, BF16, I16, I32 = jnp.float32, jnp.bfloat16, jnp.int16, jnp.int32
VMEM = pl.BlockSpec(memory_space=pltpu.VMEM)
SMEM = pl.BlockSpec(memory_space=pltpu.SMEM)
HBM = pl.BlockSpec(memory_space=pltpu.HBM)


def in_hbm(array):
    return pltpu.with_memory_space_constraint(array, pltpu.HBM)


def exchange(block, axis, step):
    return lax.ppermute(block, axis, [(i, i ^ step) for i in range(lax.axis_size(axis))])


def shifted(block, axis, distance):
    count = lax.axis_size(axis)
    return lax.ppermute(block, axis, [((i - distance) % count, i) for i in range(count)])


def times(a, b, dims=((1,), (0,))):
    return lax.dot_general(a, b, (dims, ((), ())), preferred_element_type=F32)


def chunk_shape(rows, columns):
    return (columns // LANES * rows + TAIL, LANES)


def put_chunk(ref, blocks, extra=()):
    rows = blocks[0].shape[0]
    tail = jnp.zeros((TAIL, LANES), I32)
    row = lax.broadcasted_iota(I32, (TAIL, LANES), 0)
    for j, block in enumerate(blocks):
        largest = jnp.max(jnp.abs(block), axis=0, keepdims=True)
        power = jnp.ceil(jnp.log(jnp.maximum(largest, 2.0**-100)) * (1 / STEP))
        coded = block * (TOP * jnp.exp(power * -STEP))
        ref[pl.ds(j * rows, rows), :] = coded.astype(I32).astype(I16)
        tail = jnp.where(row == j, power.astype(I32), tail)
    for j, number in enumerate(extra):
        tail = jnp.where(row == TAIL - len(extra) + j, number, tail)
    ref[pl.ds(len(blocks) * rows, TAIL), :] = tail.astype(I16)


def get_chunk(ref, rows):
    count = (ref.shape[0] - TAIL) // rows
    tail = ref[pl.ds(count * rows, TAIL), :].astype(F32)
    scale = jnp.exp(tail * STEP) * (1 / TOP)
    return [ref[pl.ds(j * rows, rows), :].astype(F32) * scale[j : j + 1, :] for j in range(count)], tail


def lanes(j):
    return slice(j * LANES, (j + 1) * LANES)


def send_kernel(depth, place, patches, grad_embed, shares, sent, left, held, p_held, arrived):
    me, core = place[0], place[2]
    count, _, columns = held.shape
    blocks, features = columns // LANES, patches.shape[1]
    rows = features // 2
    copies = [pltpu.make_async_copy(patches, p_held, arrived.at[count])]
    for k in range(count):
        here = pl.ds(pl.multiple_of((me ^ k) * columns, columns), columns)
        copies.append(pltpu.make_async_copy(grad_embed.at[:, here], held.at[k], arrived.at[k]))
    for copy in copies:
        copy.start()
    extra = shares[:, 0:1], shares[:, 1:2]
    i = lax.broadcasted_iota(I32, (features, features), 0)
    j = lax.broadcasted_iota(I32, (features, features), 1)
    half, i = i // rows, i % rows
    chosen = jnp.where(j == (i // depth * 2 + (core ^ half)) * depth + i % depth, 1.0, 0.0).astype(BF16)
    copies[0].wait()
    turned = times(chosen, p_held[...], ((1,), (1,))).astype(BF16)
    left[...] = turned[:rows]
    for k in range(count):
        copies[1 + k].wait()
        value = times(turned[rows:], held[k])
        put_chunk(sent.at[k], [value[:, lanes(j)] for j in range(blocks)], extra)


def own_kernel(left, held, kept):
    for k in range(kept.shape[0]):
        value = times(left[...], held[k])
        for j in range(kept.shape[1]):
            kept[k, j] = value[:, lanes(j)]


def pair_kernel(bounds, place, tokens, kept, came, shares, before, before_sib, *outs):
    core = place[2]
    rows = kept.shape[2]
    first, second = shares[:, 0:1].astype(F32), shares[:, 1:2].astype(F32)
    tail = get_chunk(came.at[0], rows)[1]
    first_sib, second_sib = (tail[TAIL - 2 + j : TAIL - 1 + j, 0:1] for j in range(2))
    even = core == 0
    carried = jnp.where(even, before[:, 1:2], before_sib[:, 1:2]).astype(F32)
    scale = (first + jnp.where(even, carried, second_sib)) / tokens[0].astype(F32)
    scale_sib = (first_sib + jnp.where(even, second, carried)) / tokens[0].astype(F32)
    for (lo, hi), still, sent in zip(bounds, outs[::2], outs[1::2]):

        def value(k):
            parts, _ = get_chunk(came.at[k], rows)
            return [scale * kept[k, j] + scale_sib * parts[j] for j in range(lo, hi)]

        put_chunk(sent.at[0], value(1 + core))
        put_chunk(sent.at[1], value(3))
        for at, k in enumerate((0, 2 - core)):
            for j, part in enumerate(value(k)):
                still[at, j] = part


def step_kernel(kept, came, still, sent):
    _, blocks, rows, _ = kept.shape
    parts, _ = get_chunk(came.at[1], rows)
    put_chunk(sent, [kept[1, j] + part for j, part in enumerate(parts)])
    for j, part in enumerate(get_chunk(came.at[0], rows)[0]):
        still[j] = kept[0, j] + part


def middle_kernel(depth, place, kept, came, *refs):
    *outs, held = refs
    blocks, rows, _ = kept.shape
    for j, part in enumerate(get_chunk(came, rows)[0]):
        held[j] = kept[j] + part
    for k, out in enumerate(outs):
        here = pl.ds(pl.multiple_of((place[1] ^ k) * depth, depth), depth)
        put_chunk(out, [held[j, here, :] for j in range(blocks)])


def last_kernel(bounds, *refs):
    *ins, out = refs
    count = len(ins) // len(bounds)
    for i, (lo, _) in enumerate(bounds):
        parts = [get_chunk(ref, out.shape[0])[0] for ref in ins[i * count : (i + 1) * count]]
        for j, terms in enumerate(zip(*parts)):
            out[:, lanes(lo + j)] = sum(terms[1:], terms[0])


def half_kernel(place, first, half):
    rows = half.shape[0]
    half[...] = first[pl.ds(pl.multiple_of(place[2] * rows, rows), rows), :]


def near_kernel(place, patches, own, first, second, out, p_held, held, arrived):
    core = place[2]
    copies = [
        pltpu.make_async_copy(patches, p_held, arrived.at[0]),
        pltpu.make_async_copy(own, held, arrived.at[1]),
    ]
    for copy in copies:
        copy.start()
    copies[0].wait()
    out[1 + core] = times(p_held[...], first[...]).astype(BF16)
    out[2 - core] = times(p_held[...], second[...]).astype(BF16)
    copies[1].wait()
    out[0] = times(p_held[...], held[...]).astype(BF16)


def embed_kernel(place, patches, near, far, far_sib, out, p_held, halves, arrived):
    me, core, columns = place[0], place[2], near.shape[2]
    rows = far.shape[0]
    copy = pltpu.make_async_copy(patches, p_held, arrived)
    copy.start()

    def put(k, value):
        out[:, pl.ds(pl.multiple_of((me ^ k) * columns, columns), columns)] = value

    for k in range(3):
        put(k, near[k])
    copy.wait()
    halves[0] = p_held[:, :rows]
    halves[1] = p_held[:, rows:]
    put(3, (times(halves[core], far[...]) + times(halves[1 - core], far_sib[...])).astype(BF16))


def call(kernel, outs, operands, specs=(), scratch=(), flops=0):
    moved = sum(math.prod(a.shape) * a.dtype.itemsize for a in [*operands, *jax.tree.leaves(outs)]) if flops else 0
    return pl.pallas_call(
        kernel,
        out_shape=outs,
        in_specs=[*specs] + [VMEM] * (len(operands) - len(specs)),
        out_specs=jax.tree.map(lambda _: VMEM, outs),
        scratch_shapes=scratch,
        compiler_params=pltpu.CompilerParams(vmem_limit_bytes=24 * 2**20),
        cost_estimate=pl.CostEstimate(flops=flops, bytes_accessed=moved, transcendentals=0),
    )(*operands)


def tiled_body(patches, grad_embed, weight, straggler, decode, encode):
    count_dp, count_fsdp = lax.axis_size("dp"), lax.axis_size("fsdp")
    dp, me = lax.axis_index("dp"), lax.axis_index("fsdp")
    core = dp % 2
    place = jnp.stack([me, dp // 2, core])
    tokens, features = patches.shape
    columns = weight.shape[1]
    rows, depth, blocks = features // 2, features // count_dp, columns // LANES
    chunk = chunk_shape(rows, columns)
    bounds = [(0, blocks // 2), (blocks // 2, blocks)]

    def along_planes(block, step, replicas):
        pairs = [(d * 4 + f, d * 4 + (f ^ step(d % 2))) for d in replicas for f in range(4)]
        return lax.ppermute(block, ("dp", "fsdp"), pairs)

    with jax.named_scope("gather_weight"):
        first = along_planes(weight, lambda c: 1 + c, range(count_dp))

    with jax.named_scope("shares"):
        shares = encode * straggler[:, None] * decode[:, None]
        before = shifted(shares, "dp", 1)
    with jax.named_scope("send"):
        sent, left, held = call(
            functools.partial(send_kernel, depth),
            [
                jax.ShapeDtypeStruct((count_fsdp, *chunk), I16),
                jax.ShapeDtypeStruct((rows, tokens), BF16),
                jax.ShapeDtypeStruct((count_fsdp, tokens, columns), BF16),
            ],
            [place, in_hbm(patches), in_hbm(grad_embed), shares],
            [SMEM, HBM, HBM],
            [pltpu.VMEM(patches.shape, BF16), pltpu.SemaphoreType.DMA((count_fsdp + 1,))],
        )
    with jax.named_scope("own"):
        kept = call(
            own_kernel,
            jax.ShapeDtypeStruct((count_fsdp, blocks, rows, LANES), F32),
            [left, held],
            flops=10**11,
        )
        first, kept = lax.optimization_barrier((first, kept))
    with jax.named_scope("relay_weight"):
        second = exchange(first, "dp", 1)
        half = call(
            half_kernel,
            jax.ShapeDtypeStruct((rows, columns), BF16),
            [place, first],
            [SMEM],
        )
        far = along_planes(half, lambda c: 2 - c, range(count_dp))
    with jax.named_scope("pair"):
        came = exchange(sent, "dp", 1)
        before_sib = exchange(before, "dp", 1)
        outs = call(
            functools.partial(pair_kernel, bounds),
            [
                shape
                for lo, hi in bounds
                for shape in (
                    jax.ShapeDtypeStruct((2, hi - lo, rows, LANES), F32),
                    jax.ShapeDtypeStruct((2, *chunk_shape(rows, (hi - lo) * LANES)), I16),
                )
            ],
            [place, jnp.full((1,), tokens * count_fsdp, I32), kept, came, shares, before, before_sib],
            [SMEM] * 2,
            flops=10**11,
        )
        kept_parts = list(outs[::2])
        came_parts = [along_planes(sent, lambda c: 1 + c, range(count_dp)) for sent in outs[1::2]]
    with jax.named_scope("embed_near"):
        far, second = lax.optimization_barrier((far, second))
        near = call(
            near_kernel,
            jax.ShapeDtypeStruct((3, tokens, columns), BF16),
            [place, in_hbm(patches), in_hbm(weight), first, second],
            [SMEM, HBM, HBM],
            [pltpu.VMEM(patches.shape, BF16), pltpu.VMEM(weight.shape, BF16), pltpu.SemaphoreType.DMA((2,))],
            flops=2 * 10**9,
        )
        near, came_parts[0] = lax.optimization_barrier((near, came_parts[0]))
    with jax.named_scope("steps"):
        for i, (lo, hi) in enumerate(bounds):
            kept_parts[i], sent = call(
                step_kernel,
                [
                    jax.ShapeDtypeStruct((hi - lo, rows, LANES), F32),
                    jax.ShapeDtypeStruct(chunk_shape(rows, (hi - lo) * LANES), I16),
                ],
                [kept_parts[i], came_parts[i]],
                flops=(0, 10**10)[i],
            )
            came_parts[i] = along_planes(sent, lambda c: 2 - c, range(count_dp))
    with jax.named_scope("relay_weight"):
        far, kept_parts[1] = lax.optimization_barrier((far, kept_parts[1]))
        far_sib = exchange(far, "dp", 1)
    with jax.named_scope("middle"):
        sums = []
        for i, (lo, hi) in enumerate(bounds):
            if i and 1:
                came_parts[i], sums[1] = lax.optimization_barrier((came_parts[i], sums[1]))
            parts = call(
                functools.partial(middle_kernel, depth),
                [jax.ShapeDtypeStruct(chunk_shape(depth, (hi - lo) * LANES), I16)] * (count_dp // 2),
                [place, kept_parts[i], came_parts[i]],
                [SMEM],
                [pltpu.VMEM((hi - lo, rows, LANES), F32)],
                flops=10**10,
            )
            sums += [exchange(part, "dp", 2 * k) if k else part for k, part in enumerate(parts)]
    with jax.named_scope("embed"):
        near, sums[count_dp // 2] = lax.optimization_barrier((near, sums[count_dp // 2]))
        embedded = call(
            embed_kernel,
            jax.ShapeDtypeStruct((tokens, columns * count_fsdp), BF16),
            [place, in_hbm(patches), near, far, far_sib],
            [SMEM, HBM],
            [pltpu.VMEM(patches.shape, BF16), pltpu.VMEM((2, tokens, rows), BF16), pltpu.SemaphoreType.DMA],
            flops=10**10,
        )
    with jax.named_scope("last"):
        embedded, *sums = lax.optimization_barrier((embedded, *sums))
        decoded = call(
            functools.partial(last_kernel, bounds), jax.ShapeDtypeStruct((depth, columns), F32), sums
        )
    return embedded, decoded


def plain_body(patches, grad_embed, weight, straggler, decode, encode):
    shares = (straggler * decode)[:, None] * encode
    factor = (shares[:, 0] + shifted(shares[:, 1], "dp", 1))[0]
    scale = factor.astype(F32) / (patches.shape[0] * lax.axis_size("fsdp"))
    whole = lax.all_gather(weight, "fsdp", axis=1, tiled=True)
    embedded = times(patches, whole).astype(BF16)
    term = scale * times(grad_embed, patches, ((0,), (0,)))
    term = lax.psum_scatter(term, "fsdp", scatter_dimension=0, tiled=True)
    return embedded, lax.psum_scatter(term.T, "dp", scatter_dimension=0, tiled=True)


def body(patches, grad_embed, weight, straggler, decode, encode):
    fits = patches.shape[1] % (16 * lax.axis_size("dp")) == 0 and weight.shape[1] % LANES == 0
    fits = fits and lax.axis_size("fsdp") == 4
    run = tiled_body if fits else plain_body
    return run(patches, grad_embed, weight, straggler, decode, encode)


def solution(mesh):
    return jax.shard_map(
        body,
        mesh=mesh,
        in_specs=(
            P(("dp", "fsdp"), None),
            P(("dp", "fsdp"), None),
            P(None, "fsdp"),
            P("dp"),
            P("dp"),
            P("dp", None),
        ),
        out_specs=(P(("dp", "fsdp"), None), P("dp", "fsdp")),
        check_vma=False,
    )
```

```python
import functools
import math

import jax
import jax.numpy as jnp
from jax import lax
from jax.experimental import pallas as pl
from jax.experimental.pallas import tpu as pltpu
from jax.sharding import PartitionSpec as P

LANES = 128
TAIL = 16
STEP = math.log(2) / 16
TOP = 32760.0
F32, BF16, I16, I32 = jnp.float32, jnp.bfloat16, jnp.int16, jnp.int32
VMEM = pl.BlockSpec(memory_space=pltpu.VMEM)
SMEM = pl.BlockSpec(memory_space=pltpu.SMEM)
HBM = pl.BlockSpec(memory_space=pltpu.HBM)


def in_hbm(array):
    return pltpu.with_memory_space_constraint(array, pltpu.HBM)


def exchange(block, axis, step):
    return lax.ppermute(block, axis, [(i, i ^ step) for i in range(lax.axis_size(axis))])


def shifted(block, axis, distance):
    count = lax.axis_size(axis)
    return lax.ppermute(block, axis, [((i - distance) % count, i) for i in range(count)])


def times(a, b, dims=((1,), (0,))):
    return lax.dot_general(a, b, (dims, ((), ())), preferred_element_type=F32)


def chunk_shape(rows, columns):
    return (columns // LANES * rows + TAIL, LANES)


def put_chunk(ref, blocks, extra=()):
    rows = blocks[0].shape[0]
    tail = jnp.zeros((TAIL, LANES), I32)
    row = lax.broadcasted_iota(I32, (TAIL, LANES), 0)
    for j, block in enumerate(blocks):
        largest = jnp.max(jnp.abs(block), axis=0, keepdims=True)
        power = jnp.ceil(jnp.log(jnp.maximum(largest, 2.0**-100)) * (1 / STEP))
        coded = block * (TOP * jnp.exp(power * -STEP))
        ref[pl.ds(j * rows, rows), :] = coded.astype(I32).astype(I16)
        tail = jnp.where(row == j, power.astype(I32), tail)
    for j, number in enumerate(extra):
        tail = jnp.where(row == TAIL - len(extra) + j, number, tail)
    ref[pl.ds(len(blocks) * rows, TAIL), :] = tail.astype(I16)


def get_chunk(ref, rows):
    count = (ref.shape[0] - TAIL) // rows
    tail = ref[pl.ds(count * rows, TAIL), :].astype(F32)
    scale = jnp.exp(tail * STEP) * (1 / TOP)
    return [ref[pl.ds(j * rows, rows), :].astype(F32) * scale[j : j + 1, :] for j in range(count)], tail


def lanes(j):
    return slice(j * LANES, (j + 1) * LANES)


def send_kernel(depth, place, patches, grad_embed, shares, sent, left, held, p_held, arrived):
    me, core = place[0], place[2]
    count, _, columns = held.shape
    blocks, features = columns // LANES, patches.shape[1]
    rows = features // 2
    copies = [pltpu.make_async_copy(patches, p_held, arrived.at[count])]
    for k in range(count):
        here = pl.ds(pl.multiple_of((me ^ k) * columns, columns), columns)
        copies.append(pltpu.make_async_copy(grad_embed.at[:, here], held.at[k], arrived.at[k]))
    for copy in copies:
        copy.start()
    extra = shares[:, 0:1], shares[:, 1:2]
    i = lax.broadcasted_iota(I32, (features, features), 0)
    j = lax.broadcasted_iota(I32, (features, features), 1)
    half, i = i // rows, i % rows
    chosen = jnp.where(j == (i // depth * 2 + (core ^ half)) * depth + i % depth, 1.0, 0.0).astype(BF16)
    copies[0].wait()
    turned = times(chosen, p_held[...], ((1,), (1,))).astype(BF16)
    left[...] = turned[:rows]
    for k in range(count):
        copies[1 + k].wait()
        value = times(turned[rows:], held[k])
        put_chunk(sent.at[k], [value[:, lanes(j)] for j in range(blocks)], extra)


def own_kernel(left, held, kept):
    for k in range(kept.shape[0]):
        value = times(left[...], held[k])
        for j in range(kept.shape[1]):
            kept[k, j] = value[:, lanes(j)]


def pair_kernel(bounds, place, tokens, kept, came, shares, before, before_sib, *outs):
    core = place[2]
    rows = kept.shape[2]
    first, second = shares[:, 0:1].astype(F32), shares[:, 1:2].astype(F32)
    tail = get_chunk(came.at[0], rows)[1]
    first_sib, second_sib = (tail[TAIL - 2 + j : TAIL - 1 + j, 0:1] for j in range(2))
    even = core == 0
    carried = jnp.where(even, before[:, 1:2], before_sib[:, 1:2]).astype(F32)
    scale = (first + jnp.where(even, carried, second_sib)) / tokens[0].astype(F32)
    scale_sib = (first_sib + jnp.where(even, second, carried)) / tokens[0].astype(F32)
    for (lo, hi), still, sent in zip(bounds, outs[::2], outs[1::2]):

        def value(k):
            parts, _ = get_chunk(came.at[k], rows)
            return [scale * kept[k, j] + scale_sib * parts[j] for j in range(lo, hi)]

        put_chunk(sent.at[0], value(1 + core))
        put_chunk(sent.at[1], value(3))
        for at, k in enumerate((0, 2 - core)):
            for j, part in enumerate(value(k)):
                still[at, j] = part


def step_kernel(kept, came, still, sent):
    _, blocks, rows, _ = kept.shape
    parts, _ = get_chunk(came.at[1], rows)
    put_chunk(sent, [kept[1, j] + part for j, part in enumerate(parts)])
    for j, part in enumerate(get_chunk(came.at[0], rows)[0]):
        still[j] = kept[0, j] + part


def middle_kernel(depth, kept, came, out, held):
    blocks, rows, _ = kept.shape
    for j, part in enumerate(get_chunk(came, rows)[0]):
        held[j] = kept[j] + part
    for k in range(out.shape[0]):
        put_chunk(out.at[k], [held[j, pl.ds(k * depth, depth), :] for j in range(blocks)])


def last_kernel(bounds, *refs):
    *ins, out = refs
    for (lo, _), came in zip(bounds, ins):
        parts = [get_chunk(came.at[k], out.shape[0])[0] for k in range(came.shape[0])]
        for j, terms in enumerate(zip(*parts)):
            out[:, lanes(lo + j)] = sum(terms[1:], terms[0])


def half_kernel(place, first, half):
    rows = half.shape[0]
    half[...] = first[pl.ds(pl.multiple_of(place[2] * rows, rows), rows), :]


def near_kernel(place, patches, own, first, second, out):
    core = place[2]
    for k, weight in ((1 + core, first), (2 - core, second), (0, own)):
        out[k] = times(patches[...], weight[...]).astype(BF16)


def embed_kernel(place, patches, near, far, far_sib, out, halves):
    me, core, columns = place[0], place[2], near.shape[2]
    rows = far.shape[0]

    def put(k, value):
        out[:, pl.ds(pl.multiple_of((me ^ k) * columns, columns), columns)] = value

    halves[0] = patches[:, :rows]
    halves[1] = patches[:, rows:]
    put(3, (times(halves[core], far[...]) + times(halves[1 - core], far_sib[...])).astype(BF16))
    for k in range(3):
        put(k, near[k])


def call(kernel, outs, operands, specs=(), scratch=(), flops=0):
    moved = sum(math.prod(a.shape) * a.dtype.itemsize for a in [*operands, *jax.tree.leaves(outs)]) if flops else 0
    return pl.pallas_call(
        kernel,
        out_shape=outs,
        in_specs=[*specs] + [VMEM] * (len(operands) - len(specs)),
        out_specs=jax.tree.map(lambda _: VMEM, outs),
        scratch_shapes=scratch,
        compiler_params=pltpu.CompilerParams(vmem_limit_bytes=24 * 2**20),
        cost_estimate=pl.CostEstimate(flops=flops, bytes_accessed=moved, transcendentals=0),
    )(*operands)


def tiled_body(patches, grad_embed, weight, straggler, decode, encode):
    count_dp, count_fsdp = lax.axis_size("dp"), lax.axis_size("fsdp")
    dp, me = lax.axis_index("dp"), lax.axis_index("fsdp")
    core = dp % 2
    place = jnp.stack([me, dp // 2, core])
    tokens, features = patches.shape
    columns = weight.shape[1]
    rows, depth, blocks = features // 2, features // count_dp, columns // LANES
    chunk = chunk_shape(rows, columns)
    bounds = [(0, blocks // 2), (blocks // 2, blocks)]

    def along_planes(block, step, replicas):
        pairs = [(d * 4 + f, d * 4 + (f ^ step(d % 2))) for d in replicas for f in range(4)]
        return lax.ppermute(block, ("dp", "fsdp"), pairs)

    with jax.named_scope("gather_weight"):
        first = along_planes(weight, lambda c: 1 + c, range(count_dp))

    with jax.named_scope("shares"):
        shares = encode * straggler[:, None] * decode[:, None]
        before = shifted(shares, "dp", 1)
    with jax.named_scope("send"):
        sent, left, held = call(
            functools.partial(send_kernel, depth),
            [
                jax.ShapeDtypeStruct((count_fsdp, *chunk), I16),
                jax.ShapeDtypeStruct((rows, tokens), BF16),
                jax.ShapeDtypeStruct((count_fsdp, tokens, columns), BF16),
            ],
            [place, in_hbm(patches), in_hbm(grad_embed), shares],
            [SMEM, HBM, HBM],
            [pltpu.VMEM(patches.shape, BF16), pltpu.SemaphoreType.DMA((count_fsdp + 1,))],
        )
    with jax.named_scope("own"):
        kept = call(
            own_kernel,
            jax.ShapeDtypeStruct((count_fsdp, blocks, rows, LANES), F32),
            [left, held],
            flops=10**11,
        )
        first, kept = lax.optimization_barrier((first, kept))
    with jax.named_scope("relay_weight"):
        second = exchange(first, "dp", 1)
        half = call(
            half_kernel,
            jax.ShapeDtypeStruct((rows, columns), BF16),
            [place, first],
            [SMEM],
        )
        far = along_planes(half, lambda c: 2 - c, range(count_dp))
    with jax.named_scope("pair"):
        came = exchange(sent, "dp", 1)
        before_sib = exchange(before, "dp", 1)
        outs = call(
            functools.partial(pair_kernel, bounds),
            [
                shape
                for lo, hi in bounds
                for shape in (
                    jax.ShapeDtypeStruct((2, hi - lo, rows, LANES), F32),
                    jax.ShapeDtypeStruct((2, *chunk_shape(rows, (hi - lo) * LANES)), I16),
                )
            ],
            [place, jnp.full((1,), tokens * count_fsdp, I32), kept, came, shares, before, before_sib],
            [SMEM] * 2,
            flops=10**11,
        )
        kept_parts = list(outs[::2])
        came_parts = [along_planes(sent, lambda c: 1 + c, range(count_dp)) for sent in outs[1::2]]
    with jax.named_scope("embed_near"):
        far, second = lax.optimization_barrier((far, second))
        near = call(
            near_kernel,
            jax.ShapeDtypeStruct((3, tokens, columns), BF16),
            [place, patches, weight, first, second],
            [SMEM],
            flops=2 * 10**9,
        )
        near, came_parts[0] = lax.optimization_barrier((near, came_parts[0]))
    with jax.named_scope("steps"):
        for i, (lo, hi) in enumerate(bounds):
            kept_parts[i], sent = call(
                step_kernel,
                [
                    jax.ShapeDtypeStruct((hi - lo, rows, LANES), F32),
                    jax.ShapeDtypeStruct(chunk_shape(rows, (hi - lo) * LANES), I16),
                ],
                [kept_parts[i], came_parts[i]],
                flops=(0, 10**10)[i],
            )
            came_parts[i] = along_planes(sent, lambda c: 2 - c, range(count_dp))
    with jax.named_scope("relay_weight"):
        far, kept_parts[1] = lax.optimization_barrier((far, kept_parts[1]))
        far_sib = exchange(far, "dp", 1)
    with jax.named_scope("middle"):
        sums = []
        for i, (lo, hi) in enumerate(bounds):
            part = call(
                functools.partial(middle_kernel, depth),
                jax.ShapeDtypeStruct((count_dp // 2, *chunk_shape(depth, (hi - lo) * LANES)), I16),
                [kept_parts[i], came_parts[i]],
                (),
                [pltpu.VMEM((hi - lo, rows, LANES), F32)],
                flops=10**10,
            )
            groups = [list(range(c, count_dp, 2)) for c in (0, 1)]
            sums.append(lax.all_to_all(part, "dp", 0, 0, axis_index_groups=groups))
            last_part = part
    with jax.named_scope("embed"):
        near, _ = lax.optimization_barrier((near, last_part))
        embedded = call(
            embed_kernel,
            jax.ShapeDtypeStruct((tokens, columns * count_fsdp), BF16),
            [place, patches, near, far, far_sib],
            [SMEM],
            [pltpu.VMEM((2, tokens, rows), BF16)],
            flops=10**10,
        )
    with jax.named_scope("last"):
        embedded, *sums = lax.optimization_barrier((embedded, *sums))
        decoded = call(
            functools.partial(last_kernel, bounds), jax.ShapeDtypeStruct((depth, columns), F32), sums
        )
    return embedded, decoded


def plain_body(patches, grad_embed, weight, straggler, decode, encode):
    shares = (straggler * decode)[:, None] * encode
    factor = (shares[:, 0] + shifted(shares[:, 1], "dp", 1))[0]
    scale = factor.astype(F32) / (patches.shape[0] * lax.axis_size("fsdp"))
    whole = lax.all_gather(weight, "fsdp", axis=1, tiled=True)
    embedded = times(patches, whole).astype(BF16)
    term = scale * times(grad_embed, patches, ((0,), (0,)))
    term = lax.psum_scatter(term, "fsdp", scatter_dimension=0, tiled=True)
    return embedded, lax.psum_scatter(term.T, "dp", scatter_dimension=0, tiled=True)


def body(patches, grad_embed, weight, straggler, decode, encode):
    fits = patches.shape[1] % (16 * lax.axis_size("dp")) == 0 and weight.shape[1] % LANES == 0
    fits = fits and lax.axis_size("fsdp") == 4
    run = tiled_body if fits else plain_body
    return run(patches, grad_embed, weight, straggler, decode, encode)


def solution(mesh):
    return jax.shard_map(
        body,
        mesh=mesh,
        in_specs=(
            P(("dp", "fsdp"), None),
            P(("dp", "fsdp"), None),
            P(None, "fsdp"),
            P("dp"),
            P("dp"),
            P("dp", None),
        ),
        out_specs=(P(("dp", "fsdp"), None), P("dp", "fsdp")),
        check_vma=False,
    )
```

```python
import functools
import math

import jax
import jax.numpy as jnp
from jax import lax
from jax.experimental import pallas as pl
from jax.experimental.pallas import tpu as pltpu
from jax.sharding import PartitionSpec as P

LANES = 128
TAIL = 16
STEP = math.log(2) / 16
TOP = 32760.0
F32, BF16, I16, I32 = jnp.float32, jnp.bfloat16, jnp.int16, jnp.int32
VMEM = pl.BlockSpec(memory_space=pltpu.VMEM)
SMEM = pl.BlockSpec(memory_space=pltpu.SMEM)
HBM = pl.BlockSpec(memory_space=pltpu.HBM)


def in_hbm(array):
    return pltpu.with_memory_space_constraint(array, pltpu.HBM)


def exchange(block, axis, step):
    return lax.ppermute(block, axis, [(i, i ^ step) for i in range(lax.axis_size(axis))])


def shifted(block, axis, distance):
    count = lax.axis_size(axis)
    return lax.ppermute(block, axis, [((i - distance) % count, i) for i in range(count)])


def times(a, b, dims=((1,), (0,))):
    return lax.dot_general(a, b, (dims, ((), ())), preferred_element_type=F32)


def chunk_shape(rows, columns):
    return (columns // LANES * rows + TAIL, LANES)


def put_chunk(ref, blocks, extra=()):
    rows = blocks[0].shape[0]
    tail = jnp.zeros((TAIL, LANES), I32)
    row = lax.broadcasted_iota(I32, (TAIL, LANES), 0)
    for j, block in enumerate(blocks):
        largest = jnp.max(jnp.abs(block), axis=0, keepdims=True)
        power = jnp.ceil(jnp.log(jnp.maximum(largest, 2.0**-100)) * (1 / STEP))
        coded = block * (TOP * jnp.exp(power * -STEP))
        ref[pl.ds(j * rows, rows), :] = coded.astype(I32).astype(I16)
        tail = jnp.where(row == j, power.astype(I32), tail)
    for j, number in enumerate(extra):
        tail = jnp.where(row == TAIL - len(extra) + j, number, tail)
    ref[pl.ds(len(blocks) * rows, TAIL), :] = tail.astype(I16)


def get_chunk(ref, rows):
    count = (ref.shape[0] - TAIL) // rows
    tail = ref[pl.ds(count * rows, TAIL), :].astype(F32)
    scale = jnp.exp(tail * STEP) * (1 / TOP)
    return [ref[pl.ds(j * rows, rows), :].astype(F32) * scale[j : j + 1, :] for j in range(count)], tail


def lanes(j):
    return slice(j * LANES, (j + 1) * LANES)


def send_kernel(depth, place, patches, grad_embed, shares, sent, left, held, p_held, arrived):
    me, core = place[0], place[2]
    count, _, columns = held.shape
    blocks, features = columns // LANES, patches.shape[1]
    rows = features // 2
    copies = [pltpu.make_async_copy(patches, p_held, arrived.at[count])]
    for k in range(count):
        here = pl.ds(pl.multiple_of((me ^ k) * columns, columns), columns)
        copies.append(pltpu.make_async_copy(grad_embed.at[:, here], held.at[k], arrived.at[k]))
    for copy in copies:
        copy.start()
    extra = shares[:, 0:1], shares[:, 1:2]
    i = lax.broadcasted_iota(I32, (features, features), 0)
    j = lax.broadcasted_iota(I32, (features, features), 1)
    half, i = i // rows, i % rows
    chosen = jnp.where(j == (i // depth * 2 + (core ^ half)) * depth + i % depth, 1.0, 0.0).astype(BF16)
    copies[0].wait()
    turned = times(chosen, p_held[...], ((1,), (1,))).astype(BF16)
    left[...] = turned[:rows]
    for k in range(count):
        copies[1 + k].wait()
        value = times(turned[rows:], held[k])
        put_chunk(sent.at[k], [value[:, lanes(j)] for j in range(blocks)], extra)


def own_kernel(left, held, kept):
    for k in range(kept.shape[0]):
        value = times(left[...], held[k])
        for j in range(kept.shape[1]):
            kept[k, j] = value[:, lanes(j)]


def pair_kernel(bounds, place, tokens, kept, came, shares, before, before_sib, *outs):
    core = place[2]
    rows = kept.shape[2]
    first, second = shares[:, 0:1].astype(F32), shares[:, 1:2].astype(F32)
    tail = get_chunk(came.at[0], rows)[1]
    first_sib, second_sib = (tail[TAIL - 2 + j : TAIL - 1 + j, 0:1] for j in range(2))
    even = core == 0
    carried = jnp.where(even, before[:, 1:2], before_sib[:, 1:2]).astype(F32)
    scale = (first + jnp.where(even, carried, second_sib)) / tokens[0].astype(F32)
    scale_sib = (first_sib + jnp.where(even, second, carried)) / tokens[0].astype(F32)
    for (lo, hi), still, sent in zip(bounds, outs[::2], outs[1::2]):

        def value(k):
            parts, _ = get_chunk(came.at[k], rows)
            return [scale * kept[k, j] + scale_sib * parts[j] for j in range(lo, hi)]

        put_chunk(sent.at[0], value(1 + core))
        put_chunk(sent.at[1], value(3))
        for at, k in enumerate((0, 2 - core)):
            for j, part in enumerate(value(k)):
                still[at, j] = part


def step_kernel(kept, came, still, sent):
    _, blocks, rows, _ = kept.shape
    parts, _ = get_chunk(came.at[1], rows)
    put_chunk(sent, [kept[1, j] + part for j, part in enumerate(parts)])
    for j, part in enumerate(get_chunk(came.at[0], rows)[0]):
        still[j] = kept[0, j] + part


def merge_kernel(kept, came, out):
    for j, part in enumerate(get_chunk(came, kept.shape[1])[0]):
        out[j] = kept[j] + part


def middle_kernel(split, depth, place, done, kept, came, *refs):
    *outs, held = refs
    blocks, rows, _ = held.shape
    held[:split] = done[...]
    for j, part in enumerate(get_chunk(came, rows)[0]):
        held[split + j] = kept[j] + part
    for k, out in enumerate(outs):
        here = pl.ds(pl.multiple_of((place[1] ^ k) * depth, depth), depth)
        put_chunk(out, [held[j, here, :] for j in range(blocks)])


def last_kernel(*refs):
    *ins, out = refs
    parts = [get_chunk(ref, out.shape[0])[0] for ref in ins]
    for j, terms in enumerate(zip(*parts)):
        out[:, lanes(j)] = sum(terms[1:], terms[0])


def half_kernel(place, first, half):
    rows = half.shape[0]
    half[...] = first[pl.ds(pl.multiple_of(place[2] * rows, rows), rows), :]


def near_kernel(place, patches, own, first, second, out):
    core = place[2]
    for k, weight in ((1 + core, first), (2 - core, second), (0, own)):
        out[k] = times(patches[...], weight[...]).astype(BF16)


def embed_kernel(place, patches, near, far, far_sib, out, halves):
    me, core, columns = place[0], place[2], near.shape[2]
    rows = far.shape[0]

    def put(k, value):
        out[:, pl.ds(pl.multiple_of((me ^ k) * columns, columns), columns)] = value

    halves[0] = patches[:, :rows]
    halves[1] = patches[:, rows:]
    put(3, (times(halves[core], far[...]) + times(halves[1 - core], far_sib[...])).astype(BF16))
    for k in range(3):
        put(k, near[k])


def call(kernel, outs, operands, specs=(), scratch=(), flops=0):
    moved = sum(math.prod(a.shape) * a.dtype.itemsize for a in [*operands, *jax.tree.leaves(outs)]) if flops else 0
    return pl.pallas_call(
        kernel,
        out_shape=outs,
        in_specs=[*specs] + [VMEM] * (len(operands) - len(specs)),
        out_specs=jax.tree.map(lambda _: VMEM, outs),
        scratch_shapes=scratch,
        compiler_params=pltpu.CompilerParams(vmem_limit_bytes=24 * 2**20),
        cost_estimate=pl.CostEstimate(flops=flops, bytes_accessed=moved, transcendentals=0),
    )(*operands)


def tiled_body(patches, grad_embed, weight, straggler, decode, encode):
    count_dp, count_fsdp = lax.axis_size("dp"), lax.axis_size("fsdp")
    dp, me = lax.axis_index("dp"), lax.axis_index("fsdp")
    core = dp % 2
    place = jnp.stack([me, dp // 2, core])
    tokens, features = patches.shape
    columns = weight.shape[1]
    rows, depth, blocks = features // 2, features // count_dp, columns // LANES
    chunk = chunk_shape(rows, columns)
    bounds = [(0, blocks // 2), (blocks // 2, blocks)]

    def along_planes(block, step, replicas):
        pairs = [(d * 4 + f, d * 4 + (f ^ step(d % 2))) for d in replicas for f in range(4)]
        return lax.ppermute(block, ("dp", "fsdp"), pairs)

    with jax.named_scope("gather_weight"):
        first = along_planes(weight, lambda c: 1 + c, range(count_dp))

    with jax.named_scope("shares"):
        shares = encode * straggler[:, None] * decode[:, None]
        before = shifted(shares, "dp", 1)
    with jax.named_scope("send"):
        sent, left, held = call(
            functools.partial(send_kernel, depth),
            [
                jax.ShapeDtypeStruct((count_fsdp, *chunk), I16),
                jax.ShapeDtypeStruct((rows, tokens), BF16),
                jax.ShapeDtypeStruct((count_fsdp, tokens, columns), BF16),
            ],
            [place, in_hbm(patches), in_hbm(grad_embed), shares],
            [SMEM, HBM, HBM],
            [pltpu.VMEM(patches.shape, BF16), pltpu.SemaphoreType.DMA((count_fsdp + 1,))],
        )
    with jax.named_scope("own"):
        kept = call(
            own_kernel,
            jax.ShapeDtypeStruct((count_fsdp, blocks, rows, LANES), F32),
            [left, held],
            flops=10**11,
        )
        first, kept = lax.optimization_barrier((first, kept))
    with jax.named_scope("relay_weight"):
        second = exchange(first, "dp", 1)
        half = call(
            half_kernel,
            jax.ShapeDtypeStruct((rows, columns), BF16),
            [place, first],
            [SMEM],
        )
        far = along_planes(half, lambda c: 2 - c, range(count_dp))
    with jax.named_scope("pair"):
        came = exchange(sent, "dp", 1)
        before_sib = exchange(before, "dp", 1)
        outs = call(
            functools.partial(pair_kernel, bounds),
            [
                shape
                for lo, hi in bounds
                for shape in (
                    jax.ShapeDtypeStruct((2, hi - lo, rows, LANES), F32),
                    jax.ShapeDtypeStruct((2, *chunk_shape(rows, (hi - lo) * LANES)), I16),
                )
            ],
            [place, jnp.full((1,), tokens * count_fsdp, I32), kept, came, shares, before, before_sib],
            [SMEM] * 2,
            flops=10**11,
        )
        kept_parts = list(outs[::2])
        came_parts = [along_planes(sent, lambda c: 1 + c, range(count_dp)) for sent in outs[1::2]]
    with jax.named_scope("embed_near"):
        far, second = lax.optimization_barrier((far, second))
        near = call(
            near_kernel,
            jax.ShapeDtypeStruct((3, tokens, columns), BF16),
            [place, patches, weight, first, second],
            [SMEM],
            flops=2 * 10**9,
        )
        near, came_parts[0] = lax.optimization_barrier((near, came_parts[0]))
    with jax.named_scope("steps"):
        for i, (lo, hi) in enumerate(bounds):
            kept_parts[i], sent = call(
                step_kernel,
                [
                    jax.ShapeDtypeStruct((hi - lo, rows, LANES), F32),
                    jax.ShapeDtypeStruct(chunk_shape(rows, (hi - lo) * LANES), I16),
                ],
                [kept_parts[i], came_parts[i]],
                flops=(0, 10**10)[i],
            )
            came_parts[i] = along_planes(sent, lambda c: 2 - c, range(count_dp))
    with jax.named_scope("relay_weight"):
        far, kept_parts[1] = lax.optimization_barrier((far, kept_parts[1]))
        far_sib = exchange(far, "dp", 1)
    with jax.named_scope("middle"):
        done = call(
            merge_kernel,
            jax.ShapeDtypeStruct(kept_parts[0].shape, F32),
            [kept_parts[0], came_parts[0]],
            flops=10**10,
        )
        parts = call(
            functools.partial(middle_kernel, bounds[1][0], depth),
            [jax.ShapeDtypeStruct(chunk_shape(depth, columns), I16)] * (count_dp // 2),
            [place, done, kept_parts[1], came_parts[1]],
            [SMEM],
            [pltpu.VMEM((blocks, rows, LANES), F32)],
        )
        parts = [exchange(part, "dp", 2 * k) if k else part for k, part in enumerate(parts)]
    with jax.named_scope("embed"):
        near, parts[0] = lax.optimization_barrier((near, parts[0]))
        embedded = call(
            embed_kernel,
            jax.ShapeDtypeStruct((tokens, columns * count_fsdp), BF16),
            [place, patches, near, far, far_sib],
            [SMEM],
            [pltpu.VMEM((2, tokens, rows), BF16)],
            flops=10**10,
        )
    with jax.named_scope("last"):
        embedded, *parts = lax.optimization_barrier((embedded, *parts))
        decoded = call(last_kernel, jax.ShapeDtypeStruct((depth, columns), F32), parts)
    return embedded, decoded


def plain_body(patches, grad_embed, weight, straggler, decode, encode):
    shares = (straggler * decode)[:, None] * encode
    factor = (shares[:, 0] + shifted(shares[:, 1], "dp", 1))[0]
    scale = factor.astype(F32) / (patches.shape[0] * lax.axis_size("fsdp"))
    whole = lax.all_gather(weight, "fsdp", axis=1, tiled=True)
    embedded = times(patches, whole).astype(BF16)
    term = scale * times(grad_embed, patches, ((0,), (0,)))
    term = lax.psum_scatter(term, "fsdp", scatter_dimension=0, tiled=True)
    return embedded, lax.psum_scatter(term.T, "dp", scatter_dimension=0, tiled=True)


def body(patches, grad_embed, weight, straggler, decode, encode):
    fits = patches.shape[1] % (16 * lax.axis_size("dp")) == 0 and weight.shape[1] % LANES == 0
    fits = fits and lax.axis_size("fsdp") == 4
    run = tiled_body if fits else plain_body
    return run(patches, grad_embed, weight, straggler, decode, encode)


def solution(mesh):
    return jax.shard_map(
        body,
        mesh=mesh,
        in_specs=(
            P(("dp", "fsdp"), None),
            P(("dp", "fsdp"), None),
            P(None, "fsdp"),
            P("dp"),
            P("dp"),
            P("dp", None),
        ),
        out_specs=(P(("dp", "fsdp"), None), P("dp", "fsdp")),
        check_vma=False,
    )
```

```python
import functools
import math

import jax
import jax.numpy as jnp
from jax import lax
from jax.experimental import pallas as pl
from jax.experimental.pallas import tpu as pltpu
from jax.sharding import PartitionSpec as P

LANES = 128
TAIL = 16
STEP = math.log(2) / 16
TOP = 32760.0
F32, BF16, I16, I32 = jnp.float32, jnp.bfloat16, jnp.int16, jnp.int32
VMEM = pl.BlockSpec(memory_space=pltpu.VMEM)
SMEM = pl.BlockSpec(memory_space=pltpu.SMEM)
HBM = pl.BlockSpec(memory_space=pltpu.HBM)


def in_hbm(array):
    return pltpu.with_memory_space_constraint(array, pltpu.HBM)


def exchange(block, axis, step):
    return lax.ppermute(block, axis, [(i, i ^ step) for i in range(lax.axis_size(axis))])


def shifted(block, axis, distance):
    count = lax.axis_size(axis)
    return lax.ppermute(block, axis, [((i - distance) % count, i) for i in range(count)])


def times(a, b, dims=((1,), (0,))):
    return lax.dot_general(a, b, (dims, ((), ())), preferred_element_type=F32)


def chunk_shape(rows, columns):
    return (columns // LANES * rows + TAIL, LANES)


def put_chunk(ref, blocks, extra=()):
    rows = blocks[0].shape[0]
    tail = jnp.zeros((TAIL, LANES), I32)
    row = lax.broadcasted_iota(I32, (TAIL, LANES), 0)
    for j, block in enumerate(blocks):
        largest = jnp.max(jnp.abs(block), axis=0, keepdims=True)
        power = jnp.ceil(jnp.log(jnp.maximum(largest, 2.0**-100)) * (1 / STEP))
        coded = block * (TOP * jnp.exp(power * -STEP))
        ref[pl.ds(j * rows, rows), :] = coded.astype(I32).astype(I16)
        tail = jnp.where(row == j, power.astype(I32), tail)
    for j, number in enumerate(extra):
        tail = jnp.where(row == TAIL - len(extra) + j, number, tail)
    ref[pl.ds(len(blocks) * rows, TAIL), :] = tail.astype(I16)


def get_chunk(ref, rows):
    count = (ref.shape[0] - TAIL) // rows
    tail = ref[pl.ds(count * rows, TAIL), :].astype(F32)
    scale = jnp.exp(tail * STEP) * (1 / TOP)
    return [ref[pl.ds(j * rows, rows), :].astype(F32) * scale[j : j + 1, :] for j in range(count)], tail


def lanes(j):
    return slice(j * LANES, (j + 1) * LANES)


def send_kernel(depth, place, patches, grad_embed, shares, sent, left, held, p_held, arrived):
    me, core = place[0], place[2]
    count, _, columns = held.shape
    blocks, features = columns // LANES, patches.shape[1]
    rows = features // 2
    copies = [pltpu.make_async_copy(patches, p_held, arrived.at[count])]
    for k in range(count):
        here = pl.ds(pl.multiple_of((me ^ k) * columns, columns), columns)
        copies.append(pltpu.make_async_copy(grad_embed.at[:, here], held.at[k], arrived.at[k]))
    for copy in copies:
        copy.start()
    extra = shares[:, 0:1], shares[:, 1:2]
    i = lax.broadcasted_iota(I32, (features, features), 0)
    j = lax.broadcasted_iota(I32, (features, features), 1)
    half, i = i // rows, i % rows
    chosen = jnp.where(j == (i // depth * 2 + (core ^ half)) * depth + i % depth, 1.0, 0.0).astype(BF16)
    copies[0].wait()
    turned = times(chosen, p_held[...], ((1,), (1,))).astype(BF16)
    left[...] = turned[:rows]
    for k in range(count):
        copies[1 + k].wait()
        value = times(turned[rows:], held[k])
        put_chunk(sent.at[k], [value[:, lanes(j)] for j in range(blocks)], extra)


def own_kernel(left, held, kept):
    for k in range(kept.shape[0]):
        value = times(left[...], held[k])
        for j in range(kept.shape[1]):
            kept[k, j] = value[:, lanes(j)]


def pair_kernel(bounds, place, tokens, kept, came, shares, before, before_sib, *outs):
    core = place[2]
    rows = kept.shape[2]
    first, second = shares[:, 0:1].astype(F32), shares[:, 1:2].astype(F32)
    tail = get_chunk(came.at[0], rows)[1]
    first_sib, second_sib = (tail[TAIL - 2 + j : TAIL - 1 + j, 0:1] for j in range(2))
    even = core == 0
    carried = jnp.where(even, before[:, 1:2], before_sib[:, 1:2]).astype(F32)
    scale = (first + jnp.where(even, carried, second_sib)) / tokens[0].astype(F32)
    scale_sib = (first_sib + jnp.where(even, second, carried)) / tokens[0].astype(F32)
    for (lo, hi), still, sent in zip(bounds, outs[::2], outs[1::2]):

        def value(k):
            parts, _ = get_chunk(came.at[k], rows)
            return [scale * kept[k, j] + scale_sib * parts[j] for j in range(lo, hi)]

        put_chunk(sent.at[0], value(1 + core))
        put_chunk(sent.at[1], value(3))
        for at, k in enumerate((0, 2 - core)):
            for j, part in enumerate(value(k)):
                still[at, j] = part


def step_kernel(kept, came, still, sent):
    _, blocks, rows, _ = kept.shape
    parts, _ = get_chunk(came.at[1], rows)
    put_chunk(sent, [kept[1, j] + part for j, part in enumerate(parts)])
    for j, part in enumerate(get_chunk(came.at[0], rows)[0]):
        still[j] = kept[0, j] + part


def merge_kernel(kept, came, out):
    for j, part in enumerate(get_chunk(came, kept.shape[1])[0]):
        out[j] = kept[j] + part


def middle_kernel(split, depth, place, done, kept, came, *refs):
    *outs, held = refs
    blocks, rows, _ = held.shape
    held[:split] = done[...]
    for j, part in enumerate(get_chunk(came, rows)[0]):
        held[split + j] = kept[j] + part
    for k, out in enumerate(outs):
        here = pl.ds(pl.multiple_of((place[1] ^ k) * depth, depth), depth)
        put_chunk(out, [held[j, here, :] for j in range(blocks)])


def last_kernel(*refs):
    *ins, out = refs
    parts = [get_chunk(ref, out.shape[0])[0] for ref in ins]
    for j, terms in enumerate(zip(*parts)):
        out[:, lanes(j)] = sum(terms[1:], terms[0])


def near_kernel(place, patches, own, first, second, out):
    core = place[2]
    for k, weight in ((1 + core, first), (2 - core, second), (0, own)):
        out[k] = times(patches[...], weight[...]).astype(BF16)


def embed_kernel(place, patches, near, far, out):
    me, columns = place[0], near.shape[2]

    def put(k, value):
        out[:, pl.ds(pl.multiple_of((me ^ k) * columns, columns), columns)] = value

    put(3, times(patches[...], far[...]).astype(BF16))
    for k in range(3):
        put(k, near[k])


def call(kernel, outs, operands, specs=(), scratch=(), flops=0):
    moved = sum(math.prod(a.shape) * a.dtype.itemsize for a in [*operands, *jax.tree.leaves(outs)]) if flops else 0
    return pl.pallas_call(
        kernel,
        out_shape=outs,
        in_specs=[*specs] + [VMEM] * (len(operands) - len(specs)),
        out_specs=jax.tree.map(lambda _: VMEM, outs),
        scratch_shapes=scratch,
        compiler_params=pltpu.CompilerParams(vmem_limit_bytes=24 * 2**20),
        cost_estimate=pl.CostEstimate(flops=flops, bytes_accessed=moved, transcendentals=0),
    )(*operands)


def tiled_body(patches, grad_embed, weight, straggler, decode, encode):
    count_dp, count_fsdp = lax.axis_size("dp"), lax.axis_size("fsdp")
    dp, me = lax.axis_index("dp"), lax.axis_index("fsdp")
    core = dp % 2
    place = jnp.stack([me, dp // 2, core])
    tokens, features = patches.shape
    columns = weight.shape[1]
    rows, depth, blocks = features // 2, features // count_dp, columns // LANES
    chunk = chunk_shape(rows, columns)
    bounds = [(0, blocks // 2), (blocks // 2, blocks)]

    def along_planes(block, step, replicas):
        pairs = [(d * 4 + f, d * 4 + (f ^ step(d % 2))) for d in replicas for f in range(4)]
        return lax.ppermute(block, ("dp", "fsdp"), pairs)

    with jax.named_scope("gather_weight"):
        first = along_planes(weight, lambda c: 1 + c, range(count_dp))

    with jax.named_scope("shares"):
        shares = encode * straggler[:, None] * decode[:, None]
        before = shifted(shares, "dp", 1)
    with jax.named_scope("send"):
        sent, left, held = call(
            functools.partial(send_kernel, depth),
            [
                jax.ShapeDtypeStruct((count_fsdp, *chunk), I16),
                jax.ShapeDtypeStruct((rows, tokens), BF16),
                jax.ShapeDtypeStruct((count_fsdp, tokens, columns), BF16),
            ],
            [place, in_hbm(patches), in_hbm(grad_embed), shares],
            [SMEM, HBM, HBM],
            [pltpu.VMEM(patches.shape, BF16), pltpu.SemaphoreType.DMA((count_fsdp + 1,))],
        )
    with jax.named_scope("own"):
        kept = call(
            own_kernel,
            jax.ShapeDtypeStruct((count_fsdp, blocks, rows, LANES), F32),
            [left, held],
            flops=10**11,
        )
        first, kept = lax.optimization_barrier((first, kept))
    with jax.named_scope("relay_weight"):
        second = exchange(first, "dp", 1)
    with jax.named_scope("pair"):
        came = exchange(sent, "dp", 1)
        before_sib = exchange(before, "dp", 1)
        outs = call(
            functools.partial(pair_kernel, bounds),
            [
                shape
                for lo, hi in bounds
                for shape in (
                    jax.ShapeDtypeStruct((2, hi - lo, rows, LANES), F32),
                    jax.ShapeDtypeStruct((2, *chunk_shape(rows, (hi - lo) * LANES)), I16),
                )
            ],
            [place, jnp.full((1,), tokens * count_fsdp, I32), kept, came, shares, before, before_sib],
            [SMEM] * 2,
            flops=10**11,
        )
        kept_parts = list(outs[::2])
        came_parts = [along_planes(sent, lambda c: 1 + c, range(count_dp)) for sent in outs[1::2]]
    with jax.named_scope("embed_near"):
        near = call(
            near_kernel,
            jax.ShapeDtypeStruct((3, tokens, columns), BF16),
            [place, patches, weight, first, second],
            [SMEM],
            flops=2 * 10**9,
        )
        near, came_parts[0] = lax.optimization_barrier((near, came_parts[0]))
    with jax.named_scope("steps"):
        for i, (lo, hi) in enumerate(bounds):
            kept_parts[i], sent = call(
                step_kernel,
                [
                    jax.ShapeDtypeStruct((hi - lo, rows, LANES), F32),
                    jax.ShapeDtypeStruct(chunk_shape(rows, (hi - lo) * LANES), I16),
                ],
                [kept_parts[i], came_parts[i]],
                flops=(0, 10**10)[i],
            )
            came_parts[i] = along_planes(sent, lambda c: 2 - c, range(count_dp))
    with jax.named_scope("middle"):
        done = call(
            merge_kernel,
            jax.ShapeDtypeStruct(kept_parts[0].shape, F32),
            [kept_parts[0], came_parts[0]],
            flops=10**10,
        )
        parts = call(
            functools.partial(middle_kernel, bounds[1][0], depth),
            [jax.ShapeDtypeStruct(chunk_shape(depth, columns), I16)] * (count_dp // 2),
            [place, done, kept_parts[1], came_parts[1]],
            [SMEM],
            [pltpu.VMEM((blocks, rows, LANES), F32)],
        )
        parts = [exchange(part, "dp", 2 * k) if k else part for k, part in enumerate(parts)]
    with jax.named_scope("relay_weight"):
        base, parts[0] = lax.optimization_barrier((first, parts[0]))
        far = along_planes(base, lambda c: 2 - c, range(count_dp))
    with jax.named_scope("embed"):
        near, parts[0] = lax.optimization_barrier((near, parts[0]))
        embedded = call(
            embed_kernel,
            jax.ShapeDtypeStruct((tokens, columns * count_fsdp), BF16),
            [place, patches, near, far],
            [SMEM],
            flops=10**10,
        )
    with jax.named_scope("last"):
        embedded, *parts = lax.optimization_barrier((embedded, *parts))
        decoded = call(last_kernel, jax.ShapeDtypeStruct((depth, columns), F32), parts)
    return embedded, decoded


def plain_body(patches, grad_embed, weight, straggler, decode, encode):
    shares = (straggler * decode)[:, None] * encode
    factor = (shares[:, 0] + shifted(shares[:, 1], "dp", 1))[0]
    scale = factor.astype(F32) / (patches.shape[0] * lax.axis_size("fsdp"))
    whole = lax.all_gather(weight, "fsdp", axis=1, tiled=True)
    embedded = times(patches, whole).astype(BF16)
    term = scale * times(grad_embed, patches, ((0,), (0,)))
    term = lax.psum_scatter(term, "fsdp", scatter_dimension=0, tiled=True)
    return embedded, lax.psum_scatter(term.T, "dp", scatter_dimension=0, tiled=True)


def body(patches, grad_embed, weight, straggler, decode, encode):
    fits = patches.shape[1] % (16 * lax.axis_size("dp")) == 0 and weight.shape[1] % LANES == 0
    fits = fits and lax.axis_size("fsdp") == 4
    run = tiled_body if fits else plain_body
    return run(patches, grad_embed, weight, straggler, decode, encode)


def solution(mesh):
    return jax.shard_map(
        body,
        mesh=mesh,
        in_specs=(
            P(("dp", "fsdp"), None),
            P(("dp", "fsdp"), None),
            P(None, "fsdp"),
            P("dp"),
            P("dp"),
            P("dp", None),
        ),
        out_specs=(P(("dp", "fsdp"), None), P("dp", "fsdp")),
        check_vma=False,
    )
```

```python
import functools
import math

import jax
import jax.numpy as jnp
from jax import lax
from jax.experimental import pallas as pl
from jax.experimental.pallas import tpu as pltpu
from jax.sharding import PartitionSpec as P

LANES = 128
TAIL = 16
STEP = math.log(2) / 16
TOP = 32760.0
F32, BF16, I16, I32 = jnp.float32, jnp.bfloat16, jnp.int16, jnp.int32
VMEM = pl.BlockSpec(memory_space=pltpu.VMEM)
SMEM = pl.BlockSpec(memory_space=pltpu.SMEM)
HBM = pl.BlockSpec(memory_space=pltpu.HBM)


def in_hbm(array):
    return pltpu.with_memory_space_constraint(array, pltpu.HBM)


def exchange(block, axis, step):
    return lax.ppermute(block, axis, [(i, i ^ step) for i in range(lax.axis_size(axis))])


def shifted(block, axis, distance):
    count = lax.axis_size(axis)
    return lax.ppermute(block, axis, [((i - distance) % count, i) for i in range(count)])


def times(a, b, dims=((1,), (0,))):
    return lax.dot_general(a, b, (dims, ((), ())), preferred_element_type=F32)


def chunk_shape(rows, columns):
    return (columns // LANES * rows + TAIL, LANES)


def put_chunk(ref, blocks, extra=()):
    rows = blocks[0].shape[0]
    tail = jnp.zeros((TAIL, LANES), I32)
    row = lax.broadcasted_iota(I32, (TAIL, LANES), 0)
    for j, block in enumerate(blocks):
        largest = jnp.max(jnp.abs(block), axis=0, keepdims=True)
        power = jnp.ceil(jnp.log(jnp.maximum(largest, 2.0**-100)) * (1 / STEP))
        coded = block * (TOP * jnp.exp(power * -STEP))
        ref[pl.ds(j * rows, rows), :] = coded.astype(I32).astype(I16)
        tail = jnp.where(row == j, power.astype(I32), tail)
    for j, number in enumerate(extra):
        tail = jnp.where(row == TAIL - len(extra) + j, number, tail)
    ref[pl.ds(len(blocks) * rows, TAIL), :] = tail.astype(I16)


def get_chunk(ref, rows):
    count = (ref.shape[0] - TAIL) // rows
    tail = ref[pl.ds(count * rows, TAIL), :].astype(F32)
    scale = jnp.exp(tail * STEP) * (1 / TOP)
    return [ref[pl.ds(j * rows, rows), :].astype(F32) * scale[j : j + 1, :] for j in range(count)], tail


def lanes(j):
    return slice(j * LANES, (j + 1) * LANES)


def send_kernel(depth, place, patches, grad_embed, shares, sent, left, held, p_held, arrived):
    me, core = place[0], place[2]
    count, _, columns = held.shape
    blocks, features = columns // LANES, patches.shape[1]
    rows = features // 2
    copies = [pltpu.make_async_copy(patches, p_held, arrived.at[count])]
    for k in range(count):
        here = pl.ds(pl.multiple_of((me ^ k) * columns, columns), columns)
        copies.append(pltpu.make_async_copy(grad_embed.at[:, here], held.at[k], arrived.at[k]))
    for copy in copies:
        copy.start()
    extra = shares[:, 0:1], shares[:, 1:2]
    i = lax.broadcasted_iota(I32, (features, features), 0)
    j = lax.broadcasted_iota(I32, (features, features), 1)
    half, i = i // rows, i % rows
    chosen = jnp.where(j == (i // depth * 2 + (core ^ half)) * depth + i % depth, 1.0, 0.0).astype(BF16)
    copies[0].wait()
    turned = times(chosen, p_held[...], ((1,), (1,))).astype(BF16)
    left[...] = turned[:rows]
    for k in range(count):
        copies[1 + k].wait()
        value = times(turned[rows:], held[k])
        put_chunk(sent.at[k], [value[:, lanes(j)] for j in range(blocks)], extra)


def own_kernel(left, held, kept):
    for k in range(kept.shape[0]):
        value = times(left[...], held[k])
        for j in range(kept.shape[1]):
            kept[k, j] = value[:, lanes(j)]


def pair_kernel(bounds, place, tokens, kept, came, shares, before, before_sib, *outs):
    core = place[2]
    rows = kept.shape[2]
    first, second = shares[:, 0:1].astype(F32), shares[:, 1:2].astype(F32)
    tail = get_chunk(came.at[0], rows)[1]
    first_sib, second_sib = (tail[TAIL - 2 + j : TAIL - 1 + j, 0:1] for j in range(2))
    even = core == 0
    carried = jnp.where(even, before[:, 1:2], before_sib[:, 1:2]).astype(F32)
    scale = (first + jnp.where(even, carried, second_sib)) / tokens[0].astype(F32)
    scale_sib = (first_sib + jnp.where(even, second, carried)) / tokens[0].astype(F32)
    for (lo, hi), still, sent in zip(bounds, outs[::2], outs[1::2]):

        def value(k):
            parts, _ = get_chunk(came.at[k], rows)
            return [scale * kept[k, j] + scale_sib * parts[j] for j in range(lo, hi)]

        put_chunk(sent.at[0], value(1 + core))
        put_chunk(sent.at[1], value(3))
        for at, k in enumerate((0, 2 - core)):
            for j, part in enumerate(value(k)):
                still[at, j] = part


def step_kernel(kept, came, still, sent):
    _, blocks, rows, _ = kept.shape
    parts, _ = get_chunk(came.at[1], rows)
    put_chunk(sent, [kept[1, j] + part for j, part in enumerate(parts)])
    for j, part in enumerate(get_chunk(came.at[0], rows)[0]):
        still[j] = kept[0, j] + part


def merge_kernel(kept, came, out):
    for j, part in enumerate(get_chunk(came, kept.shape[1])[0]):
        out[j] = kept[j] + part


def middle_kernel(split, depth, place, done, kept, came, *refs):
    *outs, held = refs
    blocks, rows, _ = held.shape
    held[:split] = done[...]
    for j, part in enumerate(get_chunk(came, rows)[0]):
        held[split + j] = kept[j] + part
    for k, out in enumerate(outs):
        here = pl.ds(pl.multiple_of((place[1] ^ k) * depth, depth), depth)
        put_chunk(out, [held[j, here, :] for j in range(blocks)])


def last_kernel(*refs):
    *ins, out = refs
    parts = [get_chunk(ref, out.shape[0])[0] for ref in ins]
    for j, terms in enumerate(zip(*parts)):
        out[:, lanes(j)] = sum(terms[1:], terms[0])


def half_kernel(place, first, half):
    rows = half.shape[0]
    half[...] = first[pl.ds(pl.multiple_of(place[2] * rows, rows), rows), :]


def near_kernel(place, patches, own, first, second, out):
    core = place[2]
    for k, weight in ((1 + core, first), (2 - core, second), (0, own)):
        out[k] = times(patches[...], weight[...]).astype(BF16)


def embed_kernel(place, patches, near, far, far_sib, out, halves):
    me, core, columns = place[0], place[2], near.shape[2]
    rows = far.shape[0]

    def put(k, value):
        out[:, pl.ds(pl.multiple_of((me ^ k) * columns, columns), columns)] = value

    halves[0] = patches[:, :rows]
    halves[1] = patches[:, rows:]
    put(3, (times(halves[core], far[...]) + times(halves[1 - core], far_sib[...])).astype(BF16))
    for k in range(3):
        put(k, near[k])


def call(kernel, outs, operands, specs=(), scratch=(), flops=0):
    moved = sum(math.prod(a.shape) * a.dtype.itemsize for a in [*operands, *jax.tree.leaves(outs)]) if flops else 0
    return pl.pallas_call(
        kernel,
        out_shape=outs,
        in_specs=[*specs] + [VMEM] * (len(operands) - len(specs)),
        out_specs=jax.tree.map(lambda _: VMEM, outs),
        scratch_shapes=scratch,
        compiler_params=pltpu.CompilerParams(vmem_limit_bytes=24 * 2**20),
        cost_estimate=pl.CostEstimate(flops=flops, bytes_accessed=moved, transcendentals=0),
    )(*operands)


def tiled_body(patches, grad_embed, weight, straggler, decode, encode):
    count_dp, count_fsdp = lax.axis_size("dp"), lax.axis_size("fsdp")
    dp, me = lax.axis_index("dp"), lax.axis_index("fsdp")
    core = dp % 2
    place = jnp.stack([me, dp // 2, core])
    tokens, features = patches.shape
    columns = weight.shape[1]
    rows, depth, blocks = features // 2, features // count_dp, columns // LANES
    chunk = chunk_shape(rows, columns)
    bounds = [(0, 2 * blocks // 3), (2 * blocks // 3, blocks)]

    def along_planes(block, step, replicas):
        pairs = [(d * 4 + f, d * 4 + (f ^ step(d % 2))) for d in replicas for f in range(4)]
        return lax.ppermute(block, ("dp", "fsdp"), pairs)

    with jax.named_scope("gather_weight"):
        first = along_planes(weight, lambda c: 1 + c, range(count_dp))

    with jax.named_scope("shares"):
        shares = encode * straggler[:, None] * decode[:, None]
        before = shifted(shares, "dp", 1)
    with jax.named_scope("send"):
        sent, left, held = call(
            functools.partial(send_kernel, depth),
            [
                jax.ShapeDtypeStruct((count_fsdp, *chunk), I16),
                jax.ShapeDtypeStruct((rows, tokens), BF16),
                jax.ShapeDtypeStruct((count_fsdp, tokens, columns), BF16),
            ],
            [place, in_hbm(patches), in_hbm(grad_embed), shares],
            [SMEM, HBM, HBM],
            [pltpu.VMEM(patches.shape, BF16), pltpu.SemaphoreType.DMA((count_fsdp + 1,))],
        )
    with jax.named_scope("own"):
        kept = call(
            own_kernel,
            jax.ShapeDtypeStruct((count_fsdp, blocks, rows, LANES), F32),
            [left, held],
            flops=10**11,
        )
        first, kept = lax.optimization_barrier((first, kept))
    with jax.named_scope("relay_weight"):
        second = exchange(first, "dp", 1)
    with jax.named_scope("pair"):
        came = exchange(sent, "dp", 1)
        before_sib = exchange(before, "dp", 1)
        outs = call(
            functools.partial(pair_kernel, bounds),
            [
                shape
                for lo, hi in bounds
                for shape in (
                    jax.ShapeDtypeStruct((2, hi - lo, rows, LANES), F32),
                    jax.ShapeDtypeStruct((2, *chunk_shape(rows, (hi - lo) * LANES)), I16),
                )
            ],
            [place, jnp.full((1,), tokens * count_fsdp, I32), kept, came, shares, before, before_sib],
            [SMEM] * 2,
            flops=10**11,
        )
        kept_parts = list(outs[::2])
        came_parts = [along_planes(sent, lambda c: 1 + c, range(count_dp)) for sent in outs[1::2]]
    with jax.named_scope("embed_near"):
        half = call(
            half_kernel,
            jax.ShapeDtypeStruct((rows, columns), BF16),
            [place, first],
            [SMEM],
        )
        half, kept_parts[0] = lax.optimization_barrier((half, kept_parts[0]))
        far = along_planes(half, lambda c: 2 - c, range(count_dp))
        near = call(
            near_kernel,
            jax.ShapeDtypeStruct((3, tokens, columns), BF16),
            [place, patches, weight, first, second],
            [SMEM],
            flops=2 * 10**9,
        )
        near, came_parts[0] = lax.optimization_barrier((near, came_parts[0]))
    with jax.named_scope("steps"):
        for i, (lo, hi) in enumerate(bounds):
            kept_parts[i], sent = call(
                step_kernel,
                [
                    jax.ShapeDtypeStruct((hi - lo, rows, LANES), F32),
                    jax.ShapeDtypeStruct(chunk_shape(rows, (hi - lo) * LANES), I16),
                ],
                [kept_parts[i], came_parts[i]],
                flops=(0, 10**10)[i],
            )
            came_parts[i] = along_planes(sent, lambda c: 2 - c, range(count_dp))
    with jax.named_scope("relay_weight"):
        far, kept_parts[1] = lax.optimization_barrier((far, kept_parts[1]))
        far_sib = exchange(far, "dp", 1)
    with jax.named_scope("middle"):
        done = call(
            merge_kernel,
            jax.ShapeDtypeStruct(kept_parts[0].shape, F32),
            [kept_parts[0], came_parts[0]],
            flops=10**10,
        )
        parts = call(
            functools.partial(middle_kernel, bounds[1][0], depth),
            [jax.ShapeDtypeStruct(chunk_shape(depth, columns), I16)] * (count_dp // 2),
            [place, done, kept_parts[1], came_parts[1]],
            [SMEM],
            [pltpu.VMEM((blocks, rows, LANES), F32)],
        )
        parts = [exchange(part, "dp", 2 * k) if k else part for k, part in enumerate(parts)]
    with jax.named_scope("embed"):
        near, parts[0] = lax.optimization_barrier((near, parts[0]))
        embedded = call(
            embed_kernel,
            jax.ShapeDtypeStruct((tokens, columns * count_fsdp), BF16),
            [place, patches, near, far, far_sib],
            [SMEM],
            [pltpu.VMEM((2, tokens, rows), BF16)],
            flops=10**10,
        )
    with jax.named_scope("last"):
        embedded, *parts = lax.optimization_barrier((embedded, *parts))
        decoded = call(last_kernel, jax.ShapeDtypeStruct((depth, columns), F32), parts)
    return embedded, decoded


def plain_body(patches, grad_embed, weight, straggler, decode, encode):
    shares = (straggler * decode)[:, None] * encode
    factor = (shares[:, 0] + shifted(shares[:, 1], "dp", 1))[0]
    scale = factor.astype(F32) / (patches.shape[0] * lax.axis_size("fsdp"))
    whole = lax.all_gather(weight, "fsdp", axis=1, tiled=True)
    embedded = times(patches, whole).astype(BF16)
    term = scale * times(grad_embed, patches, ((0,), (0,)))
    term = lax.psum_scatter(term, "fsdp", scatter_dimension=0, tiled=True)
    return embedded, lax.psum_scatter(term.T, "dp", scatter_dimension=0, tiled=True)


def body(patches, grad_embed, weight, straggler, decode, encode):
    fits = patches.shape[1] % (16 * lax.axis_size("dp")) == 0 and weight.shape[1] % LANES == 0
    fits = fits and lax.axis_size("fsdp") == 4
    run = tiled_body if fits else plain_body
    return run(patches, grad_embed, weight, straggler, decode, encode)


def solution(mesh):
    return jax.shard_map(
        body,
        mesh=mesh,
        in_specs=(
            P(("dp", "fsdp"), None),
            P(("dp", "fsdp"), None),
            P(None, "fsdp"),
            P("dp"),
            P("dp"),
            P("dp", None),
        ),
        out_specs=(P(("dp", "fsdp"), None), P("dp", "fsdp")),
        check_vma=False,
    )
```

```python
import functools
import math

import jax
import jax.numpy as jnp
from jax import lax
from jax.experimental import pallas as pl
from jax.experimental.pallas import tpu as pltpu
from jax.sharding import PartitionSpec as P

LANES = 128
TAIL = 16
STEP = math.log(2) / 16
TOP = 32760.0
F32, BF16, I16, I32 = jnp.float32, jnp.bfloat16, jnp.int16, jnp.int32
VMEM = pl.BlockSpec(memory_space=pltpu.VMEM)
SMEM = pl.BlockSpec(memory_space=pltpu.SMEM)
HBM = pl.BlockSpec(memory_space=pltpu.HBM)


def in_hbm(array):
    return pltpu.with_memory_space_constraint(array, pltpu.HBM)


def exchange(block, axis, step):
    return lax.ppermute(block, axis, [(i, i ^ step) for i in range(lax.axis_size(axis))])


def shifted(block, axis, distance):
    count = lax.axis_size(axis)
    return lax.ppermute(block, axis, [((i - distance) % count, i) for i in range(count)])


def times(a, b, dims=((1,), (0,))):
    return lax.dot_general(a, b, (dims, ((), ())), preferred_element_type=F32)


def chunk_shape(rows, columns):
    return (columns // LANES * rows + TAIL, LANES)


def put_chunk(ref, blocks, extra=()):
    rows = blocks[0].shape[0]
    tail = jnp.zeros((TAIL, LANES), I32)
    row = lax.broadcasted_iota(I32, (TAIL, LANES), 0)
    for j, block in enumerate(blocks):
        largest = jnp.max(jnp.abs(block), axis=0, keepdims=True)
        power = jnp.ceil(jnp.log(jnp.maximum(largest, 2.0**-100)) * (1 / STEP))
        coded = block * (TOP * jnp.exp(power * -STEP))
        ref[pl.ds(j * rows, rows), :] = coded.astype(I32).astype(I16)
        tail = jnp.where(row == j, power.astype(I32), tail)
    for j, number in enumerate(extra):
        tail = jnp.where(row == TAIL - len(extra) + j, number, tail)
    ref[pl.ds(len(blocks) * rows, TAIL), :] = tail.astype(I16)


def get_chunk(ref, rows):
    count = (ref.shape[0] - TAIL) // rows
    tail = ref[pl.ds(count * rows, TAIL), :].astype(F32)
    scale = jnp.exp(tail * STEP) * (1 / TOP)
    return [ref[pl.ds(j * rows, rows), :].astype(F32) * scale[j : j + 1, :] for j in range(count)], tail


def lanes(j):
    return slice(j * LANES, (j + 1) * LANES)


def send_kernel(depth, place, patches, grad_embed, shares, sent, left, held, p_held, arrived):
    me, core = place[0], place[2]
    count, _, columns = held.shape
    blocks, features = columns // LANES, patches.shape[1]
    rows = features // 2
    copies = [pltpu.make_async_copy(patches, p_held, arrived.at[count])]
    for k in range(count):
        here = pl.ds(pl.multiple_of((me ^ k) * columns, columns), columns)
        copies.append(pltpu.make_async_copy(grad_embed.at[:, here], held.at[k], arrived.at[k]))
    for copy in copies:
        copy.start()
    extra = shares[:, 0:1], shares[:, 1:2]
    i = lax.broadcasted_iota(I32, (features, features), 0)
    j = lax.broadcasted_iota(I32, (features, features), 1)
    half, i = i // rows, i % rows
    chosen = jnp.where(j == (i // depth * 2 + (core ^ half)) * depth + i % depth, 1.0, 0.0).astype(BF16)
    copies[0].wait()
    turned = times(chosen, p_held[...], ((1,), (1,))).astype(BF16)
    left[...] = turned[:rows]
    for k in range(count):
        copies[1 + k].wait()
        value = times(turned[rows:], held[k])
        put_chunk(sent.at[k], [value[:, lanes(j)] for j in range(blocks)], extra)


def own_kernel(left, held, kept):
    for k in range(kept.shape[0]):
        value = times(left[...], held[k])
        for j in range(kept.shape[1]):
            kept[k, j] = value[:, lanes(j)]


def pair_kernel(bounds, place, tokens, kept, came, shares, before, before_sib, *outs):
    core = place[2]
    rows = kept.shape[2]
    first, second = shares[:, 0:1].astype(F32), shares[:, 1:2].astype(F32)
    tail = get_chunk(came.at[0], rows)[1]
    first_sib, second_sib = (tail[TAIL - 2 + j : TAIL - 1 + j, 0:1] for j in range(2))
    even = core == 0
    carried = jnp.where(even, before[:, 1:2], before_sib[:, 1:2]).astype(F32)
    scale = (first + jnp.where(even, carried, second_sib)) / tokens[0].astype(F32)
    scale_sib = (first_sib + jnp.where(even, second, carried)) / tokens[0].astype(F32)
    for (lo, hi), still, sent in zip(bounds, outs[::2], outs[1::2]):

        def value(k):
            parts, _ = get_chunk(came.at[k], rows)
            return [scale * kept[k, j] + scale_sib * parts[j] for j in range(lo, hi)]

        put_chunk(sent.at[0], value(1 + core))
        put_chunk(sent.at[1], value(3))
        for at, k in enumerate((0, 2 - core)):
            for j, part in enumerate(value(k)):
                still[at, j] = part


def step_kernel(kept, came, still, sent):
    _, blocks, rows, _ = kept.shape
    parts, _ = get_chunk(came.at[1], rows)
    put_chunk(sent, [kept[1, j] + part for j, part in enumerate(parts)])
    for j, part in enumerate(get_chunk(came.at[0], rows)[0]):
        still[j] = kept[0, j] + part


def early_kernel(depth, place, kept, came, done, *outs):
    for j, part in enumerate(get_chunk(came, kept.shape[1])[0]):
        done[j] = kept[j] + part
    for k, out in enumerate(outs):
        here = pl.ds(pl.multiple_of((place[1] ^ k) * depth, depth), depth)
        put_chunk(out, [done[j, here, :] for j in range(done.shape[0])])


def middle_kernel(depth, place, done, kept, came, whole, *refs):
    *outs, held = refs
    blocks, rows, _ = held.shape
    split = done.shape[0]
    held[:split] = done[...]
    for j, part in enumerate(get_chunk(came, rows)[0]):
        held[split + j] = kept[j] + part
    for k, out in enumerate([*outs, whole]):
        here = pl.ds(pl.multiple_of((place[1] ^ k) * depth, depth), depth)
        put_chunk(out, [held[j, here, :] for j in range(0 if out is whole else split, blocks)])


def last_kernel(whole, *refs):
    *ins, out = refs
    early, late = ins[: len(ins) // 2], ins[len(ins) // 2 :]
    total = get_chunk(whole, out.shape[0])[0]
    for a, b in zip(early, late):
        parts = get_chunk(a, out.shape[0])[0] + get_chunk(b, out.shape[0])[0]
        total = [x + y for x, y in zip(total, parts)]
    for j, part in enumerate(total):
        out[:, lanes(j)] = part


def half_kernel(place, first, half):
    rows = half.shape[0]
    half[...] = first[pl.ds(pl.multiple_of(place[2] * rows, rows), rows), :]


def near_kernel(place, patches, own, first, second, out):
    core = place[2]
    for k, weight in ((1 + core, first), (2 - core, second), (0, own)):
        out[k] = times(patches[...], weight[...]).astype(BF16)


def embed_kernel(place, patches, near, far, far_sib, out, halves):
    me, core, columns = place[0], place[2], near.shape[2]
    rows = far.shape[0]

    def put(k, value):
        out[:, pl.ds(pl.multiple_of((me ^ k) * columns, columns), columns)] = value

    halves[0] = patches[:, :rows]
    halves[1] = patches[:, rows:]
    put(3, (times(halves[core], far[...]) + times(halves[1 - core], far_sib[...])).astype(BF16))
    for k in range(3):
        put(k, near[k])


def call(kernel, outs, operands, specs=(), scratch=(), flops=0):
    moved = sum(math.prod(a.shape) * a.dtype.itemsize for a in [*operands, *jax.tree.leaves(outs)]) if flops else 0
    return pl.pallas_call(
        kernel,
        out_shape=outs,
        in_specs=[*specs] + [VMEM] * (len(operands) - len(specs)),
        out_specs=jax.tree.map(lambda _: VMEM, outs),
        scratch_shapes=scratch,
        compiler_params=pltpu.CompilerParams(vmem_limit_bytes=24 * 2**20),
        cost_estimate=pl.CostEstimate(flops=flops, bytes_accessed=moved, transcendentals=0),
    )(*operands)


def tiled_body(patches, grad_embed, weight, straggler, decode, encode):
    count_dp, count_fsdp = lax.axis_size("dp"), lax.axis_size("fsdp")
    dp, me = lax.axis_index("dp"), lax.axis_index("fsdp")
    core = dp % 2
    place = jnp.stack([me, dp // 2, core])
    tokens, features = patches.shape
    columns = weight.shape[1]
    rows, depth, blocks = features // 2, features // count_dp, columns // LANES
    chunk = chunk_shape(rows, columns)
    bounds = [(0, 2 * blocks // 3), (2 * blocks // 3, blocks)]

    def along_planes(block, step, replicas):
        pairs = [(d * 4 + f, d * 4 + (f ^ step(d % 2))) for d in replicas for f in range(4)]
        return lax.ppermute(block, ("dp", "fsdp"), pairs)

    with jax.named_scope("gather_weight"):
        first = along_planes(weight, lambda c: 1 + c, range(count_dp))

    with jax.named_scope("shares"):
        shares = encode * straggler[:, None] * decode[:, None]
        before = shifted(shares, "dp", 1)
    with jax.named_scope("send"):
        sent, left, held = call(
            functools.partial(send_kernel, depth),
            [
                jax.ShapeDtypeStruct((count_fsdp, *chunk), I16),
                jax.ShapeDtypeStruct((rows, tokens), BF16),
                jax.ShapeDtypeStruct((count_fsdp, tokens, columns), BF16),
            ],
            [place, in_hbm(patches), in_hbm(grad_embed), shares],
            [SMEM, HBM, HBM],
            [pltpu.VMEM(patches.shape, BF16), pltpu.SemaphoreType.DMA((count_fsdp + 1,))],
        )
    with jax.named_scope("own"):
        kept = call(
            own_kernel,
            jax.ShapeDtypeStruct((count_fsdp, blocks, rows, LANES), F32),
            [left, held],
            flops=10**11,
        )
        first, kept = lax.optimization_barrier((first, kept))
    with jax.named_scope("relay_weight"):
        second = exchange(first, "dp", 1)
    with jax.named_scope("pair"):
        came = exchange(sent, "dp", 1)
        before_sib = exchange(before, "dp", 1)
        outs = call(
            functools.partial(pair_kernel, bounds),
            [
                shape
                for lo, hi in bounds
                for shape in (
                    jax.ShapeDtypeStruct((2, hi - lo, rows, LANES), F32),
                    jax.ShapeDtypeStruct((2, *chunk_shape(rows, (hi - lo) * LANES)), I16),
                )
            ],
            [place, jnp.full((1,), tokens * count_fsdp, I32), kept, came, shares, before, before_sib],
            [SMEM] * 2,
            flops=10**11,
        )
        kept_parts = list(outs[::2])
        came_parts = [along_planes(sent, lambda c: 1 + c, range(count_dp)) for sent in outs[1::2]]
    with jax.named_scope("embed_near"):
        half = call(
            half_kernel,
            jax.ShapeDtypeStruct((rows, columns), BF16),
            [place, first],
            [SMEM],
        )
        half, kept_parts[0] = lax.optimization_barrier((half, kept_parts[0]))
        far = along_planes(half, lambda c: 2 - c, range(count_dp))
        near = call(
            near_kernel,
            jax.ShapeDtypeStruct((3, tokens, columns), BF16),
            [place, patches, weight, first, second],
            [SMEM],
            flops=2 * 10**9,
        )
        near, came_parts[0] = lax.optimization_barrier((near, came_parts[0]))
    with jax.named_scope("steps"):
        for i, (lo, hi) in enumerate(bounds):
            kept_parts[i], sent = call(
                step_kernel,
                [
                    jax.ShapeDtypeStruct((hi - lo, rows, LANES), F32),
                    jax.ShapeDtypeStruct(chunk_shape(rows, (hi - lo) * LANES), I16),
                ],
                [kept_parts[i], came_parts[i]],
                flops=(0, 10**10)[i],
            )
            came_parts[i] = along_planes(sent, lambda c: 2 - c, range(count_dp))
    with jax.named_scope("relay_weight"):
        far, kept_parts[1] = lax.optimization_barrier((far, kept_parts[1]))
        far_sib = exchange(far, "dp", 1)
    with jax.named_scope("middle"):
        chips, split = count_dp // 2, bounds[0][1]
        done, *early = call(
            functools.partial(early_kernel, depth),
            [jax.ShapeDtypeStruct(kept_parts[0].shape, F32)]
            + [jax.ShapeDtypeStruct(chunk_shape(depth, split * LANES), I16)] * (chips - 1),
            [place, kept_parts[0], came_parts[0]],
            [SMEM],
            flops=10**10,
        )
        early = [exchange(part, "dp", 2 * k) if k else part for k, part in enumerate(early)]
        came_parts[1], early[1] = lax.optimization_barrier((came_parts[1], early[1]))
        parts = call(
            functools.partial(middle_kernel, depth),
            [jax.ShapeDtypeStruct(chunk_shape(depth, columns), I16)]
            + [jax.ShapeDtypeStruct(chunk_shape(depth, columns - split * LANES), I16)] * (chips - 1),
            [place, done, kept_parts[1], came_parts[1]],
            [SMEM],
            [pltpu.VMEM((blocks, rows, LANES), F32)],
            flops=10**10,
        )
        whole = exchange(parts[0], "dp", 2 * (chips - 1))
        parts = [exchange(part, "dp", 2 * k) if k else part for k, part in enumerate(parts[1:])]
    with jax.named_scope("embed"):
        near, parts[0] = lax.optimization_barrier((near, parts[0]))
        embedded = call(
            embed_kernel,
            jax.ShapeDtypeStruct((tokens, columns * count_fsdp), BF16),
            [place, patches, near, far, far_sib],
            [SMEM],
            [pltpu.VMEM((2, tokens, rows), BF16)],
            flops=10**10,
        )
    with jax.named_scope("last"):
        embedded, whole = lax.optimization_barrier((embedded, whole))
        decoded = call(last_kernel, jax.ShapeDtypeStruct((depth, columns), F32), [whole, *early, *parts])
    return embedded, decoded


def plain_body(patches, grad_embed, weight, straggler, decode, encode):
    shares = (straggler * decode)[:, None] * encode
    factor = (shares[:, 0] + shifted(shares[:, 1], "dp", 1))[0]
    scale = factor.astype(F32) / (patches.shape[0] * lax.axis_size("fsdp"))
    whole = lax.all_gather(weight, "fsdp", axis=1, tiled=True)
    embedded = times(patches, whole).astype(BF16)
    term = scale * times(grad_embed, patches, ((0,), (0,)))
    term = lax.psum_scatter(term, "fsdp", scatter_dimension=0, tiled=True)
    return embedded, lax.psum_scatter(term.T, "dp", scatter_dimension=0, tiled=True)


def body(patches, grad_embed, weight, straggler, decode, encode):
    fits = patches.shape[1] % (16 * lax.axis_size("dp")) == 0 and weight.shape[1] % LANES == 0
    fits = fits and lax.axis_size("fsdp") == 4
    run = tiled_body if fits else plain_body
    return run(patches, grad_embed, weight, straggler, decode, encode)


def solution(mesh):
    return jax.shard_map(
        body,
        mesh=mesh,
        in_specs=(
            P(("dp", "fsdp"), None),
            P(("dp", "fsdp"), None),
            P(None, "fsdp"),
            P("dp"),
            P("dp"),
            P("dp", None),
        ),
        out_specs=(P(("dp", "fsdp"), None), P("dp", "fsdp")),
        check_vma=False,
    )
```

```python
import functools
import math

import jax
import jax.numpy as jnp
from jax import lax
from jax.experimental import pallas as pl
from jax.experimental.pallas import tpu as pltpu
from jax.sharding import PartitionSpec as P

LANES = 128
TAIL = 16
STEP = math.log(2) / 16
TOP = 32760.0
F32, BF16, I16, I32 = jnp.float32, jnp.bfloat16, jnp.int16, jnp.int32
VMEM = pl.BlockSpec(memory_space=pltpu.VMEM)
SMEM = pl.BlockSpec(memory_space=pltpu.SMEM)
HBM = pl.BlockSpec(memory_space=pltpu.HBM)


def in_hbm(array):
    return pltpu.with_memory_space_constraint(array, pltpu.HBM)


def exchange(block, axis, step):
    return lax.ppermute(block, axis, [(i, i ^ step) for i in range(lax.axis_size(axis))])


def shifted(block, axis, distance):
    count = lax.axis_size(axis)
    return lax.ppermute(block, axis, [((i - distance) % count, i) for i in range(count)])


def times(a, b, dims=((1,), (0,))):
    return lax.dot_general(a, b, (dims, ((), ())), preferred_element_type=F32)


def chunk_shape(rows, columns):
    return (columns // LANES * rows + TAIL, LANES)


def put_chunk(ref, blocks, extra=()):
    rows = blocks[0].shape[0]
    tail = jnp.zeros((TAIL, LANES), I32)
    row = lax.broadcasted_iota(I32, (TAIL, LANES), 0)
    for j, block in enumerate(blocks):
        largest = jnp.max(jnp.abs(block), axis=0, keepdims=True)
        power = jnp.ceil(jnp.log(jnp.maximum(largest, 2.0**-100)) * (1 / STEP))
        coded = block * (TOP * jnp.exp(power * -STEP))
        ref[pl.ds(j * rows, rows), :] = coded.astype(I32).astype(I16)
        tail = jnp.where(row == j, power.astype(I32), tail)
    for j, number in enumerate(extra):
        tail = jnp.where(row == TAIL - len(extra) + j, number, tail)
    ref[pl.ds(len(blocks) * rows, TAIL), :] = tail.astype(I16)


def get_chunk(ref, rows):
    count = (ref.shape[0] - TAIL) // rows
    tail = ref[pl.ds(count * rows, TAIL), :].astype(F32)
    scale = jnp.exp(tail * STEP) * (1 / TOP)
    return [ref[pl.ds(j * rows, rows), :].astype(F32) * scale[j : j + 1, :] for j in range(count)], tail


def lanes(j):
    return slice(j * LANES, (j + 1) * LANES)


def send_kernel(depth, place, patches, grad_embed, shares, sent, left, held, p_held, arrived):
    me, core = place[0], place[2]
    count, _, columns = held.shape
    blocks, features = columns // LANES, patches.shape[1]
    rows = features // 2
    copies = [pltpu.make_async_copy(patches, p_held, arrived.at[count])]
    for k in range(count):
        here = pl.ds(pl.multiple_of((me ^ k) * columns, columns), columns)
        copies.append(pltpu.make_async_copy(grad_embed.at[:, here], held.at[k], arrived.at[k]))
    for copy in copies:
        copy.start()
    extra = shares[:, 0:1], shares[:, 1:2]
    i = lax.broadcasted_iota(I32, (features, features), 0)
    j = lax.broadcasted_iota(I32, (features, features), 1)
    half, i = i // rows, i % rows
    chosen = jnp.where(j == (i // depth * 2 + (core ^ half)) * depth + i % depth, 1.0, 0.0).astype(BF16)
    copies[0].wait()
    turned = times(chosen, p_held[...], ((1,), (1,))).astype(BF16)
    left[...] = turned[:rows]
    for k in range(count):
        copies[1 + k].wait()
        value = times(turned[rows:], held[k])
        put_chunk(sent.at[k], [value[:, lanes(j)] for j in range(blocks)], extra)


def own_kernel(left, held, kept):
    for k in range(kept.shape[0]):
        value = times(left[...], held[k])
        for j in range(kept.shape[1]):
            kept[k, j] = value[:, lanes(j)]


def pair_kernel(bounds, place, tokens, kept, came, shares, before, before_sib, *outs):
    core = place[2]
    rows = kept.shape[2]
    first, second = shares[:, 0:1].astype(F32), shares[:, 1:2].astype(F32)
    tail = get_chunk(came.at[0], rows)[1]
    first_sib, second_sib = (tail[TAIL - 2 + j : TAIL - 1 + j, 0:1] for j in range(2))
    even = core == 0
    carried = jnp.where(even, before[:, 1:2], before_sib[:, 1:2]).astype(F32)
    scale = (first + jnp.where(even, carried, second_sib)) / tokens[0].astype(F32)
    scale_sib = (first_sib + jnp.where(even, second, carried)) / tokens[0].astype(F32)
    for (lo, hi), still, sent in zip(bounds, outs[::2], outs[1::2]):

        def value(k):
            parts, _ = get_chunk(came.at[k], rows)
            return [scale * kept[k, j] + scale_sib * parts[j] for j in range(lo, hi)]

        put_chunk(sent.at[0], value(1 + core))
        put_chunk(sent.at[1], value(3))
        for at, k in enumerate((0, 2 - core)):
            for j, part in enumerate(value(k)):
                still[at, j] = part


def step_kernel(kept, came, still, sent):
    _, blocks, rows, _ = kept.shape
    parts, _ = get_chunk(came.at[1], rows)
    put_chunk(sent, [kept[1, j] + part for j, part in enumerate(parts)])
    for j, part in enumerate(get_chunk(came.at[0], rows)[0]):
        still[j] = kept[0, j] + part


def merge_kernel(kept, came, out):
    for j, part in enumerate(get_chunk(came, kept.shape[1])[0]):
        out[j] = kept[j] + part


def middle_kernel(split, depth, place, done, kept, came, *refs):
    *outs, held = refs
    blocks, rows, _ = held.shape
    held[:split] = done[...]
    for j, part in enumerate(get_chunk(came, rows)[0]):
        held[split + j] = kept[j] + part
    for k, out in enumerate(outs):
        here = pl.ds(pl.multiple_of((place[1] ^ k) * depth, depth), depth)
        put_chunk(out, [held[j, here, :] for j in range(blocks)])


def last_kernel(*refs):
    *ins, out = refs
    parts = [get_chunk(ref, out.shape[0])[0] for ref in ins]
    for j, terms in enumerate(zip(*parts)):
        out[:, lanes(j)] = sum(terms[1:], terms[0])


def half_kernel(place, first, half):
    rows = half.shape[0]
    half[...] = first[pl.ds(pl.multiple_of(place[2] * rows, rows), rows), :]


def near_kernel(place, patches, own, first, second, out):
    core = place[2]
    for k, weight in ((1 + core, first), (2 - core, second), (0, own)):
        out[k] = times(patches[...], weight[...]).astype(BF16)


def embed_kernel(place, patches, near, far, far_sib, out, halves):
    me, core, columns = place[0], place[2], near.shape[2]
    rows = far.shape[0]

    def put(k, value):
        out[:, pl.ds(pl.multiple_of((me ^ k) * columns, columns), columns)] = value

    halves[0] = patches[:, :rows]
    halves[1] = patches[:, rows:]
    put(3, (times(halves[core], far[...]) + times(halves[1 - core], far_sib[...])).astype(BF16))
    for k in range(3):
        put(k, near[k])


def call(kernel, outs, operands, specs=(), scratch=(), flops=0):
    moved = sum(math.prod(a.shape) * a.dtype.itemsize for a in [*operands, *jax.tree.leaves(outs)]) if flops else 0
    return pl.pallas_call(
        kernel,
        out_shape=outs,
        in_specs=[*specs] + [VMEM] * (len(operands) - len(specs)),
        out_specs=jax.tree.map(lambda _: VMEM, outs),
        scratch_shapes=scratch,
        compiler_params=pltpu.CompilerParams(vmem_limit_bytes=24 * 2**20),
        cost_estimate=pl.CostEstimate(flops=flops, bytes_accessed=moved, transcendentals=0),
    )(*operands)


def tiled_body(patches, grad_embed, weight, straggler, decode, encode):
    count_dp, count_fsdp = lax.axis_size("dp"), lax.axis_size("fsdp")
    dp, me = lax.axis_index("dp"), lax.axis_index("fsdp")
    core = dp % 2
    place = jnp.stack([me, dp // 2, core])
    tokens, features = patches.shape
    columns = weight.shape[1]
    rows, depth, blocks = features // 2, features // count_dp, columns // LANES
    chunk = chunk_shape(rows, columns)
    bounds = [(0, 2 * blocks // 3), (2 * blocks // 3, blocks)]

    def along_planes(block, step, replicas):
        pairs = [(d * 4 + f, d * 4 + (f ^ step(d % 2))) for d in replicas for f in range(4)]
        return lax.ppermute(block, ("dp", "fsdp"), pairs)

    with jax.named_scope("gather_weight"):
        first = along_planes(weight, lambda c: 1 + c, range(count_dp))

    with jax.named_scope("shares"):
        shares = encode * straggler[:, None] * decode[:, None]
        before = shifted(shares, "dp", 1)
    with jax.named_scope("send"):
        sent, left, held = call(
            functools.partial(send_kernel, depth),
            [
                jax.ShapeDtypeStruct((count_fsdp, *chunk), I16),
                jax.ShapeDtypeStruct((rows, tokens), BF16),
                jax.ShapeDtypeStruct((count_fsdp, tokens, columns), BF16),
            ],
            [place, in_hbm(patches), in_hbm(grad_embed), shares],
            [SMEM, HBM, HBM],
            [pltpu.VMEM(patches.shape, BF16), pltpu.SemaphoreType.DMA((count_fsdp + 1,))],
        )
    with jax.named_scope("own"):
        kept = call(
            own_kernel,
            jax.ShapeDtypeStruct((count_fsdp, blocks, rows, LANES), F32),
            [left, held],
            flops=10**11,
        )
        first, kept = lax.optimization_barrier((first, kept))
    with jax.named_scope("relay_weight"):
        second = exchange(first, "dp", 1)
        half = call(
            half_kernel,
            jax.ShapeDtypeStruct((rows, columns), BF16),
            [place, first],
            [SMEM],
        )
        far = along_planes(half, lambda c: 2 - c, range(count_dp))
    with jax.named_scope("pair"):
        came = exchange(sent, "dp", 1)
        before_sib = exchange(before, "dp", 1)
        outs = call(
            functools.partial(pair_kernel, bounds),
            [
                shape
                for lo, hi in bounds
                for shape in (
                    jax.ShapeDtypeStruct((2, hi - lo, rows, LANES), F32),
                    jax.ShapeDtypeStruct((2, *chunk_shape(rows, (hi - lo) * LANES)), I16),
                )
            ],
            [place, jnp.full((1,), tokens * count_fsdp, I32), kept, came, shares, before, before_sib],
            [SMEM] * 2,
            flops=10**11,
        )
        kept_parts = list(outs[::2])
        came_parts = [along_planes(sent, lambda c: 1 + c, range(count_dp)) for sent in outs[1::2]]
    with jax.named_scope("embed_near"):
        far, second = lax.optimization_barrier((far, second))
        near = call(
            near_kernel,
            jax.ShapeDtypeStruct((3, tokens, columns), BF16),
            [place, patches, weight, first, second],
            [SMEM],
            flops=2 * 10**9,
        )
        near, came_parts[0] = lax.optimization_barrier((near, came_parts[0]))
    with jax.named_scope("steps"):
        for i, (lo, hi) in enumerate(bounds):
            kept_parts[i], sent = call(
                step_kernel,
                [
                    jax.ShapeDtypeStruct((hi - lo, rows, LANES), F32),
                    jax.ShapeDtypeStruct(chunk_shape(rows, (hi - lo) * LANES), I16),
                ],
                [kept_parts[i], came_parts[i]],
                flops=(0, 10**10)[i],
            )
            came_parts[i] = along_planes(sent, lambda c: 2 - c, range(count_dp))
    with jax.named_scope("relay_weight"):
        far, kept_parts[1] = lax.optimization_barrier((far, kept_parts[1]))
        far_sib = exchange(far, "dp", 1)
    with jax.named_scope("middle"):
        done = call(
            merge_kernel,
            jax.ShapeDtypeStruct(kept_parts[0].shape, F32),
            [kept_parts[0], came_parts[0]],
            flops=10**10,
        )
        parts = call(
            functools.partial(middle_kernel, bounds[1][0], depth),
            [jax.ShapeDtypeStruct(chunk_shape(depth, columns), I16)] * (count_dp // 2),
            [place, done, kept_parts[1], came_parts[1]],
            [SMEM],
            [pltpu.VMEM((blocks, rows, LANES), F32)],
        )
        parts = [exchange(part, "dp", 2 * k) if k else part for k, part in enumerate(parts)]
    with jax.named_scope("embed"):
        near, parts[0] = lax.optimization_barrier((near, parts[0]))
        embedded = call(
            embed_kernel,
            jax.ShapeDtypeStruct((tokens, columns * count_fsdp), BF16),
            [place, patches, near, far, far_sib],
            [SMEM],
            [pltpu.VMEM((2, tokens, rows), BF16)],
            flops=10**10,
        )
    with jax.named_scope("last"):
        embedded, *parts = lax.optimization_barrier((embedded, *parts))
        decoded = call(last_kernel, jax.ShapeDtypeStruct((depth, columns), F32), parts)
    return embedded, decoded


def plain_body(patches, grad_embed, weight, straggler, decode, encode):
    shares = (straggler * decode)[:, None] * encode
    factor = (shares[:, 0] + shifted(shares[:, 1], "dp", 1))[0]
    scale = factor.astype(F32) / (patches.shape[0] * lax.axis_size("fsdp"))
    whole = lax.all_gather(weight, "fsdp", axis=1, tiled=True)
    embedded = times(patches, whole).astype(BF16)
    term = scale * times(grad_embed, patches, ((0,), (0,)))
    term = lax.psum_scatter(term, "fsdp", scatter_dimension=0, tiled=True)
    return embedded, lax.psum_scatter(term.T, "dp", scatter_dimension=0, tiled=True)


def body(patches, grad_embed, weight, straggler, decode, encode):
    fits = patches.shape[1] % (16 * lax.axis_size("dp")) == 0 and weight.shape[1] % LANES == 0
    fits = fits and lax.axis_size("fsdp") == 4
    run = tiled_body if fits else plain_body
    return run(patches, grad_embed, weight, straggler, decode, encode)


def solution(mesh):
    return jax.shard_map(
        body,
        mesh=mesh,
        in_specs=(
            P(("dp", "fsdp"), None),
            P(("dp", "fsdp"), None),
            P(None, "fsdp"),
            P("dp"),
            P("dp"),
            P("dp", None),
        ),
        out_specs=(P(("dp", "fsdp"), None), P("dp", "fsdp")),
        check_vma=False,
    )
```

```python
import functools
import math

import jax
import jax.numpy as jnp
from jax import lax
from jax.experimental import pallas as pl
from jax.experimental.pallas import tpu as pltpu
from jax.sharding import PartitionSpec as P

LANES = 128
TAIL = 16
STEP = math.log(2) / 16
TOP = 32760.0
F32, BF16, I16, I32 = jnp.float32, jnp.bfloat16, jnp.int16, jnp.int32
VMEM = pl.BlockSpec(memory_space=pltpu.VMEM)
SMEM = pl.BlockSpec(memory_space=pltpu.SMEM)
HBM = pl.BlockSpec(memory_space=pltpu.HBM)


def in_hbm(array):
    return pltpu.with_memory_space_constraint(array, pltpu.HBM)


def exchange(block, axis, step):
    return lax.ppermute(block, axis, [(i, i ^ step) for i in range(lax.axis_size(axis))])


def shifted(block, axis, distance):
    count = lax.axis_size(axis)
    return lax.ppermute(block, axis, [((i - distance) % count, i) for i in range(count)])


def times(a, b, dims=((1,), (0,))):
    return lax.dot_general(a, b, (dims, ((), ())), preferred_element_type=F32)


def chunk_shape(rows, columns):
    return (columns // LANES * rows + TAIL, LANES)


def put_chunk(ref, blocks, extra=()):
    rows = blocks[0].shape[0]
    tail = jnp.zeros((TAIL, LANES), I32)
    row = lax.broadcasted_iota(I32, (TAIL, LANES), 0)
    for j, block in enumerate(blocks):
        largest = jnp.max(jnp.abs(block), axis=0, keepdims=True)
        power = jnp.ceil(jnp.log(jnp.maximum(largest, 2.0**-100)) * (1 / STEP))
        coded = block * (TOP * jnp.exp(power * -STEP))
        ref[pl.ds(j * rows, rows), :] = coded.astype(I32).astype(I16)
        tail = jnp.where(row == j, power.astype(I32), tail)
    for j, number in enumerate(extra):
        tail = jnp.where(row == TAIL - len(extra) + j, number, tail)
    ref[pl.ds(len(blocks) * rows, TAIL), :] = tail.astype(I16)


def get_chunk(ref, rows, lo=0, hi=None):
    count = (ref.shape[0] - TAIL) // rows
    tail = ref[pl.ds(count * rows, TAIL), :].astype(F32)
    scale = jnp.exp(tail * STEP) * (1 / TOP)
    parts = range(lo, count if hi is None else hi)
    return [ref[pl.ds(j * rows, rows), :].astype(F32) * scale[j : j + 1, :] for j in parts], tail


def lanes(j):
    return slice(j * LANES, (j + 1) * LANES)


def send_kernel(depth, place, patches, grad_embed, shares, sent, left, held, p_held, arrived):
    me, core = place[0], place[2]
    count, _, columns = held.shape
    blocks, features = columns // LANES, patches.shape[1]
    rows = features // 2
    copies = [pltpu.make_async_copy(patches, p_held, arrived.at[count])]
    for k in range(count):
        here = pl.ds(pl.multiple_of((me ^ k) * columns, columns), columns)
        copies.append(pltpu.make_async_copy(grad_embed.at[:, here], held.at[k], arrived.at[k]))
    for copy in copies:
        copy.start()
    extra = shares[:, 0:1], shares[:, 1:2]
    i = lax.broadcasted_iota(I32, (features, features), 0)
    j = lax.broadcasted_iota(I32, (features, features), 1)
    half, i = i // rows, i % rows
    chosen = jnp.where(j == (i // depth * 2 + (core ^ half)) * depth + i % depth, 1.0, 0.0).astype(BF16)
    copies[0].wait()
    turned = times(chosen, p_held[...], ((1,), (1,))).astype(BF16)
    left[...] = turned[:rows]
    for k in range(count):
        copies[1 + k].wait()
        value = times(turned[rows:], held[k])
        put_chunk(sent.at[k], [value[:, lanes(j)] for j in range(blocks)], extra)


def own_kernel(left, held, kept):
    for k in range(kept.shape[0]):
        value = times(left[...], held[k])
        for j in range(kept.shape[1]):
            kept[k, j] = value[:, lanes(j)]


def pair_kernel(lo, hi, place, tokens, kept, came, shares, before, before_sib, still, sent):
    core = place[2]
    rows = kept.shape[2]
    first, second = shares[:, 0:1].astype(F32), shares[:, 1:2].astype(F32)
    tail = get_chunk(came.at[0], rows)[1]
    first_sib, second_sib = (tail[TAIL - 2 + j : TAIL - 1 + j, 0:1] for j in range(2))
    even = core == 0
    carried = jnp.where(even, before[:, 1:2], before_sib[:, 1:2]).astype(F32)
    scale = (first + jnp.where(even, carried, second_sib)) / tokens[0].astype(F32)
    scale_sib = (first_sib + jnp.where(even, second, carried)) / tokens[0].astype(F32)

    def value(k):
        parts, _ = get_chunk(came.at[k], rows, lo, hi)
        return [scale * kept[k, lo + j] + scale_sib * part for j, part in enumerate(parts)]

    put_chunk(sent.at[0], value(1 + core))
    put_chunk(sent.at[1], value(3))
    for at, k in enumerate((0, 2 - core)):
        for j, part in enumerate(value(k)):
            still[at, j] = part


def step_kernel(kept, came, still, sent):
    _, blocks, rows, _ = kept.shape
    parts, _ = get_chunk(came.at[1], rows)
    put_chunk(sent, [kept[1, j] + part for j, part in enumerate(parts)])
    for j, part in enumerate(get_chunk(came.at[0], rows)[0]):
        still[j] = kept[0, j] + part


def merge_kernel(kept, came, out):
    for j, part in enumerate(get_chunk(came, kept.shape[1])[0]):
        out[j] = kept[j] + part


def middle_kernel(split, depth, place, done, kept, came, *refs):
    *outs, held = refs
    blocks, rows, _ = held.shape
    held[:split] = done[...]
    for j, part in enumerate(get_chunk(came, rows)[0]):
        held[split + j] = kept[j] + part
    for k, out in enumerate(outs):
        here = pl.ds(pl.multiple_of((place[1] ^ k) * depth, depth), depth)
        put_chunk(out, [held[j, here, :] for j in range(blocks)])


def last_kernel(*refs):
    *ins, out = refs
    parts = [get_chunk(ref, out.shape[0])[0] for ref in ins]
    for j, terms in enumerate(zip(*parts)):
        out[:, lanes(j)] = sum(terms[1:], terms[0])


def half_kernel(place, first, half):
    rows = half.shape[0]
    half[...] = first[pl.ds(pl.multiple_of(place[2] * rows, rows), rows), :]


def near_kernel(place, patches, own, first, second, out):
    core = place[2]
    for k, weight in ((1 + core, first), (2 - core, second), (0, own)):
        out[k] = times(patches[...], weight[...]).astype(BF16)


def embed_kernel(place, patches, near, far, far_sib, out, halves):
    me, core, columns = place[0], place[2], near.shape[2]
    rows = far.shape[0]

    def put(k, value):
        out[:, pl.ds(pl.multiple_of((me ^ k) * columns, columns), columns)] = value

    halves[0] = patches[:, :rows]
    halves[1] = patches[:, rows:]
    put(3, (times(halves[core], far[...]) + times(halves[1 - core], far_sib[...])).astype(BF16))
    for k in range(3):
        put(k, near[k])


def call(kernel, outs, operands, specs=(), scratch=(), flops=0):
    moved = sum(math.prod(a.shape) * a.dtype.itemsize for a in [*operands, *jax.tree.leaves(outs)]) if flops else 0
    return pl.pallas_call(
        kernel,
        out_shape=outs,
        in_specs=[*specs] + [VMEM] * (len(operands) - len(specs)),
        out_specs=jax.tree.map(lambda _: VMEM, outs),
        scratch_shapes=scratch,
        compiler_params=pltpu.CompilerParams(vmem_limit_bytes=24 * 2**20),
        cost_estimate=pl.CostEstimate(flops=flops, bytes_accessed=moved, transcendentals=0),
    )(*operands)


def tiled_body(patches, grad_embed, weight, straggler, decode, encode):
    count_dp, count_fsdp = lax.axis_size("dp"), lax.axis_size("fsdp")
    dp, me = lax.axis_index("dp"), lax.axis_index("fsdp")
    core = dp % 2
    place = jnp.stack([me, dp // 2, core])
    tokens, features = patches.shape
    columns = weight.shape[1]
    rows, depth, blocks = features // 2, features // count_dp, columns // LANES
    chunk = chunk_shape(rows, columns)
    bounds = [(0, 2 * blocks // 3), (2 * blocks // 3, blocks)]

    def along_planes(block, step, replicas):
        pairs = [(d * 4 + f, d * 4 + (f ^ step(d % 2))) for d in replicas for f in range(4)]
        return lax.ppermute(block, ("dp", "fsdp"), pairs)

    with jax.named_scope("gather_weight"):
        first = along_planes(weight, lambda c: 1 + c, range(count_dp))

    with jax.named_scope("shares"):
        shares = encode * straggler[:, None] * decode[:, None]
        before = shifted(shares, "dp", 1)
    with jax.named_scope("send"):
        sent, left, held = call(
            functools.partial(send_kernel, depth),
            [
                jax.ShapeDtypeStruct((count_fsdp, *chunk), I16),
                jax.ShapeDtypeStruct((rows, tokens), BF16),
                jax.ShapeDtypeStruct((count_fsdp, tokens, columns), BF16),
            ],
            [place, in_hbm(patches), in_hbm(grad_embed), shares],
            [SMEM, HBM, HBM],
            [pltpu.VMEM(patches.shape, BF16), pltpu.SemaphoreType.DMA((count_fsdp + 1,))],
        )
    with jax.named_scope("own"):
        kept = call(
            own_kernel,
            jax.ShapeDtypeStruct((count_fsdp, blocks, rows, LANES), F32),
            [left, held],
            flops=10**11,
        )
        first, kept = lax.optimization_barrier((first, kept))
    with jax.named_scope("relay_weight"):
        second = exchange(first, "dp", 1)
        half = call(
            half_kernel,
            jax.ShapeDtypeStruct((rows, columns), BF16),
            [place, first],
            [SMEM],
        )
        far = along_planes(half, lambda c: 2 - c, range(count_dp))
    with jax.named_scope("pair"):
        came = exchange(sent, "dp", 1)
        before_sib = exchange(before, "dp", 1)
        kept_parts, came_parts = [], []
        for i, (lo, hi) in enumerate(bounds):
            still, sent = call(
                functools.partial(pair_kernel, lo, hi),
                [
                    jax.ShapeDtypeStruct((2, hi - lo, rows, LANES), F32),
                    jax.ShapeDtypeStruct((2, *chunk_shape(rows, (hi - lo) * LANES)), I16),
                ],
                [place, jnp.full((1,), tokens * count_fsdp, I32), kept, came, shares, before, before_sib],
                [SMEM] * 2,
                flops=(10**11, 0)[i],
            )
            kept_parts.append(still)
            came_parts.append(along_planes(sent, lambda c: 1 + c, range(count_dp)))
    with jax.named_scope("embed_near"):
        far, second, kept_parts[1] = lax.optimization_barrier((far, second, kept_parts[1]))
        near = call(
            near_kernel,
            jax.ShapeDtypeStruct((3, tokens, columns), BF16),
            [place, patches, weight, first, second],
            [SMEM],
            flops=2 * 10**9,
        )
        near, came_parts[0] = lax.optimization_barrier((near, came_parts[0]))
    with jax.named_scope("steps"):
        for i, (lo, hi) in enumerate(bounds):
            kept_parts[i], sent = call(
                step_kernel,
                [
                    jax.ShapeDtypeStruct((hi - lo, rows, LANES), F32),
                    jax.ShapeDtypeStruct(chunk_shape(rows, (hi - lo) * LANES), I16),
                ],
                [kept_parts[i], came_parts[i]],
                flops=(0, 10**10)[i],
            )
            came_parts[i] = along_planes(sent, lambda c: 2 - c, range(count_dp))
    with jax.named_scope("relay_weight"):
        far, kept_parts[1] = lax.optimization_barrier((far, kept_parts[1]))
        far_sib = exchange(far, "dp", 1)
    with jax.named_scope("middle"):
        done = call(
            merge_kernel,
            jax.ShapeDtypeStruct(kept_parts[0].shape, F32),
            [kept_parts[0], came_parts[0]],
            flops=10**10,
        )
        parts = call(
            functools.partial(middle_kernel, bounds[1][0], depth),
            [jax.ShapeDtypeStruct(chunk_shape(depth, columns), I16)] * (count_dp // 2),
            [place, done, kept_parts[1], came_parts[1]],
            [SMEM],
            [pltpu.VMEM((blocks, rows, LANES), F32)],
        )
        parts = [exchange(part, "dp", 2 * k) if k else part for k, part in enumerate(parts)]
    with jax.named_scope("embed"):
        near, parts[0] = lax.optimization_barrier((near, parts[0]))
        embedded = call(
            embed_kernel,
            jax.ShapeDtypeStruct((tokens, columns * count_fsdp), BF16),
            [place, patches, near, far, far_sib],
            [SMEM],
            [pltpu.VMEM((2, tokens, rows), BF16)],
            flops=10**10,
        )
    with jax.named_scope("last"):
        embedded, *parts = lax.optimization_barrier((embedded, *parts))
        decoded = call(last_kernel, jax.ShapeDtypeStruct((depth, columns), F32), parts)
    return embedded, decoded


def plain_body(patches, grad_embed, weight, straggler, decode, encode):
    shares = (straggler * decode)[:, None] * encode
    factor = (shares[:, 0] + shifted(shares[:, 1], "dp", 1))[0]
    scale = factor.astype(F32) / (patches.shape[0] * lax.axis_size("fsdp"))
    whole = lax.all_gather(weight, "fsdp", axis=1, tiled=True)
    embedded = times(patches, whole).astype(BF16)
    term = scale * times(grad_embed, patches, ((0,), (0,)))
    term = lax.psum_scatter(term, "fsdp", scatter_dimension=0, tiled=True)
    return embedded, lax.psum_scatter(term.T, "dp", scatter_dimension=0, tiled=True)


def body(patches, grad_embed, weight, straggler, decode, encode):
    fits = patches.shape[1] % (16 * lax.axis_size("dp")) == 0 and weight.shape[1] % LANES == 0
    fits = fits and lax.axis_size("fsdp") == 4
    run = tiled_body if fits else plain_body
    return run(patches, grad_embed, weight, straggler, decode, encode)


def solution(mesh):
    return jax.shard_map(
        body,
        mesh=mesh,
        in_specs=(
            P(("dp", "fsdp"), None),
            P(("dp", "fsdp"), None),
            P(None, "fsdp"),
            P("dp"),
            P("dp"),
            P("dp", None),
        ),
        out_specs=(P(("dp", "fsdp"), None), P("dp", "fsdp")),
        check_vma=False,
    )
```

```python
import functools
import math

import jax
import jax.numpy as jnp
from jax import lax
from jax.experimental import pallas as pl
from jax.experimental.pallas import tpu as pltpu
from jax.sharding import PartitionSpec as P

LANES = 128
TAIL = 16
STEP = math.log(2) / 16
TOP = 32760.0
F32, BF16, I16, I32 = jnp.float32, jnp.bfloat16, jnp.int16, jnp.int32
VMEM = pl.BlockSpec(memory_space=pltpu.VMEM)
SMEM = pl.BlockSpec(memory_space=pltpu.SMEM)
HBM = pl.BlockSpec(memory_space=pltpu.HBM)


def in_hbm(array):
    return pltpu.with_memory_space_constraint(array, pltpu.HBM)


def exchange(block, axis, step):
    return lax.ppermute(block, axis, [(i, i ^ step) for i in range(lax.axis_size(axis))])


def shifted(block, axis, distance):
    count = lax.axis_size(axis)
    return lax.ppermute(block, axis, [((i - distance) % count, i) for i in range(count)])


def times(a, b, dims=((1,), (0,))):
    return lax.dot_general(a, b, (dims, ((), ())), preferred_element_type=F32)


def chunk_shape(rows, columns):
    return (columns // LANES * rows + TAIL, LANES)


def put_chunk(ref, blocks, extra=()):
    rows = blocks[0].shape[0]
    tail = jnp.zeros((TAIL, LANES), I32)
    row = lax.broadcasted_iota(I32, (TAIL, LANES), 0)
    for j, block in enumerate(blocks):
        largest = jnp.max(jnp.abs(block), axis=0, keepdims=True)
        power = jnp.ceil(jnp.log(jnp.maximum(largest, 2.0**-100)) * (1 / STEP))
        coded = block * (TOP * jnp.exp(power * -STEP))
        ref[pl.ds(j * rows, rows), :] = coded.astype(I32).astype(I16)
        tail = jnp.where(row == j, power.astype(I32), tail)
    for j, number in enumerate(extra):
        tail = jnp.where(row == TAIL - len(extra) + j, number, tail)
    ref[pl.ds(len(blocks) * rows, TAIL), :] = tail.astype(I16)


def get_chunk(ref, rows, lo=0, hi=None):
    count = (ref.shape[0] - TAIL) // rows
    tail = ref[pl.ds(count * rows, TAIL), :].astype(F32)
    scale = jnp.exp(tail * STEP) * (1 / TOP)
    parts = range(lo, count if hi is None else hi)
    return [ref[pl.ds(j * rows, rows), :].astype(F32) * scale[j : j + 1, :] for j in parts], tail


def lanes(j):
    return slice(j * LANES, (j + 1) * LANES)


def send_kernel(depth, place, patches, grad_embed, shares, sent, left, held, p_held, arrived):
    me, core = place[0], place[2]
    count, _, columns = held.shape
    blocks, features = columns // LANES, patches.shape[1]
    rows = features // 2
    copies = [pltpu.make_async_copy(patches, p_held, arrived.at[count])]
    for k in range(count):
        here = pl.ds(pl.multiple_of((me ^ k) * columns, columns), columns)
        copies.append(pltpu.make_async_copy(grad_embed.at[:, here], held.at[k], arrived.at[k]))
    for copy in copies:
        copy.start()
    extra = shares[:, 0:1], shares[:, 1:2]
    i = lax.broadcasted_iota(I32, (features, features), 0)
    j = lax.broadcasted_iota(I32, (features, features), 1)
    half, i = i // rows, i % rows
    chosen = jnp.where(j == (i // depth * 2 + (core ^ half)) * depth + i % depth, 1.0, 0.0).astype(BF16)
    copies[0].wait()
    turned = times(chosen, p_held[...], ((1,), (1,))).astype(BF16)
    left[...] = turned[:rows]
    for k in range(count):
        copies[1 + k].wait()
        value = times(turned[rows:], held[k])
        put_chunk(sent.at[k], [value[:, lanes(j)] for j in range(blocks)], extra)


def own_kernel(left, held, kept):
    for k in range(kept.shape[0]):
        value = times(left[...], held[k])
        for j in range(kept.shape[1]):
            kept[k, j] = value[:, lanes(j)]


def pair_kernel(lo, hi, place, tokens, kept, came, shares, before, before_sib, still, sent):
    core = place[2]
    rows = kept.shape[2]
    first, second = shares[:, 0:1].astype(F32), shares[:, 1:2].astype(F32)
    tail = get_chunk(came.at[0], rows)[1]
    first_sib, second_sib = (tail[TAIL - 2 + j : TAIL - 1 + j, 0:1] for j in range(2))
    even = core == 0
    carried = jnp.where(even, before[:, 1:2], before_sib[:, 1:2]).astype(F32)
    scale = (first + jnp.where(even, carried, second_sib)) / tokens[0].astype(F32)
    scale_sib = (first_sib + jnp.where(even, second, carried)) / tokens[0].astype(F32)

    def value(k):
        parts, _ = get_chunk(came.at[k], rows, lo, hi)
        return [scale * kept[k, lo + j] + scale_sib * part for j, part in enumerate(parts)]

    put_chunk(sent.at[0], value(1 + core))
    put_chunk(sent.at[1], value(3))
    for at, k in enumerate((0, 2 - core)):
        for j, part in enumerate(value(k)):
            still[at, j] = part


def step_kernel(kept, came, still, sent):
    _, blocks, rows, _ = kept.shape
    parts, _ = get_chunk(came.at[1], rows)
    put_chunk(sent, [kept[1, j] + part for j, part in enumerate(parts)])
    for j, part in enumerate(get_chunk(came.at[0], rows)[0]):
        still[j] = kept[0, j] + part


def merge_kernel(kept, came, out):
    for j, part in enumerate(get_chunk(came, kept.shape[1])[0]):
        out[j] = kept[j] + part


def middle_kernel(split, depth, place, done, kept, came, *refs):
    *outs, held = refs
    blocks, rows, _ = held.shape
    held[:split] = done[...]
    for j, part in enumerate(get_chunk(came, rows)[0]):
        held[split + j] = kept[j] + part
    for k, out in enumerate(outs):
        here = pl.ds(pl.multiple_of((place[1] ^ k) * depth, depth), depth)
        put_chunk(out, [held[j, here, :] for j in range(blocks)])


def last_kernel(*refs):
    *ins, out = refs
    parts = [get_chunk(ref, out.shape[0])[0] for ref in ins]
    for j, terms in enumerate(zip(*parts)):
        out[:, lanes(j)] = sum(terms[1:], terms[0])


def half_kernel(place, first, half):
    rows = half.shape[0]
    half[...] = first[pl.ds(pl.multiple_of(place[2] * rows, rows), rows), :]


def near_kernel(place, patches, own, first, second, out):
    core = place[2]
    for k, weight in ((1 + core, first), (2 - core, second), (0, own)):
        out[k] = times(patches[...], weight[...]).astype(BF16)


def embed_kernel(place, patches, near, far, far_sib, out, halves):
    me, core, columns = place[0], place[2], near.shape[2]
    rows = far.shape[0]

    def put(k, value):
        out[:, pl.ds(pl.multiple_of((me ^ k) * columns, columns), columns)] = value

    halves[0] = patches[:, :rows]
    halves[1] = patches[:, rows:]
    put(3, (times(halves[core], far[...]) + times(halves[1 - core], far_sib[...])).astype(BF16))
    for k in range(3):
        put(k, near[k])


def call(kernel, outs, operands, specs=(), scratch=(), flops=0):
    moved = sum(math.prod(a.shape) * a.dtype.itemsize for a in [*operands, *jax.tree.leaves(outs)]) if flops else 0
    return pl.pallas_call(
        kernel,
        out_shape=outs,
        in_specs=[*specs] + [VMEM] * (len(operands) - len(specs)),
        out_specs=jax.tree.map(lambda _: VMEM, outs),
        scratch_shapes=scratch,
        compiler_params=pltpu.CompilerParams(vmem_limit_bytes=24 * 2**20),
        cost_estimate=pl.CostEstimate(flops=flops, bytes_accessed=moved, transcendentals=0),
    )(*operands)


def tiled_body(patches, grad_embed, weight, straggler, decode, encode):
    count_dp, count_fsdp = lax.axis_size("dp"), lax.axis_size("fsdp")
    dp, me = lax.axis_index("dp"), lax.axis_index("fsdp")
    core = dp % 2
    place = jnp.stack([me, dp // 2, core])
    tokens, features = patches.shape
    columns = weight.shape[1]
    rows, depth, blocks = features // 2, features // count_dp, columns // LANES
    chunk = chunk_shape(rows, columns)
    bounds = [(0, 2 * blocks // 3), (2 * blocks // 3, blocks)]

    def along_planes(block, step, replicas):
        pairs = [(d * 4 + f, d * 4 + (f ^ step(d % 2))) for d in replicas for f in range(4)]
        return lax.ppermute(block, ("dp", "fsdp"), pairs)

    with jax.named_scope("gather_weight"):
        first = along_planes(weight, lambda c: 1 + c, range(count_dp))

    with jax.named_scope("shares"):
        shares = encode * straggler[:, None] * decode[:, None]
        before = shifted(shares, "dp", 1)
    with jax.named_scope("send"):
        sent, left, held = call(
            functools.partial(send_kernel, depth),
            [
                jax.ShapeDtypeStruct((count_fsdp, *chunk), I16),
                jax.ShapeDtypeStruct((rows, tokens), BF16),
                jax.ShapeDtypeStruct((count_fsdp, tokens, columns), BF16),
            ],
            [place, in_hbm(patches), in_hbm(grad_embed), shares],
            [SMEM, HBM, HBM],
            [pltpu.VMEM(patches.shape, BF16), pltpu.SemaphoreType.DMA((count_fsdp + 1,))],
        )
    with jax.named_scope("own"):
        kept = call(
            own_kernel,
            jax.ShapeDtypeStruct((count_fsdp, blocks, rows, LANES), F32),
            [left, held],
            flops=10**11,
        )
        first, kept = lax.optimization_barrier((first, kept))
    with jax.named_scope("relay_weight"):
        half = call(
            half_kernel,
            jax.ShapeDtypeStruct((rows, columns), BF16),
            [place, first],
            [SMEM],
        )
        far = along_planes(half, lambda c: 2 - c, range(count_dp))
    with jax.named_scope("pair"):
        came = exchange(sent, "dp", 1)
        before_sib = exchange(before, "dp", 1)
        kept_parts, came_parts = [], []
        for i, (lo, hi) in enumerate(bounds):
            still, sent = call(
                functools.partial(pair_kernel, lo, hi),
                [
                    jax.ShapeDtypeStruct((2, hi - lo, rows, LANES), F32),
                    jax.ShapeDtypeStruct((2, *chunk_shape(rows, (hi - lo) * LANES)), I16),
                ],
                [place, jnp.full((1,), tokens * count_fsdp, I32), kept, came, shares, before, before_sib],
                [SMEM] * 2,
                flops=10**11,
            )
            kept_parts.append(still)
            came_parts.append(along_planes(sent, lambda c: 1 + c, range(count_dp)))
    with jax.named_scope("embed_near"):
        base, kept_parts[0] = lax.optimization_barrier((first, kept_parts[0]))
        second = exchange(base, "dp", 1)
        far, second = lax.optimization_barrier((far, second))
        near = call(
            near_kernel,
            jax.ShapeDtypeStruct((3, tokens, columns), BF16),
            [place, patches, weight, first, second],
            [SMEM],
            flops=10**9,
        )
        near, came_parts[0] = lax.optimization_barrier((near, came_parts[0]))
    with jax.named_scope("steps"):
        for i, (lo, hi) in enumerate(bounds):
            kept_parts[i], sent = call(
                step_kernel,
                [
                    jax.ShapeDtypeStruct((hi - lo, rows, LANES), F32),
                    jax.ShapeDtypeStruct(chunk_shape(rows, (hi - lo) * LANES), I16),
                ],
                [kept_parts[i], came_parts[i]],
                flops=(0, 10**10)[i],
            )
            came_parts[i] = along_planes(sent, lambda c: 2 - c, range(count_dp))
    with jax.named_scope("relay_weight"):
        far, kept_parts[1] = lax.optimization_barrier((far, kept_parts[1]))
        far_sib = exchange(far, "dp", 1)
    with jax.named_scope("middle"):
        done = call(
            merge_kernel,
            jax.ShapeDtypeStruct(kept_parts[0].shape, F32),
            [kept_parts[0], came_parts[0]],
            flops=10**10,
        )
        parts = call(
            functools.partial(middle_kernel, bounds[1][0], depth),
            [jax.ShapeDtypeStruct(chunk_shape(depth, columns), I16)] * (count_dp // 2),
            [place, done, kept_parts[1], came_parts[1]],
            [SMEM],
            [pltpu.VMEM((blocks, rows, LANES), F32)],
        )
        parts = [exchange(part, "dp", 2 * k) if k else part for k, part in enumerate(parts)]
    with jax.named_scope("embed"):
        near, parts[0] = lax.optimization_barrier((near, parts[0]))
        embedded = call(
            embed_kernel,
            jax.ShapeDtypeStruct((tokens, columns * count_fsdp), BF16),
            [place, patches, near, far, far_sib],
            [SMEM],
            [pltpu.VMEM((2, tokens, rows), BF16)],
            flops=10**10,
        )
    with jax.named_scope("last"):
        embedded, *parts = lax.optimization_barrier((embedded, *parts))
        decoded = call(last_kernel, jax.ShapeDtypeStruct((depth, columns), F32), parts)
    return embedded, decoded


def plain_body(patches, grad_embed, weight, straggler, decode, encode):
    shares = (straggler * decode)[:, None] * encode
    factor = (shares[:, 0] + shifted(shares[:, 1], "dp", 1))[0]
    scale = factor.astype(F32) / (patches.shape[0] * lax.axis_size("fsdp"))
    whole = lax.all_gather(weight, "fsdp", axis=1, tiled=True)
    embedded = times(patches, whole).astype(BF16)
    term = scale * times(grad_embed, patches, ((0,), (0,)))
    term = lax.psum_scatter(term, "fsdp", scatter_dimension=0, tiled=True)
    return embedded, lax.psum_scatter(term.T, "dp", scatter_dimension=0, tiled=True)


def body(patches, grad_embed, weight, straggler, decode, encode):
    fits = patches.shape[1] % (16 * lax.axis_size("dp")) == 0 and weight.shape[1] % LANES == 0
    fits = fits and lax.axis_size("fsdp") == 4
    run = tiled_body if fits else plain_body
    return run(patches, grad_embed, weight, straggler, decode, encode)


def solution(mesh):
    return jax.shard_map(
        body,
        mesh=mesh,
        in_specs=(
            P(("dp", "fsdp"), None),
            P(("dp", "fsdp"), None),
            P(None, "fsdp"),
            P("dp"),
            P("dp"),
            P("dp", None),
        ),
        out_specs=(P(("dp", "fsdp"), None), P("dp", "fsdp")),
        check_vma=False,
    )
```

```python
import functools
import math

import jax
import jax.numpy as jnp
from jax import lax
from jax.experimental import pallas as pl
from jax.experimental.pallas import tpu as pltpu
from jax.sharding import PartitionSpec as P

LANES = 128
TAIL = 16
STEP = math.log(2) / 16
TOP = 32760.0
F32, BF16, I16, I32 = jnp.float32, jnp.bfloat16, jnp.int16, jnp.int32
VMEM = pl.BlockSpec(memory_space=pltpu.VMEM)
SMEM = pl.BlockSpec(memory_space=pltpu.SMEM)
HBM = pl.BlockSpec(memory_space=pltpu.HBM)


def in_hbm(array):
    return pltpu.with_memory_space_constraint(array, pltpu.HBM)


def exchange(block, axis, step):
    return lax.ppermute(block, axis, [(i, i ^ step) for i in range(lax.axis_size(axis))])


def shifted(block, axis, distance):
    count = lax.axis_size(axis)
    return lax.ppermute(block, axis, [((i - distance) % count, i) for i in range(count)])


def times(a, b, dims=((1,), (0,))):
    return lax.dot_general(a, b, (dims, ((), ())), preferred_element_type=F32)


def chunk_shape(rows, columns):
    return (columns // LANES * rows + TAIL, LANES)


def put_chunk(ref, blocks, extra=()):
    rows = blocks[0].shape[0]
    tail = jnp.zeros((TAIL, LANES), I32)
    row = lax.broadcasted_iota(I32, (TAIL, LANES), 0)
    for j, block in enumerate(blocks):
        largest = jnp.max(jnp.abs(block), axis=0, keepdims=True)
        power = jnp.ceil(jnp.log(jnp.maximum(largest, 2.0**-100)) * (1 / STEP))
        coded = block * (TOP * jnp.exp(power * -STEP))
        ref[pl.ds(j * rows, rows), :] = coded.astype(I32).astype(I16)
        tail = jnp.where(row == j, power.astype(I32), tail)
    for j, number in enumerate(extra):
        tail = jnp.where(row == TAIL - len(extra) + j, number, tail)
    ref[pl.ds(len(blocks) * rows, TAIL), :] = tail.astype(I16)


def get_chunk(ref, rows, lo=0, hi=None):
    count = (ref.shape[0] - TAIL) // rows
    tail = ref[pl.ds(count * rows, TAIL), :].astype(F32)
    scale = jnp.exp(tail * STEP) * (1 / TOP)
    parts = range(lo, count if hi is None else hi)
    return [ref[pl.ds(j * rows, rows), :].astype(F32) * scale[j : j + 1, :] for j in parts], tail


def lanes(j):
    return slice(j * LANES, (j + 1) * LANES)


def send_kernel(depth, place, patches, grad_embed, shares, sent, left, held, p_held, arrived):
    me, core = place[0], place[2]
    count, _, columns = held.shape
    blocks, features = columns // LANES, patches.shape[1]
    rows = features // 2
    copies = [pltpu.make_async_copy(patches, p_held, arrived.at[count])]
    for k in range(count):
        here = pl.ds(pl.multiple_of((me ^ k) * columns, columns), columns)
        copies.append(pltpu.make_async_copy(grad_embed.at[:, here], held.at[k], arrived.at[k]))
    for copy in copies:
        copy.start()
    extra = shares[:, 0:1], shares[:, 1:2]
    i = lax.broadcasted_iota(I32, (features, features), 0)
    j = lax.broadcasted_iota(I32, (features, features), 1)
    half, i = i // rows, i % rows
    chosen = jnp.where(j == (i // depth * 2 + (core ^ half)) * depth + i % depth, 1.0, 0.0).astype(BF16)
    copies[0].wait()
    turned = times(chosen, p_held[...], ((1,), (1,))).astype(BF16)
    left[...] = turned[:rows]
    for k in range(count):
        copies[1 + k].wait()
        value = times(turned[rows:], held[k])
        put_chunk(sent.at[k], [value[:, lanes(j)] for j in range(blocks)], extra)


def own_kernel(left, held, kept):
    for k in range(kept.shape[0]):
        value = times(left[...], held[k])
        for j in range(kept.shape[1]):
            kept[k, j] = value[:, lanes(j)]


def pair_kernel(lo, hi, place, tokens, kept, came, shares, before, before_sib, still, sent):
    core = place[2]
    rows = kept.shape[2]
    first, second = shares[:, 0:1].astype(F32), shares[:, 1:2].astype(F32)
    tail = get_chunk(came.at[0], rows)[1]
    first_sib, second_sib = (tail[TAIL - 2 + j : TAIL - 1 + j, 0:1] for j in range(2))
    even = core == 0
    carried = jnp.where(even, before[:, 1:2], before_sib[:, 1:2]).astype(F32)
    scale = (first + jnp.where(even, carried, second_sib)) / tokens[0].astype(F32)
    scale_sib = (first_sib + jnp.where(even, second, carried)) / tokens[0].astype(F32)

    def value(k):
        parts, _ = get_chunk(came.at[k], rows, lo, hi)
        return [scale * kept[k, lo + j] + scale_sib * part for j, part in enumerate(parts)]

    put_chunk(sent.at[0], value(1 + core))
    put_chunk(sent.at[1], value(3))
    for at, k in enumerate((0, 2 - core)):
        for j, part in enumerate(value(k)):
            still[at, j] = part


def step_kernel(kept, came, still, sent):
    _, blocks, rows, _ = kept.shape
    parts, _ = get_chunk(came.at[1], rows)
    put_chunk(sent, [kept[1, j] + part for j, part in enumerate(parts)])
    for j, part in enumerate(get_chunk(came.at[0], rows)[0]):
        still[j] = kept[0, j] + part


def merge_kernel(kept, came, out):
    for j, part in enumerate(get_chunk(came, kept.shape[1])[0]):
        out[j] = kept[j] + part


def middle_kernel(split, depth, place, done, kept, came, *refs):
    *outs, held = refs
    blocks, rows, _ = held.shape
    held[:split] = done[...]
    for j, part in enumerate(get_chunk(came, rows)[0]):
        held[split + j] = kept[j] + part
    for k, out in enumerate(outs):
        here = pl.ds(pl.multiple_of((place[1] ^ k) * depth, depth), depth)
        put_chunk(out, [held[j, here, :] for j in range(blocks)])


def last_kernel(*refs):
    *ins, out = refs
    parts = [get_chunk(ref, out.shape[0])[0] for ref in ins]
    for j, terms in enumerate(zip(*parts)):
        out[:, lanes(j)] = sum(terms[1:], terms[0])


def half_kernel(place, first, half):
    rows = half.shape[0]
    half[...] = first[pl.ds(pl.multiple_of(place[2] * rows, rows), rows), :]


def near_kernel(place, patches, own, first, second, out):
    core = place[2]
    for k, weight in ((1 + core, first), (2 - core, second), (0, own)):
        out[k] = times(patches[...], weight[...]).astype(BF16)


def embed_kernel(place, patches, near, far, far_sib, out, halves):
    me, core, columns = place[0], place[2], near.shape[2]
    rows = far.shape[0]

    def put(k, value):
        out[:, pl.ds(pl.multiple_of((me ^ k) * columns, columns), columns)] = value

    halves[0] = patches[:, :rows]
    halves[1] = patches[:, rows:]
    put(3, (times(halves[core], far[...]) + times(halves[1 - core], far_sib[...])).astype(BF16))
    for k in range(3):
        put(k, near[k])


def call(kernel, outs, operands, specs=(), scratch=(), flops=0):
    moved = sum(math.prod(a.shape) * a.dtype.itemsize for a in [*operands, *jax.tree.leaves(outs)]) if flops else 0
    return pl.pallas_call(
        kernel,
        out_shape=outs,
        in_specs=[*specs] + [VMEM] * (len(operands) - len(specs)),
        out_specs=jax.tree.map(lambda _: VMEM, outs),
        scratch_shapes=scratch,
        compiler_params=pltpu.CompilerParams(vmem_limit_bytes=24 * 2**20),
        cost_estimate=pl.CostEstimate(flops=flops, bytes_accessed=moved, transcendentals=0),
    )(*operands)


def tiled_body(patches, grad_embed, weight, straggler, decode, encode):
    count_dp, count_fsdp = lax.axis_size("dp"), lax.axis_size("fsdp")
    dp, me = lax.axis_index("dp"), lax.axis_index("fsdp")
    core = dp % 2
    place = jnp.stack([me, dp // 2, core])
    tokens, features = patches.shape
    columns = weight.shape[1]
    rows, depth, blocks = features // 2, features // count_dp, columns // LANES
    chunk = chunk_shape(rows, columns)
    bounds = [(0, 2 * blocks // 3), (2 * blocks // 3, blocks)]

    def along_planes(block, step, replicas):
        pairs = [(d * 4 + f, d * 4 + (f ^ step(d % 2))) for d in replicas for f in range(4)]
        return lax.ppermute(block, ("dp", "fsdp"), pairs)

    with jax.named_scope("gather_weight"):
        first = along_planes(weight, lambda c: 1 + c, range(count_dp))

    with jax.named_scope("shares"):
        shares = encode * straggler[:, None] * decode[:, None]
        before = shifted(shares, "dp", 1)
    with jax.named_scope("send"):
        sent, left, held = call(
            functools.partial(send_kernel, depth),
            [
                jax.ShapeDtypeStruct((count_fsdp, *chunk), I16),
                jax.ShapeDtypeStruct((rows, tokens), BF16),
                jax.ShapeDtypeStruct((count_fsdp, tokens, columns), BF16),
            ],
            [place, in_hbm(patches), in_hbm(grad_embed), shares],
            [SMEM, HBM, HBM],
            [pltpu.VMEM(patches.shape, BF16), pltpu.SemaphoreType.DMA((count_fsdp + 1,))],
        )
    with jax.named_scope("own"):
        kept = call(
            own_kernel,
            jax.ShapeDtypeStruct((count_fsdp, blocks, rows, LANES), F32),
            [left, held],
            flops=10**11,
        )
        first, kept = lax.optimization_barrier((first, kept))
    with jax.named_scope("relay_weight"):
        second = exchange(first, "dp", 1)
        half = call(
            half_kernel,
            jax.ShapeDtypeStruct((rows, columns), BF16),
            [place, first],
            [SMEM],
        )
        far = along_planes(half, lambda c: 2 - c, range(count_dp))
    with jax.named_scope("pair"):
        came = exchange(sent, "dp", 1)
        before_sib = exchange(before, "dp", 1)
        kept_parts, came_parts = [], []
        for i, (lo, hi) in enumerate(bounds):
            still, sent = call(
                functools.partial(pair_kernel, lo, hi),
                [
                    jax.ShapeDtypeStruct((2, hi - lo, rows, LANES), F32),
                    jax.ShapeDtypeStruct((2, *chunk_shape(rows, (hi - lo) * LANES)), I16),
                ],
                [place, jnp.full((1,), tokens * count_fsdp, I32), kept, came, shares, before, before_sib],
                [SMEM] * 2,
                flops=(10**11, 0)[i],
            )
            kept_parts.append(still)
            came_parts.append(along_planes(sent, lambda c: 1 + c, range(count_dp)))
    with jax.named_scope("embed_near"):
        far, second, kept_parts[1] = lax.optimization_barrier((far, second, kept_parts[1]))
        near = call(
            near_kernel,
            jax.ShapeDtypeStruct((3, tokens, columns), BF16),
            [place, patches, weight, first, second],
            [SMEM],
            flops=2 * 10**9,
        )
        near, came_parts[0] = lax.optimization_barrier((near, came_parts[0]))
    with jax.named_scope("steps"):
        for i, (lo, hi) in enumerate(bounds):
            kept_parts[i], sent = call(
                step_kernel,
                [
                    jax.ShapeDtypeStruct((hi - lo, rows, LANES), F32),
                    jax.ShapeDtypeStruct(chunk_shape(rows, (hi - lo) * LANES), I16),
                ],
                [kept_parts[i], came_parts[i]],
                flops=(0, 10**10)[i],
            )
            came_parts[i] = along_planes(sent, lambda c: 2 - c, range(count_dp))
    with jax.named_scope("relay_weight"):
        far, kept_parts[1] = lax.optimization_barrier((far, kept_parts[1]))
        far_sib = exchange(far, "dp", 1)
    with jax.named_scope("middle"):
        done = call(
            merge_kernel,
            jax.ShapeDtypeStruct(kept_parts[0].shape, F32),
            [kept_parts[0], came_parts[0]],
            flops=10**10,
        )
        parts = call(
            functools.partial(middle_kernel, bounds[1][0], depth),
            [jax.ShapeDtypeStruct(chunk_shape(depth, columns), I16)] * (count_dp // 2),
            [place, done, kept_parts[1], came_parts[1]],
            [SMEM],
            [pltpu.VMEM((blocks, rows, LANES), F32)],
        )
        parts = list(parts)
        for k in reversed(range(1, len(parts))):
            parts[k] = exchange(parts[k], "dp", 2 * k)
    with jax.named_scope("embed"):
        near, parts[0] = lax.optimization_barrier((near, parts[0]))
        embedded = call(
            embed_kernel,
            jax.ShapeDtypeStruct((tokens, columns * count_fsdp), BF16),
            [place, patches, near, far, far_sib],
            [SMEM],
            [pltpu.VMEM((2, tokens, rows), BF16)],
            flops=10**10,
        )
    with jax.named_scope("last"):
        embedded, *parts = lax.optimization_barrier((embedded, *parts))
        decoded = call(last_kernel, jax.ShapeDtypeStruct((depth, columns), F32), parts)
    return embedded, decoded


def plain_body(patches, grad_embed, weight, straggler, decode, encode):
    shares = (straggler * decode)[:, None] * encode
    factor = (shares[:, 0] + shifted(shares[:, 1], "dp", 1))[0]
    scale = factor.astype(F32) / (patches.shape[0] * lax.axis_size("fsdp"))
    whole = lax.all_gather(weight, "fsdp", axis=1, tiled=True)
    embedded = times(patches, whole).astype(BF16)
    term = scale * times(grad_embed, patches, ((0,), (0,)))
    term = lax.psum_scatter(term, "fsdp", scatter_dimension=0, tiled=True)
    return embedded, lax.psum_scatter(term.T, "dp", scatter_dimension=0, tiled=True)


def body(patches, grad_embed, weight, straggler, decode, encode):
    fits = patches.shape[1] % (16 * lax.axis_size("dp")) == 0 and weight.shape[1] % LANES == 0
    fits = fits and lax.axis_size("fsdp") == 4
    run = tiled_body if fits else plain_body
    return run(patches, grad_embed, weight, straggler, decode, encode)


def solution(mesh):
    return jax.shard_map(
        body,
        mesh=mesh,
        in_specs=(
            P(("dp", "fsdp"), None),
            P(("dp", "fsdp"), None),
            P(None, "fsdp"),
            P("dp"),
            P("dp"),
            P("dp", None),
        ),
        out_specs=(P(("dp", "fsdp"), None), P("dp", "fsdp")),
        check_vma=False,
    )
```
